32 devices in a mesh: dp: 8 (over y, x, core), mp: 4 (over z).
Axes of the slice: x: 2, y: 2, z: 4, core: 2. Of those that a mesh axis runs over, the one named last changes fastest.
Arguments:
- inputs: bfloat16 [12288, 768], P(('dp', 'mp')), may hold values from -6 to 6
- token_ids: int32 [12288], P(('dp', 'mp')), may hold values from 0 to 501152, as said below
- out_cot: bfloat16 [12288, 768], P(('dp', 'mp')), as said below
- pair_ids: int32 [96], replicated, may hold values from 0 to 108
- w_qkv: bfloat16 [3, 768, 768], P(None, None, 'mp'), may hold values from -0.21875 to 0.21875
- b_qv: bfloat16 [2, 768], P(None, 'mp'), may hold values from -3 to 3
- w_attn: bfloat16 [768, 768], P('mp'), may hold values from -0.875 to 0.875
- b_attn: bfloat16 [768], replicated, may hold values from -3 to 3
- norm1_gain: bfloat16 [768], replicated, may hold values from 0.5 to 1.5
- norm1_bias: bfloat16 [768], replicated, may hold values from -3 to 3
- w_in: bfloat16 [768, 3072], P(None, 'mp'), may hold values from -0.21875 to 0.21875
- b_in: bfloat16 [3072], P('mp'), may hold values from -3 to 3
- w_out: bfloat16 [3072, 768], P('mp'), may hold values from -0.109375 to 0.109375
- b_out: bfloat16 [768], replicated, may hold values from -3 to 3
- norm2_gain: bfloat16 [768], replicated, may hold values from 0.5 to 1.5
- norm2_bias: bfloat16 [768], replicated, may hold values from -3 to 3
- w_pool: bfloat16 [768, 768], replicated, may hold values from -0.21875 to 0.21875
- b_pool: bfloat16 [768], replicated, may hold values from -3 to 3
- scale: float32 [1], replicated, may hold values from 20 to 40
Outputs:
- layer_out: bfloat16 [12288, 768], P(('dp', 'mp'))
- input_grad: float32 [12288, 768], P(('dp', 'mp'))
- grad_qkv: float32 [3, 768, 768], P(None, None, 'mp')
- grad_b_qv: float32 [2, 768], P(None, 'mp')
- grad_attn: float32 [768, 768], P('mp')
- grad_b_attn: float32 [768], replicated
- grad_norm1_gain: float32 [768], replicated
- grad_norm1_bias: float32 [768], replicated
- grad_w_in: float32 [768, 3072], P(None, 'mp')
- grad_b_in: float32 [3072], P('mp')
- grad_w_out: float32 [3072, 768], P('mp')
- grad_b_out: float32 [768], replicated
- grad_norm2_gain: float32 [768], replicated
- grad_norm2_bias: float32 [768], replicated
- grad_pool: float32 [768, 768], replicated
- grad_b_pool: float32 [768], replicated
- new_scale: float32 [1], replicated
The draws below stay inside these ranges and needn't reach their ends.
Inputs may be any that keep to these rules, and one draw needn't show every extreme that they name: `token_ids`: id 0 marks padding. Each sentence of 64 positions holds its nonzero ids first and its zeros after them; at least 8 ids of a sentence are nonzero, and some sentences hold no zero. `out_cot`: Real-valued entries, nonzero in every row.
All inputs are finite; a program needn't handle non-finite values.
Results may differ from the reference program's by a relative error of at most 0.02.
Values may be sent and summed in bfloat16 or wider, within the bound.
No kernel may reach another device: no remote copies, remote signals or barrier semaphores. Data moves between devices by JAX's collectives and lax.ppermute only.
A program may use at most 128 MiB of HBM per device.

```python
import math
import jax
import jax.numpy as jnp
import numpy as np
from jax import lax

D = 768
HEADS = 12
HEAD_DIM = 64
FF = 3072
SEQ = 64
LANGS = 109
TOK_DEV = 1536
TOKENS = 12288
NPAIR = 96
N_MP = 4


cot_scale = 0.0002


def draw_token_ids(key, part):
    sents = TOKENS // SEQ
    key_len, key_full, key_ids = jax.random.split(key, 3)
    least = max(SEQ // 8, 1)
    lengths = jax.random.randint(key_len, (sents,), least, SEQ + 1)
    whole = jax.random.randint(key_full, (sents,), 0, 4) == 0
    lengths = jnp.where(whole, SEQ, lengths)
    lengths = lengths.at[0].set(SEQ)
    ids = jax.random.randint(key_ids, (sents, SEQ), 1, 501153)
    position = jnp.arange(SEQ)[None, :]
    return jnp.where(position < lengths[:, None], ids, 0).reshape(TOKENS).astype(jnp.int32)


def draw_out_cot(key, part):
    key_main = jax.random.fold_in(key, 17)
    key_cols = jax.random.fold_in(key, 41)
    key_signs = jax.random.fold_in(key, 53)
    block_rows = TOK_DEV // N_MP
    nblocks = TOKENS // block_rows
    values = jnp.clip(jax.random.normal(key_main, (TOKENS, D), jnp.float32), -6.0, 6.0)
    columns = jax.random.permutation(key_cols, nblocks) % D
    signs = (2 * jax.random.randint(key_signs, (nblocks,), 0, 2) - 1).astype(jnp.float32)
    marks = (jnp.arange(D)[None, :] == columns[:, None]).astype(jnp.float32) * signs[:, None] / block_rows
    values = (values * cot_scale).reshape(nblocks, block_rows, D) + marks[:, None, :]
    return values.reshape(TOKENS, D).astype(jnp.bfloat16)


def touch_ends(drawn, stream_key, low, largest):
    spot = [jax.random.randint(jax.random.fold_in(stream_key, axis), (), 0, length) for axis, length in enumerate(drawn.shape)]
    longest = drawn.shape.index(max(drawn.shape))
    neighbour = spot[:longest] + [(spot[longest] + 1) % drawn.shape[longest]] + spot[longest + 1:]
    return drawn.at[tuple(spot)].set(low).at[tuple(neighbour)].set(largest)


def level_of(rng, extent, cuts, low, largest):
    level = 1.0
    for axis_at, shards_of in cuts:
        draws = jax.random.uniform(jax.random.fold_in(jax.random.fold_in(rng, 6), axis_at), (shards_of,), jnp.float32, low / len(cuts), largest / len(cuts))
        level = level * jnp.repeat(jnp.exp(draws), extent[axis_at] // shards_of).reshape((-1,) + (1,) * (len(extent) - 1 - axis_at))
    return level


def rank_table(amount, lean):
    weights = [(1 << 20) // math.isqrt(grade ** lean) + 1 for grade in range(1, amount + 1)]
    scale = 1 + sum(weights) // (1 << 30)
    return np.cumsum(np.array([max(1, weight // scale) for weight in weights]))


def skewed_ids(stream_key, shape, number_of, skew):
    table = rank_table(number_of, skew)
    ticket = jax.random.randint(jax.random.fold_in(stream_key, 1), shape, 0, int(table[number_of - 1]))
    standing = jnp.searchsorted(jnp.asarray(table, jnp.int32), ticket, side="right")
    return jax.random.permutation(jax.random.fold_in(stream_key, 2), number_of)[standing].astype(jnp.int32)


def normal_values(rng, shape, scale, reach, cuts=(), held_as=jnp.bfloat16):
    drawn = scale * jax.random.normal(rng, shape, jnp.float32)
    if cuts:
        drawn = drawn * level_of(rng, shape, cuts, -0.22, 0.18)
    return jnp.clip(drawn, -reach, reach).astype(held_as)


def setup_inputs(seed: int = 0) -> dict:
    key_list = jax.random.split(jax.random.key(seed), 20)
    return {
        "inputs": normal_values(key_list[0], (TOKENS, D), 1.0, 6.0, ((0, 32),)),
        "token_ids": draw_token_ids(jax.random.fold_in(key_list[19], 71), 0),
        "out_cot": draw_out_cot(jax.random.fold_in(key_list[19], 71), 0),
        "pair_ids": touch_ends(skewed_ids(key_list[3], (NPAIR,), LANGS, 2), jax.random.fold_in(key_list[3], 3), 0, LANGS - 1).astype(jnp.int32),
        "w_qkv": normal_values(key_list[4], (3, D, D), D ** -0.5, 0.21875, ((2, 4),)),
        "b_qv": normal_values(key_list[5], (2, D), 0.5, 3.0, ((1, 4),)),
        "w_attn": normal_values(key_list[6], (D, D), (D // 16) ** -0.5, 0.875, ((0, 4),)),
        "b_attn": normal_values(key_list[7], (D,), 0.5, 3.0),
        "norm1_gain": jnp.clip(1.0 + 0.1 * jax.random.normal(key_list[8], (D,), jnp.float32), 0.5, 1.5).astype(jnp.bfloat16),
        "norm1_bias": normal_values(key_list[9], (D,), 0.5, 3.0),
        "w_in": normal_values(key_list[10], (D, FF), D ** -0.5, 0.21875, ((1, 4),)),
        "b_in": normal_values(key_list[11], (FF,), 0.5, 3.0, ((0, 4),)),
        "w_out": normal_values(key_list[12], (FF, D), FF ** -0.5, 0.109375, ((0, 4),)),
        "b_out": normal_values(key_list[13], (D,), 0.5, 3.0),
        "norm2_gain": jnp.clip(1.0 + 0.1 * jax.random.normal(key_list[14], (D,), jnp.float32), 0.5, 1.5).astype(jnp.bfloat16),
        "norm2_bias": normal_values(key_list[15], (D,), 0.5, 3.0),
        "w_pool": normal_values(key_list[16], (D, D), D ** -0.5, 0.21875),
        "b_pool": normal_values(key_list[17], (D,), 0.5, 3.0),
        "scale": jnp.clip(jax.random.uniform(key_list[18], (1,), jnp.float32, 20.0, 40.0), 20.0, 40.0),
    }


@jax.custom_vjp
def low(v):
    return lax.optimization_barrier(v.astype(jnp.bfloat16)).astype(jnp.float32)

@jax.custom_vjp
def low_back(v):
    return v

def low_keep(v):
    return (low(v), None)

def low_pass(kept, grad):
    return (grad,)

def back_keep(v):
    return (v, None)

def back_low(kept, grad):
    return (low(grad),)
low.defvjp(low_keep, low_pass)
low_back.defvjp(back_keep, back_low)
high = lax.Precision.HIGHEST
eps_norm = 1e-12
margin = 0.3
step_rate = 1.0

def norm_rows(values, gain, shift):
    center = values - lax.optimization_barrier(jnp.mean(values, axis=-1, keepdims=True))
    spread = lax.optimization_barrier(jnp.mean(center * center, axis=-1, keepdims=True))
    return center * lax.rsqrt(spread + eps_norm) * gain + shift

def layer_block(layer, values, ids):
    w_qkv, b_qv, w_attn, b_attn, gain_one, shift_one, w_in, b_in, w_out, b_out, gain_two, shift_two = layer
    rows = values.shape[0]
    sents = rows // SEQ
    qkv = jnp.einsum('td,kde->kte', values, w_qkv, precision=high)
    biases = jnp.stack([b_qv[0], jnp.zeros_like(b_qv[0]), b_qv[1]])
    qkv = low_back(low(qkv + biases[:, None, :]))
    qkv = qkv.reshape(3, sents, SEQ, HEADS, HEAD_DIM)
    raw = low_back(jnp.einsum('sqhd,skhd->shqk', qkv[0], qkv[1], precision=high))
    valid = (ids.reshape(sents, SEQ) != 0)[:, None, None, :]
    scores = jnp.where(valid, raw * 0.125, -1e+30)
    probs = low(jax.nn.softmax(scores, axis=-1))
    context = jnp.einsum('shqk,skhd->sqhd', probs, qkv[2], precision=high).reshape(rows, D)
    context = low_back(low(context))
    attn = low_back(jnp.dot(context, w_attn, precision=high))
    normed_one = norm_rows(values + attn + b_attn, gain_one, shift_one)
    pre_act = low_back(jnp.dot(low(normed_one), w_in, precision=high) + b_in)
    hidden = low(jax.nn.gelu(pre_act, approximate=False))
    ffn = low_back(jnp.dot(hidden, w_out, precision=high))
    return norm_rows(normed_one + ffn + b_out, gain_two, shift_two)

def embed(first_rows, w_pool, b_pool):
    pooled = jnp.tanh(low_back(jnp.dot(low(first_rows), w_pool, precision=high) + b_pool))
    return low(pooled * lax.rsqrt(lax.optimization_barrier(jnp.sum(pooled * pooled, axis=-1, keepdims=True)) + eps_norm))

def ranking(source, target, pairs, scale_value):
    npairs = source.shape[0]
    cosine = jnp.dot(source, target.T, precision=high)
    diag_mask = jnp.eye(npairs, dtype=jnp.float32)
    same = pairs[:, None] == pairs[None, :]
    logits = scale_value[0] * (cosine - margin * diag_mask)
    masked = jnp.where(same, logits, -1e+30)
    diagonal = lax.optimization_barrier(jnp.sum(logits * diag_mask, axis=1))
    row_lse = jax.nn.logsumexp(masked, axis=1)
    col_lse = jax.nn.logsumexp(masked, axis=0)
    counts = lax.optimization_barrier(jnp.sum(same.astype(jnp.float32), axis=1))
    return jnp.sum((row_lse + col_lse - 2.0 * diagonal) / counts)

def reference(inputs, token_ids, out_cot, pair_ids, w_qkv, b_qv, w_attn, b_attn, norm1_gain, norm1_bias, w_in, b_in, w_out, b_out, norm2_gain, norm2_bias, w_pool, b_pool, scale):
    layer = tuple((arr.astype(jnp.float32) for arr in (w_qkv, b_qv, w_attn, b_attn, norm1_gain, norm1_bias, w_in, b_in, w_out, b_out, norm2_gain, norm2_bias)))
    pool = (w_pool.astype(jnp.float32), b_pool.astype(jnp.float32))
    sents = TOKENS // SEQ
    per_block = math.gcd(sents, 64) * SEQ
    blocks = TOKENS // per_block
    ids_blocks = token_ids.reshape(blocks, per_block)
    cot_blocks = out_cot.astype(jnp.float32).reshape(blocks, per_block, D)

    def objective(layer, values, pool, scale_value):

        def step(carry, pieces):
            rows_in, ids, cot = pieces
            out_rows = layer_block(layer, rows_in, ids)
            emb = embed(out_rows.reshape(-1, SEQ, D)[:, 0, :], pool[0], pool[1])
            return (carry + jnp.sum(out_rows * cot), (out_rows, emb))
        total, (outs, embs) = lax.scan(jax.checkpoint(step), jnp.zeros((), jnp.float32), (values.reshape(blocks, per_block, D), ids_blocks, cot_blocks))
        embs = embs.reshape(sents // 2, 2, D)
        loss = total + ranking(embs[:, 0, :], embs[:, 1, :], pair_ids, scale_value)
        return (loss, outs.reshape(TOKENS, D))
    loss, grad_fn, outputs = jax.vjp(objective, layer, inputs.astype(jnp.float32), pool, scale, has_aux=True)
    g_layer, g_inputs, g_pool, g_scale = grad_fn(jnp.ones((), jnp.float32))
    new_scale = scale - step_rate * g_scale
    return (outputs.astype(jnp.bfloat16), g_inputs, g_layer[0], g_layer[1], g_layer[2], g_layer[3], g_layer[4], g_layer[5], g_layer[6], g_layer[7], g_layer[8], g_layer[9], g_layer[10], g_layer[11], g_pool[0], g_pool[1], new_scale)
```

```python
import jax
import jax.numpy as jnp
from jax import lax
from jax.sharding import PartitionSpec as P

HEAD_DIM = 64
SEQ = 64
SLICES = 8

eps_norm = 1e-12
margin = 0.3
step_rate = 1.0
masked_low = -1e30
high = lax.Precision.HIGHEST
f32 = jnp.float32
low = jnp.bfloat16


def norm_forward(rows_in, gain, shift):
    center = rows_in - jnp.mean(rows_in, axis=-1, keepdims=True)
    inv_std = lax.rsqrt(jnp.mean(center * center, axis=-1, keepdims=True) + eps_norm)
    normed = center * inv_std
    return (normed * gain + shift, normed, inv_std)


def norm_backward(grad_out, normed, inv_std, gain):
    scaled = grad_out * gain
    inner = (
        scaled
        - jnp.mean(scaled, axis=-1, keepdims=True)
        - normed * jnp.mean(scaled * normed, axis=-1, keepdims=True)
    )
    return (inv_std * inner, jnp.sum(grad_out * normed, axis=0), jnp.sum(grad_out, axis=0))


def gelu_slope(pre_act):
    return (
        0.5 * (1.0 + lax.erf(pre_act * 0.7071067811865476))
        + pre_act * jnp.exp(-0.5 * pre_act * pre_act) * 0.3989422804014327
    )


def rank_terms(cosine, same, diag_mask, weight, scale_value, axis_of):
    shifted = cosine - margin * diag_mask
    logits = jnp.where(same, scale_value * shifted, masked_low)
    top = jnp.max(logits, axis=axis_of, keepdims=True)
    lse = top + jnp.log(jnp.sum(jnp.exp(logits - top), axis=axis_of, keepdims=True))
    probs = jnp.exp(logits - lse)
    grad_logit = weight * (probs - diag_mask)
    return (grad_logit, grad_logit * shifted)


def make(mesh):
    n_dp = mesh.shape["dp"]
    n_mp = mesh.shape["mp"]

    def dpx(x, bit):
        return lax.ppermute(x, "dp", [(i, i ^ bit) for i in range(n_dp)])

    def mpx(x, bit):
        return lax.ppermute(x, "mp", [(i, i ^ bit) for i in range(n_mp)])

    def bit_of(axis, bit):
        return (lax.axis_index(axis) & bit) != 0

    def flips(v, axis, bits, dims):
        for bit, dim in zip(bits, dims):
            v = jnp.where(bit_of(axis, bit), jnp.flip(v, dim), v)
        return v

    def gather_plane(r):
        half = r.shape[1] // 2
        at_x, at_y = dpx(r, 2), dpx(r, 4)
        at_d = jnp.concatenate([dpx(at_y[:, :half], 2), dpx(at_x[:, half:], 4)], 1)
        z = jnp.stack([r, at_x, at_y, at_d])
        c = dpx(z, 1)
        v = jnp.stack([z, c], 1)
        return v.reshape((2, 2, 2) + r.shape)

    def gather_block(shard, tie):
        rows = shard.shape[0] // SLICES
        piece = lax.dynamic_slice_in_dim(shard, (lax.axis_index("dp") % SLICES) * rows, rows, 0)
        if tie is not None:
            piece, _ = lax.optimization_barrier((piece, tie))
        r = jnp.stack([mpx(piece, s) for s in range(1, n_mp)])
        v = gather_plane(r)
        v = flips(v, "dp", (4, 2, 1), (0, 1, 2))
        v = v.reshape((SLICES, n_mp - 1, rows, -1)).transpose(1, 0, 2, 3)
        v = v.reshape((n_mp - 1,) + shard.shape)
        return jnp.concatenate([shard[None], v], 0), r

    def reduce_block(g):
        rows = g.shape[1] // SLICES
        half = rows // 2
        v = g.reshape(n_mp, 2, 2, 2, rows, g.shape[2]).transpose(1, 2, 3, 0, 4, 5)
        v = flips(v, "dp", (4, 2, 1), (0, 1, 2)).astype(low)
        v = v[:, :, 0].astype(f32) + dpx(v[:, :, 1], 1).astype(f32)
        a, b = v[..., :half, :].astype(low), v[..., half:, :].astype(low)
        a = a[:, 0].astype(f32) + dpx(a[:, 1], 2).astype(f32)
        b = b[0].astype(f32) + dpx(b[1], 4).astype(f32)
        a, b = a.astype(low), b.astype(low)
        a = a[0].astype(f32) + dpx(a[1], 4).astype(f32)
        b = b[0].astype(f32) + dpx(b[1], 2).astype(f32)
        u = jnp.concatenate([a, b], 1)
        bit = SLICES
        while bit < n_dp:
            w = u.astype(low)
            u = w.astype(f32) + dpx(w, bit).astype(f32)
            bit *= 2
        w = u.astype(low)
        total = w[0].astype(f32)
        for s in range(1, n_mp):
            total = total + mpx(w[s], s).astype(f32)
        return total

    def regather(total):
        v = gather_plane(total.astype(low)[None])
        v = flips(v, "dp", (4, 2, 1), (0, 1, 2))
        return v.reshape(SLICES * total.shape[0], total.shape[1]).astype(f32)

    def sum_all(v):
        bit = 1
        while bit < n_dp:
            v = v + dpx(v, bit)
            bit *= 2
        bit = 1
        while bit < n_mp:
            v = v + mpx(v, bit)
            bit *= 2
        return v

    def mp_natural(v):
        bits = [1 << i for i in reversed(range(n_mp.bit_length() - 1))]
        shape = v.shape
        v = v.reshape((2,) * len(bits) + shape[1:])
        return flips(v, "mp", bits, range(len(bits))).reshape(shape)

    def gather_all(own):
        r = jnp.stack([own] + [mpx(own, s) for s in range(1, n_mp)])
        r = mp_natural(r)
        z = jnp.stack([r] + [dpx(r, b) for b in (2, 4, 6)])
        v = jnp.stack([z, dpx(z, 1)], 1).reshape((2, 2, 2) + r.shape)
        v = flips(v, "dp", (4, 2, 1), (0, 1, 2)).reshape((SLICES,) + r.shape)
        bit = SLICES
        while bit < n_dp:
            o = dpx(v, bit)
            up = bit_of("dp", bit)
            v = jnp.concatenate([jnp.where(up, o, v), jnp.where(up, v, o)], 0)
            bit *= 2
        return v.reshape((n_dp * n_mp,) + own.shape)

    def on_device(
        inputs,
        token_ids,
        out_cot,
        pair_ids,
        w_qkv,
        b_qv,
        w_attn,
        b_attn,
        norm1_gain,
        norm1_bias,
        w_in,
        b_in,
        w_out,
        b_out,
        norm2_gain,
        norm2_bias,
        w_pool,
        b_pool,
        scale,
    ):
        rows = inputs.shape[0]
        width = inputs.shape[1]
        cols = w_qkv.shape[2]
        heads = cols // HEAD_DIM
        sents = rows // SEQ
        gain_one = norm1_gain.astype(f32)
        gain_two = norm2_gain.astype(f32)

        small = jnp.concatenate([b_qv.reshape(-1), b_in])
        small = jnp.stack([small] + [mpx(small, s) for s in range(1, n_mp)]).astype(f32)
        b_q, b_v = small[:, :cols], small[:, cols : 2 * cols]
        b_mid = small[:, 2 * cols :]
        att_shard = jnp.concatenate([w_qkv.transpose(0, 2, 1).reshape(3 * cols, width), w_attn])
        att_all, tie = gather_block(att_shard, None)
        in_all, tie = gather_block(w_in.T, tie)
        out_all, _ = gather_block(w_out, tie)
        att_all = att_all.reshape(n_mp, 4, cols, width)

        qkv = jnp.einsum("td,skcd->kstc", inputs, att_all[:, :3], preferred_element_type=f32)
        biases = jnp.stack([b_q, jnp.zeros_like(b_q), b_v])[:, :, None, :]
        qkv = (qkv + biases).astype(low).reshape(3, n_mp, sents, SEQ, heads, HEAD_DIM)
        query, key_part, value_part = (qkv[0], qkv[1], qkv[2])
        valid = (token_ids != 0).reshape(1, sents, 1, 1, SEQ)
        raw = jnp.einsum("msqhd,mskhd->mshqk", query, key_part, preferred_element_type=f32)
        scores = jnp.where(valid, raw * 0.125, masked_low)
        top = jnp.max(scores, axis=-1, keepdims=True)
        expd = jnp.exp(scores - top)
        totals = jnp.sum(expd, axis=-1, keepdims=True)
        probs = expd / totals
        probs_low = probs.astype(low)
        context = jnp.einsum("mshqk,mskhd->msqhd", probs_low, value_part, preferred_element_type=f32)
        context = context.reshape(n_mp, rows, cols).astype(low)
        attn = jnp.einsum("mte,med->td", context, att_all[:, 3], preferred_element_type=f32)
        normed_one, hat_one, inv_one = norm_forward(
            inputs.astype(f32) + attn + b_attn.astype(f32), gain_one, norm1_bias.astype(f32)
        )
        normed_low = normed_one.astype(low)
        pre_act = jnp.einsum("td,mfd->mtf", normed_low, in_all, preferred_element_type=f32)
        pre_act = pre_act + b_mid[:, None, :]
        hidden = jax.nn.gelu(pre_act, approximate=False).astype(low)
        ffn = jnp.einsum("mtf,mfd->td", hidden, out_all, preferred_element_type=f32)
        out_rows, hat_two, inv_two = norm_forward(
            normed_one + ffn + b_out.astype(f32), gain_two, norm2_bias.astype(f32)
        )
        layer_out = out_rows.astype(low)

        own_first = layer_out.reshape(sents, SEQ, width)[:, 0, :]
        n_all = n_dp * n_mp
        first_rows = gather_all(own_first).reshape(n_all * sents, width)
        npairs = n_all * sents // 2
        pooled = jnp.tanh(
            jnp.dot(first_rows, w_pool, preferred_element_type=f32) + b_pool.astype(f32)
        )
        inv_len = lax.rsqrt(jnp.sum(pooled * pooled, axis=-1, keepdims=True) + eps_norm)
        emb_full = pooled * inv_len
        emb_pairs = emb_full.astype(low).reshape(npairs, 2, width)
        all_src, all_tgt = emb_pairs[:, 0, :], emb_pairs[:, 1, :]
        scale_value = scale[0]
        cosine = jnp.einsum("kd,md->km", all_src, all_tgt, preferred_element_type=f32)
        same = pair_ids[:, None] == pair_ids[None, :]
        counts = jnp.sum(same.astype(f32), axis=1)
        index_all = jnp.arange(npairs)
        diag_mask = (index_all[:, None] == index_all[None, :]).astype(f32)
        grad_row, part_row = rank_terms(
            cosine, same, diag_mask, (1.0 / counts)[:, None], scale_value, 1
        )
        grad_col, part_col = rank_terms(
            cosine, same, diag_mask, (1.0 / counts)[None, :], scale_value, 0
        )
        grad_all = grad_row + grad_col
        grad_src = scale_value * jnp.dot(grad_all, all_tgt.astype(f32), precision=high)
        grad_tgt = scale_value * jnp.einsum(
            "km,kd->md", grad_all, all_src.astype(f32), precision=high
        )
        new_scale = scale - step_rate * (jnp.sum(part_row) + jnp.sum(part_col))
        grad_emb = jnp.stack([grad_src, grad_tgt], axis=1).reshape(2 * npairs, width)
        grad_pooled = inv_len * (
            grad_emb - emb_full * jnp.sum(emb_full * grad_emb, axis=-1, keepdims=True)
        )
        grad_ppre = (grad_pooled * (1.0 - pooled * pooled)).astype(low)
        grad_pool = jnp.einsum("sd,se->de", first_rows, grad_ppre, preferred_element_type=f32)
        grad_b_pool = jnp.sum(grad_ppre.astype(f32), axis=0)
        own_ppre = lax.dynamic_slice_in_dim(
            grad_ppre, lax.axis_index(("dp", "mp")) * sents, sents, 0
        )
        grad_first = jnp.einsum("se,de->sd", own_ppre, w_pool, preferred_element_type=f32)
        grad_out = out_cot.astype(f32).reshape(sents, SEQ, width)
        grad_out = grad_out.at[:, 0, :].add(grad_first).reshape(rows, width)

        grad_z2, grad_norm2_gain, grad_norm2_bias = norm_backward(
            grad_out, hat_two, inv_two, gain_two
        )
        grad_b_out = jnp.sum(grad_z2, axis=0)
        grad_ffn = grad_z2.astype(low)
        grad_w_out = jnp.einsum("mtf,td->mfd", hidden, grad_ffn, preferred_element_type=f32)
        red_out = reduce_block(grad_w_out)
        grad_hidden = jnp.einsum("td,mfd->mtf", grad_ffn, out_all, preferred_element_type=f32)
        grad_pre = (grad_hidden * gelu_slope(pre_act)).astype(low)
        grad_b_in = jnp.sum(grad_pre.astype(f32), axis=1)
        grad_w_in = jnp.einsum("mtf,td->mfd", grad_pre, normed_low, preferred_element_type=f32)
        red_in = reduce_block(grad_w_in)
        grad_h1 = grad_z2 + jnp.einsum(
            "mtf,mfd->td", grad_pre, in_all, preferred_element_type=f32
        )
        grad_z1, grad_norm1_gain, grad_norm1_bias = norm_backward(
            grad_h1, hat_one, inv_one, gain_one
        )
        grad_b_attn = jnp.sum(grad_z1, axis=0)
        grad_att_low = grad_z1.astype(low)
        grad_attn = jnp.einsum("mte,td->med", context, grad_att_low, preferred_element_type=f32)
        grad_context = jnp.einsum(
            "td,med->mte", grad_att_low, att_all[:, 3], preferred_element_type=f32
        )
        grad_context = grad_context.astype(low).reshape(n_mp, sents, SEQ, heads, HEAD_DIM)
        grad_value = jnp.einsum(
            "mshqk,msqhd->mskhd", probs_low, grad_context, preferred_element_type=f32
        )
        grad_probs = jnp.einsum(
            "msqhd,mskhd->mshqk", grad_context, value_part, preferred_element_type=f32
        )
        inner_sum = jnp.sum(probs * grad_probs, axis=-1, keepdims=True)
        grad_raw = jnp.where(valid, probs * (grad_probs - inner_sum) * 0.125, 0.0).astype(low)
        grad_query = jnp.einsum("mshqk,mskhd->msqhd", grad_raw, key_part, preferred_element_type=f32)
        grad_key = jnp.einsum("mshqk,msqhd->mskhd", grad_raw, query, preferred_element_type=f32)
        grad_rows = (
            jnp.stack([grad_query, grad_key, grad_value], 1).astype(low).reshape(n_mp, 3, rows, cols)
        )
        grad_b_qv = jnp.sum(grad_rows[:, 0::2].astype(f32), axis=2)
        grad_qkv = jnp.einsum("mkte,td->mked", grad_rows, inputs, preferred_element_type=f32)
        grad_att = jnp.concatenate([grad_qkv, grad_attn[:, None]], 1).reshape(
            n_mp, 4 * cols, width
        )
        red_att = reduce_block(grad_att)
        input_grad = grad_z1 + jnp.einsum(
            "mkte,mked->td", grad_rows, att_all[:, :3], preferred_element_type=f32
        )
        late = jnp.concatenate(
            [mp_natural(grad_b_qv).reshape(-1), grad_b_attn, grad_norm1_gain, grad_norm1_bias]
        )
        early = jnp.concatenate(
            [mp_natural(grad_b_in).reshape(-1), grad_b_out, grad_norm2_gain, grad_norm2_bias]
        )
        late, early = sum_all(late), sum_all(early)
        n_qv, n_in = n_mp * 2 * cols, early.shape[0] - 3 * width
        take = lax.axis_index("mp")
        out_b_qv = lax.dynamic_slice_in_dim(late[:n_qv].reshape(n_mp, 2, cols), take, 1, 0)[0]
        out_b_in = lax.dynamic_slice_in_dim(early[:n_in].reshape(n_mp, -1), take, 1, 0)[0]
        late, early = late[n_qv:].reshape(3, width), early[n_in:].reshape(3, width)
        done_out = regather(red_out)
        done_in = regather(red_in).T
        done_att = regather(red_att)
        done_qkv = done_att[: 3 * cols].reshape(3, cols, width).transpose(0, 2, 1)
        return (
            layer_out,
            input_grad,
            done_qkv,
            out_b_qv,
            done_att[3 * cols :],
            late[0],
            late[1],
            late[2],
            done_in,
            out_b_in,
            done_out,
            early[0],
            early[1],
            early[2],
            grad_pool,
            grad_b_pool,
            new_scale,
        )

    return on_device


def solution(mesh):
    rows, whole = P(("dp", "mp"), None), P()
    in_specs = (
        rows,
        P(("dp", "mp")),
        rows,
        whole,
        P(None, None, "mp"),
        P(None, "mp"),
        P("mp", None),
        whole,
        whole,
        whole,
        P(None, "mp"),
        P("mp"),
        P("mp", None),
        whole,
        whole,
        whole,
        whole,
        whole,
        whole,
    )
    out_specs = (
        rows,
        rows,
        P(None, None, "mp"),
        P(None, "mp"),
        P("mp", None),
        whole,
        whole,
        whole,
        P(None, "mp"),
        P("mp"),
        P("mp", None),
        whole,
        whole,
        whole,
        whole,
        whole,
        whole,
    )
    return jax.shard_map(
        make(mesh), mesh=mesh, in_specs=in_specs, out_specs=out_specs, check_vma=False
    )
```

```python
import functools

import jax
import jax.numpy as jnp
from jax import lax
from jax.experimental import pallas as pl
from jax.experimental.pallas import tpu as pltpu
from jax.sharding import PartitionSpec as P

HEAD_DIM = 64
SEQ = 64
SLICES = 8
PARTS = 10
PAIR = 2 * SEQ
LANES = 2 * HEAD_DIM
BLOCK = 8

eps_norm = 1e-12
margin = 0.3
step_rate = 1.0
masked_low = -1e30
high = lax.Precision.HIGHEST
f32 = jnp.float32
low = jnp.bfloat16
VMEM_BYTES = 58 << 20


def nn(a, b):
    return jnp.dot(a, b, preferred_element_type=f32)


def nt(a, b):
    return lax.dot_general(a, b, (((1,), (1,)), ((), ())), preferred_element_type=f32)


def tn(a, b):
    return lax.dot_general(a, b, (((0,), (0,)), ((), ())), preferred_element_type=f32)


def rank_terms(cosine, same, diag_mask, weight, scale_value, axis_of):
    shifted = cosine - margin * diag_mask
    logits = jnp.where(same, scale_value * shifted, masked_low)
    top = jnp.max(logits, axis=axis_of, keepdims=True)
    lse = top + jnp.log(jnp.sum(jnp.exp(logits - top), axis=axis_of, keepdims=True))
    probs = jnp.exp(logits - lse)
    grad_logit = weight * (probs - diag_mask)
    return (grad_logit, grad_logit * shifted)


def call(body, ins, outs, scratch, micros):
    def spec(vmem):
        return pl.BlockSpec(memory_space=pltpu.VMEM if vmem else pl.ANY)

    return pl.pallas_call(
        body,
        out_shape=[jax.ShapeDtypeStruct(o.shape, o.dtype) for o, _ in outs],
        in_specs=[spec(v) for _, v in ins],
        out_specs=[spec(v) for _, v in outs],
        scratch_shapes=scratch,
        compiler_params=pltpu.CompilerParams(vmem_limit_bytes=VMEM_BYTES),
        cost_estimate=pl.CostEstimate(flops=int(micros * 1.1e9), bytes_accessed=0, transcendentals=0),
    )(*[a for a, _ in ins])


def slot(p):
    me = lax.rem(lax.axis_index("dp"), SLICES)
    return jnp.bitwise_xor(me, p)


def start_all(copies):
    for c in copies:
        c.start()
    return copies


def wait_all(copies):
    for c in copies:
        c.wait()


def att_spot(ref, s, p, cols, size, first=0, rows=None):
    at = slot(p)
    row = pl.multiple_of(s * cols + lax.rem(at, 2) * size + first, 16)
    return ref.at[at // 2, pl.ds(row, rows or size)]


def row_spot(ref, s, p, size, first=0, rows=None):
    return ref.at[s, pl.ds(pl.multiple_of(slot(p) * size + first, 16), rows or size)]


def slices_of(parts):
    full = parts[0].shape[-2]
    half = full // 2
    count = len(parts) // 2
    out = []
    for c in (0, 1):
        own, at_x, at_y, *rest = parts[count * c : count * (c + 1)]
        out += [(own, c, 0, full), (at_x, 2 + c, 0, full), (at_y, 4 + c, 0, full)]
        if len(rest) == 1:
            out += [(rest[0], 6 + c, 0, full)]
        else:
            out += [(rest[0], 6 + c, 0, half), (rest[1], 6 + c, half, half)]
    return out


def fetch_att(own_qkv, own_o, parts, dst, sem, cols):
    copies = []
    for i in range(3):
        copies.append(pltpu.make_async_copy(own_qkv.at[i], dst.at[i, pl.ds(0, cols)], sem.at[i]))
    copies.append(pltpu.make_async_copy(own_o, dst.at[3, pl.ds(0, cols)], sem.at[3]))
    k = 4
    size = parts[0].shape[1]
    for part, p, at, n in slices_of(parts):
        for s in range(part.shape[0]):
            spot = att_spot(dst, s + 1, p, cols, size, at, n)
            copies.append(pltpu.make_async_copy(part.at[s], spot, sem.at[k]))
            k += 1
    return start_all(copies)


def fetch_rows(own, parts, dst, sem, base):
    copies = [pltpu.make_async_copy(own, dst.at[0], sem.at[base])]
    k = base + 1
    size = parts[0].shape[1]
    for part, p, at, n in slices_of(parts):
        for s in range(part.shape[0]):
            spot = row_spot(dst, s + 1, p, size, at, n)
            copies.append(pltpu.make_async_copy(part.at[s], spot, sem.at[k]))
            k += 1
    return start_all(copies)


def n_copies(n_mp):
    return 4 + PARTS * (n_mp - 1)


def send_slices(src_of, g_keep, g_send, sem, n_mp):
    copies = []
    k = 0
    for p in range(SLICES):
        dst = g_send if p & 1 else g_keep
        for s in range(n_mp):
            spot = dst.at[s // 2, p >> 2, (p >> 1) & 1, s % 2]
            copies.append(pltpu.make_async_copy(src_of(s, p), spot, sem.at[k]))
            k += 1
    return start_all(copies)


def mean_of(v):
    return jnp.sum(v, axis=-1, keepdims=True) * (1.0 / v.shape[-1])


def norm_rows(z):
    center = z - mean_of(z)
    inv = lax.rsqrt(mean_of(center * center) + eps_norm)
    return center * inv, inv


def norm_back(grad_out, hat, inv, gain):
    scaled = grad_out * gain
    return inv * (scaled - mean_of(scaled) - hat * mean_of(scaled * hat))


def pair_mask(ids_row):
    row = lax.broadcasted_iota(jnp.int32, (PAIR, PAIR), 0) >= SEQ
    col = lax.broadcasted_iota(jnp.int32, (PAIR, PAIR), 1) >= SEQ
    return jnp.logical_and(row == col, ids_row != 0)


def split_heads(v):
    first = lax.broadcasted_iota(jnp.int32, v.shape, 1) < HEAD_DIM
    zero = jnp.zeros_like(v)
    return jnp.concatenate([jnp.where(first, v, zero), jnp.where(first, zero, v)], axis=0)


def join_heads(v):
    half = v.shape[0] // 2
    first = lax.broadcasted_iota(jnp.int32, (half, v.shape[1]), 1) < HEAD_DIM
    return jnp.where(first, v[:half], v[half:])


def softmax_of(scores, mask):
    scores = jnp.where(mask, scores * 0.125, masked_low)
    expd = jnp.exp(scores - jnp.max(scores, axis=-1, keepdims=True))
    return expd / jnp.sum(expd, axis=-1, keepdims=True)


def attention_forward(n_mp, cols, *refs):
    x, ids, b_q, b_v, b_attn, gain, shift, own_qkv, own_o = refs[:9]
    parts = refs[9 : 9 + PARTS]
    q, k, v, ctx, hat_out, inv_out, h1 = refs[19:26]
    w, sem = refs[26:]
    copies = fetch_att(own_qkv, own_o, parts, w, sem, cols)
    wait_all(copies)
    rows, width = x.shape
    q[...] = (nt(x[...], w[0]) + b_q[...]).astype(low)
    k[...] = nt(x[...], w[1]).astype(low)
    v[...] = (nt(x[...], w[2]) + b_v[...]).astype(low)

    @pl.loop(0, rows // PAIR)
    def _(t):
        at = pl.ds(pl.multiple_of(t * PAIR, PAIR), PAIR)
        mask = pair_mask(ids[t])
        for j in range(width // LANES):
            lanes = slice(j * LANES, (j + 1) * LANES)
            raw = nt(q[at, lanes], split_heads(k[at, lanes]))
            probs = [softmax_of(raw[:, i * PAIR : (i + 1) * PAIR], mask).astype(low) for i in (0, 1)]
            out = nn(jnp.concatenate(probs, axis=1), split_heads(v[at, lanes]))
            ctx[at, lanes] = out.astype(low)

    z = x[...].astype(f32) + nn(ctx[...], w[3]) + b_attn[...]
    hat, inv = norm_rows(z)
    hat_out[...] = hat
    inv_out[...] = jnp.broadcast_to(inv, inv_out.shape)
    h1[...] = (hat * gain[...] + shift[...]).astype(low)


def gelu_pair(pre):
    size = jnp.abs(pre)
    t = 1.0 / (1.0 + 0.2316418882663604 * size)
    bell = jnp.exp(-0.5 * pre * pre)
    poly = t * (
        0.127414796
        + t * (-0.142248368 + t * (0.7107068705 + t * (-0.7265760135 + t * 0.5307027145)))
    )
    tail = poly * bell
    phi = jnp.where(pre >= 0.0, 1.0 - tail, tail)
    return pre * phi, phi + pre * (bell * 0.3989422804014327)


def ffn_in_forward(n_mp, *refs):
    h1, b_mid, own_in = refs[:3]
    parts = refs[3 : 3 + SLICES]
    hidden, slope, w_in, sem = refs[11:]
    wait_all(fetch_rows(own_in, parts, w_in, sem, 0))

    @pl.loop(0, n_mp)
    def _(s):
        pre = nn(h1[...], w_in[s]) + b_mid[s]
        act, grad = gelu_pair(pre)
        hidden[s] = act.astype(low)
        slope[s] = grad.astype(low)


def ffn_out_forward(n_mp, *refs):
    hidden, hat1, gain1, shift1, b_out, gain2, shift2, own_out = refs[:8]
    parts = refs[8 : 8 + SLICES]
    layer_out, hat_out, inv_out, first = refs[16:20]
    w_out, acc, sem = refs[20:]
    copies = fetch_rows(own_out, parts, w_out, sem, 0)
    acc[...] = hat1[...] * gain1[...] + shift1[...] + b_out[...]
    wait_all(copies)

    @pl.loop(0, n_mp)
    def _(s):
        acc[...] += nn(hidden[s], w_out[s])

    hat, inv = norm_rows(acc[...])
    hat_out[...] = hat
    inv_out[...] = jnp.broadcast_to(inv, inv_out.shape)
    out = (hat * gain2[...] + shift2[...]).astype(low)
    layer_out[...] = out
    first[...] = jnp.zeros_like(first)
    for i in range(out.shape[0] // SEQ):
        first[i : i + 1] = out[i * SEQ : i * SEQ + 1].astype(f32)


def out_backward(n_mp, *refs):
    cot, g_first, hat, inv, gain, hidden = refs[:6]
    g_z2, small, keep, send = refs[6:10]
    g_w, sem = refs[10:]
    rows = cot.shape[0]
    g_z2[...] = cot[...].astype(f32)
    for i in range(rows // SEQ):
        g_z2[i * SEQ : i * SEQ + 1] += g_first[i : i + 1]
    g_y = g_z2[...]
    small[...] = jnp.zeros_like(small)
    small[1:2] = jnp.sum(g_y * hat[...], axis=0, keepdims=True)
    small[2:3] = jnp.sum(g_y, axis=0, keepdims=True)
    g_z = norm_back(g_y, hat[...], inv[:, :1], gain[...])
    g_z2[...] = g_z
    small[0:1] = jnp.sum(g_z, axis=0, keepdims=True)
    g_ffn = g_z.astype(low)

    @pl.loop(0, n_mp)
    def _(s):
        g_w[s] = tn(hidden[s], g_ffn).astype(low)

    size = keep.shape[-2]
    wait_all(send_slices(lambda s, p: row_spot(g_w, s, p, size), keep, send, sem, n_mp))


def in_backward(n_mp, *refs):
    g_z2, slope, h1, hat, inv, gain, own_in, own_out = refs[:8]
    in_parts = refs[8 : 8 + SLICES]
    out_parts = refs[16 : 16 + SLICES]
    g_z1, g_mid, small, keep, send = refs[24:29]
    w_in, w_out, g_w, acc, sem, sem2 = refs[29:]
    copies = fetch_rows(own_in, in_parts, w_in, sem, 0)
    copies += fetch_rows(own_out, out_parts, w_out, sem, n_copies(n_mp))
    wait_all(copies)
    acc[...] = g_z2[...]
    g_ffn = g_z2[...].astype(low)

    @pl.loop(0, n_mp)
    def _(s):
        g_pre = (nt(g_ffn, w_out[s]) * slope[s].astype(f32)).astype(low)
        g_mid[s] = jnp.sum(g_pre.astype(f32), axis=0, keepdims=True)
        g_w[s] = tn(h1[...], g_pre).astype(low)
        acc[...] += nt(g_pre, w_in[s])

    size = keep.shape[-2]
    copies = send_slices(lambda s, p: row_spot(g_w, s, p, size), keep, send, sem2, n_mp)
    g_h1 = acc[...]
    small[...] = jnp.zeros_like(small)
    small[1:2] = jnp.sum(g_h1 * hat[...], axis=0, keepdims=True)
    small[2:3] = jnp.sum(g_h1, axis=0, keepdims=True)
    g_z = norm_back(g_h1, hat[...], inv[:, :1], gain[...])
    g_z1[...] = g_z
    small[0:1] = jnp.sum(g_z, axis=0, keepdims=True)
    wait_all(copies)


def attention_backward(n_mp, cols, *refs):
    g_z1, q, k, v, ctx, ids, own_qkv, own_o = refs[:8]
    parts = refs[8 : 8 + PARTS]
    g_q, g_k, g_v, g_bias, g_wo = refs[18:23]
    w, g_ctx, sem = refs[23:]
    copies = fetch_att(own_qkv, own_o, parts, w, sem, cols)
    rows, width = g_z1.shape
    g_attn = g_z1[...].astype(low)
    wait_all(copies)
    g_ctx[...] = nt(g_attn, w[3]).astype(low)

    @pl.loop(0, rows // PAIR)
    def _(t):
        at = pl.ds(pl.multiple_of(t * PAIR, PAIR), PAIR)
        mask = pair_mask(ids[t])
        for j in range(width // LANES):
            lanes = slice(j * LANES, (j + 1) * LANES)
            q2, g2 = q[at, lanes], g_ctx[at, lanes]
            k2, v2 = split_heads(k[at, lanes]), split_heads(v[at, lanes])
            raw = nt(q2, k2)
            g_p = nt(g2, v2)
            p_low, g_raw = [], []
            for i in (0, 1):
                half = slice(i * PAIR, (i + 1) * PAIR)
                p = softmax_of(raw[:, half], mask)
                inner = jnp.sum(p * g_p[:, half], axis=-1, keepdims=True)
                p_low.append(p.astype(low))
                g_raw.append((p * (g_p[:, half] - inner) * 0.125).astype(low))
            p_low = jnp.concatenate(p_low, axis=1)
            g_raw = jnp.concatenate(g_raw, axis=1)
            g_v[at, lanes] = join_heads(tn(p_low, g2)).astype(low)
            g_q[at, lanes] = nn(g_raw, k2).astype(low)
            g_k[at, lanes] = join_heads(tn(g_raw, q2)).astype(low)

    g_wo[...] = tn(ctx[...], g_attn).astype(low)
    g_bias[...] = jnp.zeros_like(g_bias)
    g_bias[0:1] = jnp.sum(g_q[...].astype(f32), axis=0, keepdims=True)
    g_bias[1:2] = jnp.sum(g_v[...].astype(f32), axis=0, keepdims=True)


def attention_weights(n_mp, cols, *refs):
    x, g_q, g_k, g_v, g_wo, keep, send, g_w, sem = refs
    g_w[3] = g_wo[...]
    g_w[0] = tn(g_q[...], x[...]).astype(low)
    g_w[1] = tn(g_k[...], x[...]).astype(low)
    g_w[2] = tn(g_v[...], x[...]).astype(low)
    size = keep.shape[-2]
    wait_all(send_slices(lambda s, p: att_spot(g_w, s, p, cols, size), keep, send, sem, n_mp))


def attention_inputs(n_mp, cols, *refs):
    g_z1, g_q, g_k, g_v, own_qkv, own_o = refs[:6]
    parts = refs[6 : 6 + PARTS]
    g_x, w, sem = refs[16:]
    wait_all(fetch_att(own_qkv, own_o, parts, w, sem, cols))
    g_x[...] = g_z1[...] + nn(g_q[...], w[0]) + nn(g_k[...], w[1]) + nn(g_v[...], w[2])


def finish_rows(*refs):
    parts = refs[:SLICES]
    out_a, out_b, got, sem = refs[SLICES:]
    size = parts[0].shape[0] // 2
    copies = []
    for p in range(SLICES):
        for i in (0, 1):
            part = parts[p].at[pl.ds(i * size, size)]
            spot = row_spot(got, i, p, size)
            copies.append(pltpu.make_async_copy(part, spot, sem.at[2 * p + i]))
    wait_all(start_all(copies))
    out_a[...] = got[0].astype(f32)
    out_b[...] = got[1].astype(f32)


def finish_att(cols, *refs):
    parts = refs[:SLICES]
    out_qkv, out_o, got, sem = refs[SLICES:]
    size = parts[0].shape[0]
    copies = [
        pltpu.make_async_copy(parts[p], att_spot(got, 0, p, cols, size), sem.at[p])
        for p in range(SLICES)
    ]
    wait_all(start_all(copies))
    for i in range(3):
        out_qkv[i] = got[i].astype(f32).T
    out_o[...] = got[3].astype(f32)


def make(mesh):
    n_dp = mesh.shape["dp"]
    n_mp = mesh.shape["mp"]

    def dpx(x, bit):
        return lax.ppermute(x, "dp", [(i, i ^ bit) for i in range(n_dp)])

    def mpx(x, bit):
        return lax.ppermute(x, "mp", [(i, i ^ bit) for i in range(n_mp)])

    def bit_of(axis, bit):
        return (lax.axis_index(axis) & bit) != 0

    def flips(v, axis, bits, dims):
        for bit, dim in zip(bits, dims):
            v = jnp.where(bit_of(axis, bit), jnp.flip(v, dim), v)
        return v

    def plane_parts(r):
        got = [None] * SLICES
        for p in (0, 2, 4, 6):
            got[p] = dpx(r, p) if p else r
        for p in (0, 2, 4, 6):
            got[p + 1] = dpx(got[p], 1)
        return got

    def over_z(piece):
        return [mpx(piece, i) for i in range(1, n_mp)]

    def over_xy(r):
        return [dpx(r, 2), dpx(r, 4)]

    def over_plane(r):
        return [dpx(r, 2), dpx(r, 4), dpx(r, 6)]

    def over_corner(near):
        at_x, at_y = near
        half = at_x.shape[1] // 2
        return [dpx(at_y[:, :half], 2), dpx(at_x[:, half:], 4)]

    def over_core(parts):
        return parts + [dpx(part, 1) for part in parts]

    def after(x, *deps):
        return lax.optimization_barrier((x, deps))[0]

    def own_piece(shard):
        rows = shard.shape[0] // SLICES
        return lax.dynamic_slice_in_dim(shard, (lax.axis_index("dp") % SLICES) * rows, rows, 0)

    def add(a, b):
        return (a.astype(f32) + b.astype(f32)).astype(low)

    def reduce_one(keep, got):
        return (
            add(keep[0, :, 1], got[0, :, 1]),
            add(keep[1, 1], got[1, 1]),
            add(keep[0, :, 0], got[0, :, 0]),
            add(keep[1, 0], got[1, 0]),
        )

    def reduce_two(a0, b0, a1, b1):
        return add(a0[1], a1[1]), add(b0[1], b1[1]), a0[0], a1[0], b0[0], b1[0]

    def reduce_three(a0, a1, b0, b1, a2, b2):
        a = a0.astype(f32) + a1.astype(f32) + a2.astype(f32)
        b = b0.astype(f32) + b1.astype(f32) + b2.astype(f32)
        u = [a[0], a[1], b[0], b[1]]
        bit = SLICES
        while bit < n_dp:
            u = [w.astype(low) for w in u]
            u = [w.astype(f32) + dpx(w, bit).astype(f32) for w in u]
            bit *= 2
        return [w.astype(low) for w in u]

    def reduce_last(u):
        total = u[0].astype(f32)
        for w in u[1:]:
            total = total + w.astype(f32)
        return total.astype(low)

    def sum_all(v):
        bit = 1
        while bit < n_dp:
            v = v + dpx(v, bit)
            bit *= 2
        bit = 1
        while bit < n_mp:
            v = v + mpx(v, bit)
            bit *= 2
        return v

    def mp_natural(v):
        bits = [1 << i for i in reversed(range(n_mp.bit_length() - 1))]
        shape = v.shape
        v = v.reshape((2,) * len(bits) + shape[1:])
        return flips(v, "mp", bits, range(len(bits))).reshape(shape)

    def gather_all(own):
        r = jnp.stack([own] + [mpx(own, s) for s in range(1, n_mp)])
        r = mp_natural(r)
        z = jnp.stack([r] + [dpx(r, b) for b in (2, 4, 6)])
        v = jnp.stack([z, dpx(z, 1)], 1).reshape((2, 2, 2) + r.shape)
        v = flips(v, "dp", (4, 2, 1), (0, 1, 2)).reshape((SLICES,) + r.shape)
        bit = SLICES
        while bit < n_dp:
            o = dpx(v, bit)
            up = bit_of("dp", bit)
            v = jnp.concatenate([jnp.where(up, o, v), jnp.where(up, v, o)], 0)
            bit *= 2
        return v.reshape((n_dp * n_mp,) + own.shape)

    def rank_part(first_rows, sents, pair_ids, w_pool, b_pool, scale):
        n_all = n_dp * n_mp
        width = first_rows.shape[-1]
        first_rows = first_rows[:, :sents].reshape(n_all * sents, width).astype(low)
        npairs = n_all * sents // 2
        pooled = jnp.tanh(
            jnp.dot(first_rows, w_pool, preferred_element_type=f32) + b_pool.astype(f32)
        )
        inv_len = lax.rsqrt(jnp.sum(pooled * pooled, axis=-1, keepdims=True) + eps_norm)
        emb_full = pooled * inv_len
        emb_pairs = emb_full.astype(low).reshape(npairs, 2, width)
        all_src, all_tgt = emb_pairs[:, 0, :], emb_pairs[:, 1, :]
        scale_value = scale[0]
        cosine = jnp.einsum("kd,md->km", all_src, all_tgt, preferred_element_type=f32)
        same = pair_ids[:, None] == pair_ids[None, :]
        counts = jnp.sum(same.astype(f32), axis=1)
        index_all = jnp.arange(npairs)
        diag_mask = (index_all[:, None] == index_all[None, :]).astype(f32)
        grad_row, part_row = rank_terms(
            cosine, same, diag_mask, (1.0 / counts)[:, None], scale_value, 1
        )
        grad_col, part_col = rank_terms(
            cosine, same, diag_mask, (1.0 / counts)[None, :], scale_value, 0
        )
        grad_all = grad_row + grad_col
        grad_src = scale_value * jnp.dot(grad_all, all_tgt.astype(f32), precision=high)
        grad_tgt = scale_value * jnp.einsum(
            "km,kd->md", grad_all, all_src.astype(f32), precision=high
        )
        new_scale = scale - step_rate * (jnp.sum(part_row) + jnp.sum(part_col))
        grad_emb = jnp.stack([grad_src, grad_tgt], axis=1).reshape(2 * npairs, width)
        grad_pooled = inv_len * (
            grad_emb - emb_full * jnp.sum(emb_full * grad_emb, axis=-1, keepdims=True)
        )
        grad_ppre = (grad_pooled * (1.0 - pooled * pooled)).astype(low)
        grad_pool = jnp.einsum("sd,se->de", first_rows, grad_ppre, preferred_element_type=f32)
        grad_b_pool = jnp.sum(grad_ppre.astype(f32), axis=0)
        own_ppre = lax.dynamic_slice_in_dim(
            grad_ppre, lax.axis_index(("dp", "mp")) * sents, sents, 0
        )
        grad_first = jnp.einsum("se,de->sd", own_ppre, w_pool, preferred_element_type=f32)
        grad_first = jnp.pad(grad_first, ((0, BLOCK - sents), (0, 0)))
        return grad_first, grad_pool, grad_b_pool, new_scale

    def on_device(
        inputs,
        token_ids,
        out_cot,
        pair_ids,
        w_qkv,
        b_qv,
        w_attn,
        b_attn,
        norm1_gain,
        norm1_bias,
        w_in,
        b_in,
        w_out,
        b_out,
        norm2_gain,
        norm2_bias,
        w_pool,
        b_pool,
        scale,
    ):
        rows, width = inputs.shape
        cols = w_qkv.shape[2]
        units = w_in.shape[1]
        sents = rows // SEQ
        shape = jax.ShapeDtypeStruct
        dma = pltpu.SemaphoreType.DMA
        vmem = pltpu.VMEM

        def row(v):
            return v.astype(f32)[None, :]

        qkv_t = w_qkv.transpose(0, 2, 1)
        att_shard = jnp.concatenate([qkv_t.reshape(3 * cols, width), w_attn])
        size = att_shard.shape[0] // SLICES
        small = jnp.pad(jnp.concatenate([b_qv.reshape(-1), b_in]), (0, 2 * width - 2 * cols - units))
        small = small.reshape(2, width)
        att_r = over_z(jnp.concatenate([own_piece(att_shard), small]))
        small = jnp.stack([small] + [r[size:] for r in att_r]).reshape(n_mp, -1).astype(f32)
        b_q, b_v = small[:, :cols].reshape(1, -1), small[:, cols : 2 * cols].reshape(1, -1)
        b_mid = small[:, None, 2 * cols : 2 * cols + units]
        att_r = jnp.stack([r[:size] for r in att_r])
        att_near = over_xy(att_r)
        in_r = jnp.stack(over_z(after(own_piece(w_in), att_r)))
        att_parts = over_core([att_r] + att_near + over_corner(att_near))
        in_near = over_plane(after(in_r, *att_near))
        out_own = after(own_piece(w_out), in_r, *att_near)
        out_z = [mpx(out_own, 1)]
        bit = 2
        while bit < n_mp:
            far = mpx(jnp.stack([out_own] + out_z), bit)
            out_z += [far[i] for i in range(bit)]
            bit *= 2
        nc = n_copies(n_mp)
        own_qkv = att_shard[: 3 * cols].reshape(3, cols, width)

        def here(*arrays):
            return [(a, True) for a in arrays]

        def away(*arrays):
            return [(a, False) for a in arrays]

        gain_one, shift_one = row(norm1_gain), row(norm1_bias)
        gain_two, shift_two = row(norm2_gain), row(norm2_bias)
        ids = token_ids.reshape(rows // PAIR, 1, PAIR)

        rows_low, rows_f = shape((rows, width), low), shape((rows, width), f32)
        thin = shape((rows, 128), f32)
        query, key_part, value_part, context, hat_one, inv_one, h1 = call(
            functools.partial(attention_forward, n_mp, cols),
            here(after(inputs, out_z[0]), ids, b_q, b_v, row(b_attn), gain_one, shift_one)
            + away(own_qkv, w_attn, *att_parts),
            here(rows_low, rows_low, rows_low, rows_low, rows_f, thin, rows_low),
            [vmem((4, n_mp * cols, width), low), dma((nc,))],
            11,
        )
        out_r = jnp.stack(after(out_z, h1))
        out_near = over_plane(out_r)
        in_parts = over_core(after([in_r] + in_near, h1))
        mid = shape((n_mp, rows, units), low)
        hidden, slope = call(
            functools.partial(ffn_in_forward, n_mp),
            here(h1, b_mid) + away(w_in, *in_parts),
            here(mid, mid),
            [vmem((n_mp, width, units), low), dma((nc,))],
            9,
        )
        out_parts = over_core(after([out_r] + out_near, hidden))
        layer_out, hat_two, inv_two, own_first = call(
            functools.partial(ffn_out_forward, n_mp),
            here(hidden, hat_one, gain_one, shift_one, row(b_out), gain_two, shift_two)
            + away(w_out, *out_parts),
            here(rows_low, rows_f, thin, shape((BLOCK, width), f32)),
            [vmem((n_mp, units, width), low), vmem((rows, width), f32), dma((nc,))],
            6,
        )
        grad_first, grad_pool, grad_b_pool, new_scale = rank_part(
            gather_all(own_first), sents, pair_ids, w_pool, b_pool, scale
        )
        lot = shape((2, 2, 2, n_mp // 2, size, width), low)
        tiny = shape((BLOCK, width), f32)
        grad_z2, small_two, keep_o, send = call(
            functools.partial(out_backward, n_mp),
            here(out_cot, grad_first, hat_two, inv_two, gain_two, hidden),
            here(rows_f, tiny) + away(lot, lot),
            [vmem((n_mp, units, width), low), dma((SLICES * n_mp,))],
            10,
        )
        got_o = dpx(send, 1)
        grad_z1, grad_b_in, small_one, keep_i, send = call(
            functools.partial(in_backward, n_mp),
            here(grad_z2, slope, h1, hat_one, inv_one, gain_one) + away(w_in, w_out, *in_parts, *out_parts),
            here(rows_f, shape((n_mp, 1, units), f32), tiny) + away(lot, lot),
            [
                vmem((n_mp, width, units), low),
                vmem((n_mp, units, width), low),
                vmem((n_mp, width, units), low),
                vmem((rows, width), f32),
                dma((2 * nc,)),
                dma((SLICES * n_mp,)),
            ],
            17,
        )
        got_i = dpx(send, 1)
        step_o = reduce_one(keep_o, after(got_o, grad_z1))
        a_o, b_o = dpx(step_o[0], 2), dpx(step_o[1], 4)
        grad_q, grad_k, grad_v, grad_b_qv, grad_wo = call(
            functools.partial(attention_backward, n_mp, cols),
            here(after(grad_z1, step_o[0], step_o[1]), query, key_part, value_part, context, ids)
            + away(own_qkv, w_attn, *att_parts),
            here(rows_low, rows_low, rows_low, tiny, shape((n_mp * cols, width), low)),
            [vmem((4, n_mp * cols, width), low), vmem((rows, width), low), dma((nc,))],
            12,
        )
        step_i = reduce_one(keep_i, after(got_i, grad_q))
        a_i, b_i = dpx(step_i[0], 2), dpx(step_i[1], 4)
        step_o = reduce_two(step_o[2], step_o[3], after(a_o, grad_q), after(b_o, grad_q))
        a2_o, b2_o = dpx(step_o[0], 4), dpx(step_o[1], 2)
        keep_a, send = call(
            functools.partial(attention_weights, n_mp, cols),
            here(after(inputs, step_i[0], step_i[1], step_o[0], step_o[1]))
            + here(grad_q, grad_k, grad_v, grad_wo),
            away(lot, lot),
            [vmem((4, n_mp * cols, width), low), dma((SLICES * n_mp,))],
            6,
        )
        got_a = dpx(send, 1)
        (input_grad,) = call(
            functools.partial(attention_inputs, n_mp, cols),
            here(grad_z1, after(grad_q, keep_a), grad_k, grad_v)
            + away(own_qkv, w_attn, *att_parts),
            here(rows_f),
            [vmem((4, n_mp * cols, width), low), dma((nc,))],
            6,
        )
        step_a = reduce_one(keep_a, after(got_a, input_grad))
        a_a, b_a = dpx(step_a[0], 2), dpx(step_a[1], 4)
        step_o = after(reduce_three(*step_o[2:], a2_o, b2_o), step_a[0])
        z_o = [mpx(step_o[i], i) for i in range(1, n_mp)]
        step_i = reduce_two(step_i[2], step_i[3], after(a_i, step_o[0]), b_i)
        a2_i, b2_i = dpx(step_i[0], 4), dpx(step_i[1], 2)
        step_a = reduce_two(step_a[2], step_a[3], after(a_a, step_i[0]), after(b_a, step_i[1]))
        a2_a, b2_a = dpx(step_a[0], 4), dpx(step_a[1], 2)
        step_i = after(reduce_three(*step_i[2:], a2_i, b2_i), step_a[0])
        z_i = [mpx(step_i[i], i) for i in range(1, n_mp)]
        step_a = after(reduce_three(*step_a[2:], a2_a, b2_a), step_i)
        z_a = [mpx(step_a[i], i) for i in range(1, n_mp)]
        red_out = reduce_last([step_o[0]] + z_o)
        red_in = reduce_last([step_i[0]] + z_i)
        red_att = reduce_last([step_a[0]] + z_a)
        grad_b_qv = grad_b_qv[:2].reshape(2, n_mp, cols).transpose(1, 0, 2)
        total = jnp.concatenate(
            [
                mp_natural(grad_b_qv).reshape(-1),
                mp_natural(grad_b_in).reshape(-1),
                small_one[:3].reshape(-1),
                small_two[:3].reshape(-1),
            ]
        )
        total = sum_all(after(total, step_a[0]))
        n_qv, n_in = n_mp * 2 * cols, n_mp * units
        take = lax.axis_index("mp")
        out_b_qv = lax.dynamic_slice_in_dim(total[:n_qv].reshape(n_mp, 2, cols), take, 1, 0)[0]
        out_b_in = lax.dynamic_slice_in_dim(
            total[n_qv : n_qv + n_in].reshape(n_mp, -1), take, 1, 0
        )[0]
        total = total[n_qv + n_in :].reshape(6, width)
        whole = shape((SLICES * size, width), f32)

        done_in, done_out = call(
            finish_rows,
            away(*plane_parts(jnp.concatenate([red_in, red_out]))),
            here(whole, whole),
            [vmem((2, SLICES * size, width), low), dma((2 * SLICES,))],
            4,
        )
        done_qkv, done_attn = call(
            functools.partial(finish_att, cols),
            away(*plane_parts(red_att)),
            here(shape((3, width, cols), f32), shape((cols, width), f32)),
            [vmem((4, cols, width), low), dma((SLICES,))],
            3,
        )
        return (
            layer_out,
            input_grad,
            done_qkv,
            out_b_qv,
            done_attn,
            total[0],
            total[1],
            total[2],
            done_in,
            out_b_in,
            done_out,
            total[3],
            total[4],
            total[5],
            grad_pool,
            grad_b_pool,
            new_scale,
        )

    return on_device


def solution(mesh):
    rows, whole = P(("dp", "mp"), None), P()
    in_specs = (
        rows,
        P(("dp", "mp")),
        rows,
        whole,
        P(None, None, "mp"),
        P(None, "mp"),
        P("mp", None),
        whole,
        whole,
        whole,
        P(None, "mp"),
        P("mp"),
        P("mp", None),
        whole,
        whole,
        whole,
        whole,
        whole,
        whole,
    )
    out_specs = (
        rows,
        rows,
        P(None, None, "mp"),
        P(None, "mp"),
        P("mp", None),
        whole,
        whole,
        whole,
        P(None, "mp"),
        P("mp"),
        P("mp", None),
        whole,
        whole,
        whole,
        whole,
        whole,
        whole,
    )
    return jax.shard_map(
        make(mesh), mesh=mesh, in_specs=in_specs, out_specs=out_specs, check_vma=False
    )
```

```python
import functools

import jax
import jax.numpy as jnp
from jax import lax
from jax.experimental import pallas as pl
from jax.experimental.pallas import tpu as pltpu
from jax.sharding import PartitionSpec as P

HEAD_DIM = 64
SEQ = 64
SLICES = 8
PARTS = 16
PAIR = 2 * SEQ
LANES = 2 * HEAD_DIM
BLOCK = 8

eps_norm = 1e-12
margin = 0.3
step_rate = 1.0
masked_low = -1e30
high = lax.Precision.HIGHEST
f32 = jnp.float32
low = jnp.bfloat16
VMEM_BYTES = 58 << 20


def nn(a, b):
    return jnp.dot(a, b, preferred_element_type=f32)


def nt(a, b):
    return lax.dot_general(a, b, (((1,), (1,)), ((), ())), preferred_element_type=f32)


def tn(a, b):
    return lax.dot_general(a, b, (((0,), (0,)), ((), ())), preferred_element_type=f32)


def rank_terms(cosine, same, diag_mask, weight, scale_value, axis_of):
    shifted = cosine - margin * diag_mask
    logits = jnp.where(same, scale_value * shifted, masked_low)
    top = jnp.max(logits, axis=axis_of, keepdims=True)
    lse = top + jnp.log(jnp.sum(jnp.exp(logits - top), axis=axis_of, keepdims=True))
    probs = jnp.exp(logits - lse)
    grad_logit = weight * (probs - diag_mask)
    return (grad_logit, grad_logit * shifted)


def call(body, ins, outs, scratch, micros):
    def spec(vmem):
        return pl.BlockSpec(memory_space=pltpu.VMEM if vmem else pltpu.HBM)

    return pl.pallas_call(
        body,
        out_shape=[jax.ShapeDtypeStruct(o.shape, o.dtype) for o, _ in outs],
        in_specs=[spec(v) for _, v in ins],
        out_specs=[spec(v) for _, v in outs],
        scratch_shapes=scratch,
        compiler_params=pltpu.CompilerParams(vmem_limit_bytes=VMEM_BYTES),
        cost_estimate=pl.CostEstimate(flops=int(micros * 1.1e9), bytes_accessed=0, transcendentals=0),
    )(*[a for a, _ in ins])


def slot(p):
    me = lax.rem(lax.axis_index("dp"), SLICES)
    return jnp.bitwise_xor(me, p)


def start_all(copies):
    for c in copies:
        c.start()
    return copies


def wait_all(copies):
    for c in copies:
        c.wait()


def att_spot(ref, s, p, cols, size, first=0, rows=None):
    at = slot(p)
    row = pl.multiple_of(s * cols + lax.rem(at, 2) * size + first, 16)
    return ref.at[at // 2, pl.ds(row, rows or size)]


def row_spot(ref, s, p, size, first=0, rows=None):
    return ref.at[s, pl.ds(pl.multiple_of(slot(p) * size + first, 16), rows or size)]


def slices_of(parts):
    full = parts[0].shape[-2]
    half = full // 2
    count = len(parts) // 2
    out = []
    for c in (0, 1):
        own, at_x, at_y, *rest = parts[count * c : count * (c + 1)]
        out += [(own, c, 0, full), (at_x, 2 + c, 0, full), (at_y, 4 + c, 0, full)]
        if len(rest) == 1:
            out += [(rest[0], 6 + c, 0, full)]
        else:
            out += [(rest[0], 6 + c, 0, half), (rest[1], 6 + c, half, half)]
    return out


def fetch_att(own_qkv, own_o, parts, dst, sem, cols):
    copies = []
    for i in range(3):
        copies.append(pltpu.make_async_copy(own_qkv.at[i], dst.at[i, pl.ds(0, cols)], sem.at[i]))
    copies.append(pltpu.make_async_copy(own_o, dst.at[3, pl.ds(0, cols)], sem.at[3]))
    k = 4
    size = parts[0].shape[1]
    first = 1
    for group in (parts[:SLICES], parts[SLICES:]):
        for part, p, at, n in slices_of(group):
            for s in range(part.shape[0]):
                spot = att_spot(dst, first + s, p, cols, size, at, n)
                copies.append(pltpu.make_async_copy(part.at[s], spot, sem.at[k]))
                k += 1
        first += group[0].shape[0]
    return start_all(copies)


def fetch_rows(own, parts, dst, sem, base):
    copies = [[pltpu.make_async_copy(own, dst.at[0], sem.at[base])]]
    k = base + 1
    size = parts[0].shape[1]
    for s in range(parts[0].shape[0]):
        copies.append([])
        for part, p, at, n in slices_of(parts):
            spot = row_spot(dst, s + 1, p, size, at, n)
            copies[-1].append(pltpu.make_async_copy(part.at[s], spot, sem.at[k]))
            k += 1
    for group in copies:
        start_all(group)
    return copies


def fetch_each(src, dst, sem):
    return start_all(
        [pltpu.make_async_copy(src.at[i], dst.at[i], sem.at[i]) for i in range(src.shape[0])]
    )


def n_copies(n_mp):
    return 4 + PARTS * (n_mp - 1)


def send_shard(src_of, s, g_keep, g_send, sem, n_mp):
    copies = []
    for p in range(SLICES):
        dst = g_send if p & 1 else g_keep
        spot = dst.at[s // 2, p >> 2, (p >> 1) & 1, s % 2]
        copies.append(pltpu.make_async_copy(src_of(s, p), spot, sem.at[SLICES * s + p]))
    return start_all(copies)


def mean_of(v):
    return jnp.sum(v, axis=-1, keepdims=True) * (1.0 / v.shape[-1])


def norm_rows(z):
    center = z - mean_of(z)
    inv = lax.rsqrt(mean_of(center * center) + eps_norm)
    return center * inv, inv


def norm_back(grad_out, hat, inv, gain):
    scaled = grad_out * gain
    return inv * (scaled - mean_of(scaled) - hat * mean_of(scaled * hat))


def pair_mask(ids_row):
    row = lax.broadcasted_iota(jnp.int32, (PAIR, PAIR), 0) >= SEQ
    col = lax.broadcasted_iota(jnp.int32, (PAIR, PAIR), 1) >= SEQ
    return jnp.logical_and(row == col, ids_row != 0)


def split_heads(v):
    first = lax.broadcasted_iota(jnp.int32, v.shape, 1) < HEAD_DIM
    zero = jnp.zeros_like(v)
    return jnp.concatenate([jnp.where(first, v, zero), jnp.where(first, zero, v)], axis=0)


def join_heads(v):
    half = v.shape[0] // 2
    first = lax.broadcasted_iota(jnp.int32, (half, v.shape[1]), 1) < HEAD_DIM
    return jnp.where(first, v[:half], v[half:])


def softmax_of(scores, mask):
    scores = jnp.where(mask, scores * 0.125, masked_low)
    expd = jnp.exp(scores - jnp.max(scores, axis=-1, keepdims=True))
    return expd / jnp.sum(expd, axis=-1, keepdims=True)


def attention_forward(n_mp, cols, *refs):
    x, ids, b_q, b_v, b_attn, gain, shift, own_qkv, own_o = refs[:9]
    parts = refs[9 : 9 + PARTS]
    q, k, v, ctx, hat_out, inv_out, h1, w_all, p_all = refs[25:34]
    w, p_keep, sem, sem2 = refs[34:]
    copies = fetch_att(own_qkv, own_o, parts, w, sem, cols)
    wait_all(copies)
    sent = start_all([pltpu.make_async_copy(w, w_all, sem2.at[0])])
    rows, width = x.shape
    q[...] = (nt(x[...], w[0]) + b_q[...]).astype(low)
    k[...] = nt(x[...], w[1]).astype(low)
    v[...] = (nt(x[...], w[2]) + b_v[...]).astype(low)

    @pl.loop(0, rows // PAIR)
    def _(t):
        at = pl.ds(pl.multiple_of(t * PAIR, PAIR), PAIR)
        mask = pair_mask(ids[t])
        for j in range(width // LANES):
            lanes = slice(j * LANES, (j + 1) * LANES)
            raw = nt(q[at, lanes], split_heads(k[at, lanes]))
            probs = [softmax_of(raw[:, i * PAIR : (i + 1) * PAIR], mask) for i in (0, 1)]
            probs = jnp.concatenate(probs, axis=1)
            p_keep[t, j] = probs
            out = nn(probs.astype(low), split_heads(v[at, lanes]))
            ctx[at, lanes] = out.astype(low)

    sent += start_all([pltpu.make_async_copy(p_keep, p_all, sem2.at[1])])
    z = x[...].astype(f32) + nn(ctx[...], w[3]) + b_attn[...]
    hat, inv = norm_rows(z)
    hat_out[...] = hat
    inv_out[...] = jnp.broadcast_to(inv, inv_out.shape)
    h1[...] = (hat * gain[...] + shift[...]).astype(low)
    wait_all(sent)


def gelu_pair(pre):
    size = jnp.abs(pre)
    t = 1.0 / (1.0 + 0.2316418882663604 * size)
    bell = jnp.exp(-0.5 * pre * pre)
    poly = t * (
        0.127414796
        + t * (-0.142248368 + t * (0.7107068705 + t * (-0.7265760135 + t * 0.5307027145)))
    )
    tail = poly * bell
    phi = jnp.where(pre >= 0.0, 1.0 - tail, tail)
    return pre * phi, phi + pre * (bell * 0.3989422804014327)


def ffn_in_forward(n_mp, *refs):
    h1, b_mid, own_in = refs[:3]
    parts = refs[3 : 3 + SLICES]
    hidden, slope, w_in, act_s, slope_s, sem, sem2 = refs[11:]
    copies = fetch_rows(own_in, parts, w_in, sem, 0)
    sent = []
    for s in range(n_mp):
        wait_all(copies[s])
        pre = nn(h1[...], w_in[s]) + b_mid[s]
        act, grad = gelu_pair(pre)
        act_s[s] = act.astype(low)
        slope_s[s] = grad.astype(low)
        sent.append(pltpu.make_async_copy(act_s.at[s], hidden.at[s], sem2.at[2 * s]))
        sent.append(pltpu.make_async_copy(slope_s.at[s], slope.at[s], sem2.at[2 * s + 1]))
        start_all(sent[-2:])
    wait_all(sent)


def ffn_out_forward(n_mp, *refs):
    hat1, gain1, shift1, b_out, gain2, shift2, hidden, own_out = refs[:8]
    parts = refs[8 : 8 + SLICES]
    layer_out, hat_out, inv_out, first = refs[16:20]
    w_out, act_s, acc, sem, sem2 = refs[20:]
    acts = fetch_each(hidden, act_s, sem2)
    copies = fetch_rows(own_out, parts, w_out, sem, 0)
    acc[...] = hat1[...] * gain1[...] + shift1[...] + b_out[...]
    for s in range(n_mp):
        wait_all([acts[s]] + copies[s])
        acc[...] += nn(act_s[s], w_out[s])

    hat, inv = norm_rows(acc[...])
    hat_out[...] = hat
    inv_out[...] = jnp.broadcast_to(inv, inv_out.shape)
    out = (hat * gain2[...] + shift2[...]).astype(low)
    layer_out[...] = out
    rows = [out[i * SEQ : i * SEQ + 1].astype(f32) for i in range(out.shape[0] // SEQ)]
    rows.append(jnp.zeros((BLOCK - len(rows), out.shape[1]), f32))
    first[...] = jnp.concatenate(rows, axis=0).astype(low)


def ranking(n_mp, sents, *refs):
    ids_row, ids_col, w_pool, b_pool, scale = refs[:5]
    parts = refs[5:9]
    g_first, rows_out, g_out, g_bias, scale_out = refs[9:14]
    got, g_all, sem = refs[14:]
    me = lax.axis_index("mp")
    copies = []
    for p in range(SLICES):
        for s in range(n_mp):
            spot = got.at[slot(p) * n_mp + jnp.bitwise_xor(me, s)]
            copies.append(
                pltpu.make_async_copy(parts[p >> 1].at[s, p & 1], spot, sem.at[p * n_mp + s])
            )
    wait_all(start_all(copies))
    n = ids_row.shape[1]
    first = got[...].astype(f32).reshape(n, -1).astype(low)
    rows_out[...] = first
    pooled = jnp.tanh(nn(first, w_pool[...]) + b_pool[...])
    inv_len = lax.rsqrt(jnp.sum(pooled * pooled, axis=-1, keepdims=True) + eps_norm)
    emb = pooled * inv_len
    emb_low = emb.astype(low)
    cosine = nt(emb_low, emb_low)
    row = lax.broadcasted_iota(jnp.int32, (n, n), 0)
    col = lax.broadcasted_iota(jnp.int32, (n, n), 1)
    even = lax.rem(row, 2) == 0
    in_row = jnp.logical_and(even, lax.rem(row, BLOCK) < sents)
    in_col = jnp.logical_and(lax.rem(col, 2) == 1, lax.rem(col, BLOCK) < sents)
    in_both = jnp.logical_and(in_row, in_col)
    same = jnp.logical_and(in_both, ids_col[...] == ids_row[...])
    one = same.astype(f32)
    diag = jnp.logical_and(in_both, col == row + 1).astype(f32)
    shifted = cosine - margin * diag
    logits = jnp.where(same, scale[...] * shifted, masked_low)
    grad = jnp.zeros_like(cosine)
    for axis in (1, 0):
        expd = jnp.exp(logits - jnp.max(logits, axis=axis, keepdims=True))
        expd = jnp.where(same, expd, 0.0)
        total = jnp.maximum(jnp.sum(expd, axis=axis, keepdims=True), 1e-30)
        count = jnp.maximum(jnp.sum(one, axis=axis, keepdims=True), 1.0)
        grad = grad + (expd / total - diag) / count
    scale_grad = jnp.sum(jnp.sum(grad * shifted, axis=1, keepdims=True), axis=0, keepdims=True)
    scale_out[...] = scale[...] - step_rate * jnp.broadcast_to(scale_grad, scale_out.shape)
    both = grad + grad.T
    g_emb = jnp.zeros_like(pooled)
    for _ in range(3):
        part = both.astype(low)
        both = both - part.astype(f32)
        g_emb = g_emb + nn(part, emb_low)
    g_emb = scale[0:1, 0:1] * g_emb
    g_pooled = inv_len * (g_emb - emb * jnp.sum(emb * g_emb, axis=-1, keepdims=True))
    g_pre = (g_pooled * (1.0 - pooled * pooled)).astype(low)
    g_out[...] = g_pre
    g_all[...] = g_pre.astype(f32)
    g_bias[...] = jnp.sum(g_all[...], axis=0, keepdims=True)
    at = (lax.axis_index("dp") * n_mp + me) * BLOCK
    own = g_all[pl.ds(pl.multiple_of(at, BLOCK), BLOCK)].astype(low)
    g_first[...] = nt(own, w_pool[...])


def out_backward(n_mp, *refs):
    cot, g_first, hat, inv, gain, hidden = refs[:6]
    g_z2, small, keep, send = refs[6:10]
    g_w, act_s, sem, sem2 = refs[10:]
    acts = fetch_each(hidden, act_s, sem2)
    rows = cot.shape[0]
    g_z2[...] = cot[...].astype(f32)
    for i in range(rows // SEQ):
        g_z2[i * SEQ : i * SEQ + 1] += g_first[i : i + 1]
    g_y = g_z2[...]
    small[...] = jnp.zeros_like(small)
    small[1:2] = jnp.sum(g_y * hat[...], axis=0, keepdims=True)
    small[2:3] = jnp.sum(g_y, axis=0, keepdims=True)
    g_z = norm_back(g_y, hat[...], inv[:, :1], gain[...])
    g_z2[...] = g_z
    small[0:1] = jnp.sum(g_z, axis=0, keepdims=True)
    g_ffn = g_z.astype(low)

    size = keep.shape[-2]
    sent = []
    for s in range(n_mp):
        acts[s].wait()
        g_w[s] = tn(act_s[s], g_ffn).astype(low)
        sent += send_shard(lambda s, p: row_spot(g_w, s, p, size), s, keep, send, sem, n_mp)
    wait_all(sent)


def in_backward(n_mp, *refs):
    g_z2, h1, hat, inv, gain, slope, own_in, own_out = refs[:8]
    in_parts = refs[8 : 8 + SLICES]
    out_parts = refs[16 : 16 + SLICES]
    g_z1, g_mid, small, keep, send = refs[24:29]
    w_in, w_out, slope_s, g_w, acc, sem, sem2, sem3 = refs[29:]
    slopes = fetch_each(slope, slope_s, sem3)
    out_copies = fetch_rows(own_out, out_parts, w_out, sem, 0)
    in_copies = fetch_rows(own_in, in_parts, w_in, sem, n_copies(n_mp))
    acc[...] = g_z2[...]
    g_ffn = g_z2[...].astype(low)
    size = keep.shape[-2]
    copies = []
    for s in range(n_mp):
        wait_all([slopes[s]] + out_copies[s])
        g_pre = (nt(g_ffn, w_out[s]) * slope_s[s].astype(f32)).astype(low)
        g_mid[s] = jnp.sum(g_pre.astype(f32), axis=0, keepdims=True)
        g_w[s] = tn(h1[...], g_pre).astype(low)
        copies += send_shard(lambda s, p: row_spot(g_w, s, p, size), s, keep, send, sem2, n_mp)
        wait_all(in_copies[s])
        acc[...] += nt(g_pre, w_in[s])
    g_h1 = acc[...]
    small[...] = jnp.zeros_like(small)
    small[1:2] = jnp.sum(g_h1 * hat[...], axis=0, keepdims=True)
    small[2:3] = jnp.sum(g_h1, axis=0, keepdims=True)
    g_z = norm_back(g_h1, hat[...], inv[:, :1], gain[...])
    g_z1[...] = g_z
    small[0:1] = jnp.sum(g_z, axis=0, keepdims=True)
    wait_all(copies)


def attention_backward(n_mp, cols, *refs):
    g_z1, q, k, v, ctx, g_mid, small_one, small_two, w_all, p_all = refs[:10]
    g_q, g_k, g_v, total, g_wo = refs[10:15]
    w, p_keep, g_ctx, sem, sem2 = refs[15:]
    fetch = start_all([pltpu.make_async_copy(w_all.at[3], w, sem.at[0])])
    probs = fetch_each(p_all, p_keep, sem2)
    rows, width = g_z1.shape
    g_attn = g_z1[...].astype(low)
    wait_all(fetch)
    g_ctx[...] = nt(g_attn, w[...]).astype(low)
    for t in range(rows // PAIR):
        at = slice(t * PAIR, (t + 1) * PAIR)
        probs[t].wait()
        for j in range(width // LANES):
            lanes = slice(j * LANES, (j + 1) * LANES)
            q2, g2 = q[at, lanes], g_ctx[at, lanes]
            k2, v2 = split_heads(k[at, lanes]), split_heads(v[at, lanes])
            p = p_keep[t, j]
            g_p = nt(g2, v2)
            g_raw = []
            for i in (0, 1):
                half = slice(i * PAIR, (i + 1) * PAIR)
                inner = jnp.sum(p[:, half] * g_p[:, half], axis=-1, keepdims=True)
                g_raw.append((p[:, half] * (g_p[:, half] - inner) * 0.125).astype(low))
            g_raw = jnp.concatenate(g_raw, axis=1)
            g_v[at, lanes] = join_heads(tn(p.astype(low), g2)).astype(low)
            g_q[at, lanes] = nn(g_raw, k2).astype(low)
            g_k[at, lanes] = join_heads(tn(g_raw, q2)).astype(low)

    g_wo[...] = tn(ctx[...], g_attn).astype(low)
    total[...] = jnp.zeros_like(total)
    total[0:3] = small_one[0:3]
    total[3:6] = small_two[0:3]
    b_q = jnp.sum(g_q[...].astype(f32), axis=0, keepdims=True)
    b_v = jnp.sum(g_v[...].astype(f32), axis=0, keepdims=True)
    for s in range(n_mp):
        at = jnp.bitwise_xor(lax.axis_index("mp"), s)
        total[pl.ds(BLOCK + at, 1)] = g_mid[s]
        lanes = slice(s * cols, (s + 1) * cols)
        total[pl.ds(BLOCK + n_mp + at, 1), 0:cols] = b_q[:, lanes]
        total[pl.ds(BLOCK + n_mp + at, 1), cols : 2 * cols] = b_v[:, lanes]


def attention_weights(n_mp, cols, *refs):
    x, g_q, g_k, g_v, g_wo, keep, send, g_w, sem = refs
    g_w[3] = g_wo[...]
    g_w[0] = tn(g_q[...], x[...]).astype(low)
    g_w[1] = tn(g_k[...], x[...]).astype(low)
    g_w[2] = tn(g_v[...], x[...]).astype(low)
    size = keep.shape[-2]
    sent = []
    for s in range(n_mp):
        sent += send_shard(lambda s, p: att_spot(g_w, s, p, cols, size), s, keep, send, sem, n_mp)
    wait_all(sent)


def attention_inputs(n_mp, cols, *refs):
    g_z1, g_q, g_k, g_v, w_all, g_x, w, sem = refs
    fetch = start_all([pltpu.make_async_copy(w_all.at[i], w.at[i], sem.at[i]) for i in range(3)])
    total = g_z1[...]
    for i, g in enumerate((g_q, g_k, g_v)):
        fetch[i].wait()
        total = total + nn(g[...], w[i])
    g_x[...] = total


def finish_rows(cols, *refs):
    parts = refs[:SLICES]
    if cols:
        out, out_qkv, out_o, got, sem, got_att, sem_att = refs[SLICES:]
    else:
        out, got, sem = refs[SLICES:]
    size = parts[0].shape[0] // (2 if cols else 1)
    copies, more = [], []
    for p in range(SLICES):
        part = parts[p].at[pl.ds(0, size)]
        copies.append(pltpu.make_async_copy(part, row_spot(got, 0, p, size), sem.at[p]))
        if cols:
            part = parts[p].at[pl.ds(size, size)]
            spot = att_spot(got_att, 0, p, cols, size)
            more.append(pltpu.make_async_copy(part, spot, sem_att.at[p]))
    start_all(copies + more)
    wait_all(copies)
    out[...] = got[0].astype(f32)
    if cols:
        wait_all(more)
        for i in range(3):
            out_qkv[i] = got_att[i].astype(f32)
        out_o[...] = got_att[3].astype(f32)


def make(mesh):
    n_dp = mesh.shape["dp"]
    n_mp = mesh.shape["mp"]

    def dpx(x, bit):
        return lax.ppermute(x, "dp", [(i, i ^ bit) for i in range(n_dp)])

    def mpx(x, bit):
        return lax.ppermute(x, "mp", [(i, i ^ bit) for i in range(n_mp)])

    def bit_of(axis, bit):
        return (lax.axis_index(axis) & bit) != 0

    def flips(v, axis, bits, dims):
        for bit, dim in zip(bits, dims):
            v = jnp.where(bit_of(axis, bit), jnp.flip(v, dim), v)
        return v

    def plane_parts(r):
        got = [None] * SLICES
        for p in (0, 2, 4, 6):
            got[p] = dpx(r, p) if p else r
        for p in (0, 2, 4, 6):
            got[p + 1] = dpx(got[p], 1)
        return got

    def over_z(piece):
        return [mpx(piece, i) for i in range(1, n_mp)]

    def over_z_slow(own):
        got = [mpx(own, 1)]
        bit = 2
        while bit < n_mp:
            far = mpx(jnp.stack([own] + got), bit)
            got += [far[i] for i in range(bit)]
            bit *= 2
        return got

    def over_plane(r):
        return [dpx(r, 2), dpx(r, 4), dpx(r, 6)]

    def over_core(parts):
        return parts + [dpx(part, 1) for part in parts]

    def after(x, *deps):
        return lax.optimization_barrier((x, deps))[0]

    def own_piece(shard):
        rows = shard.shape[0] // SLICES
        return lax.dynamic_slice_in_dim(shard, (lax.axis_index("dp") % SLICES) * rows, rows, 0)

    def add(a, b):
        return (a.astype(f32) + b.astype(f32)).astype(low)

    def reduce_one(keep, got):
        return (
            add(keep[0, :, 1], got[0, :, 1]),
            add(keep[1, 1], got[1, 1]),
            add(keep[0, :, 0], got[0, :, 0]),
            add(keep[1, 0], got[1, 0]),
        )

    def reduce_two(a0, b0, a1, b1):
        return add(a0[1], a1[1]), add(b0[1], b1[1]), a0[0], a1[0], b0[0], b1[0]

    def reduce_three(a0, a1, b0, b1, a2, b2):
        a = a0.astype(f32) + a1.astype(f32) + a2.astype(f32)
        b = b0.astype(f32) + b1.astype(f32) + b2.astype(f32)
        u = [a[0], a[1], b[0], b[1]]
        bit = SLICES
        while bit < n_dp:
            u = [w.astype(low) for w in u]
            u = [w.astype(f32) + dpx(w, bit).astype(f32) for w in u]
            bit *= 2
        return [w.astype(low) for w in u]

    def reduce_last(u):
        total = u[0].astype(f32)
        for w in u[1:]:
            total = total + w.astype(f32)
        return total.astype(low)

    def mp_natural(v):
        bits = [1 << i for i in reversed(range(n_mp.bit_length() - 1))]
        shape = v.shape
        v = v.reshape((2,) * len(bits) + shape[1:])
        return flips(v, "mp", bits, range(len(bits))).reshape(shape)

    def gather_all(own):
        r = jnp.stack([own] + [mpx(own, s) for s in range(1, n_mp)])
        r = mp_natural(r)
        z = jnp.stack([r] + [dpx(r, b) for b in (2, 4, 6)])
        v = jnp.stack([z, dpx(z, 1)], 1).reshape((2, 2, 2) + r.shape)
        v = flips(v, "dp", (4, 2, 1), (0, 1, 2)).reshape((SLICES,) + r.shape)
        bit = SLICES
        while bit < n_dp:
            o = dpx(v, bit)
            up = bit_of("dp", bit)
            v = jnp.concatenate([jnp.where(up, o, v), jnp.where(up, v, o)], 0)
            bit *= 2
        return v.reshape((n_dp * n_mp,) + own.shape)

    def rank_part(first_rows, sents, pair_ids, w_pool, b_pool, scale):
        n_all = n_dp * n_mp
        width = first_rows.shape[-1]
        first_rows = first_rows[:, :sents].reshape(n_all * sents, width).astype(low)
        npairs = n_all * sents // 2
        pooled = jnp.tanh(
            jnp.dot(first_rows, w_pool, preferred_element_type=f32) + b_pool.astype(f32)
        )
        inv_len = lax.rsqrt(jnp.sum(pooled * pooled, axis=-1, keepdims=True) + eps_norm)
        emb_full = pooled * inv_len
        emb_pairs = emb_full.astype(low).reshape(npairs, 2, width)
        all_src, all_tgt = emb_pairs[:, 0, :], emb_pairs[:, 1, :]
        scale_value = scale[0]
        cosine = jnp.einsum("kd,md->km", all_src, all_tgt, preferred_element_type=f32)
        same = pair_ids[:, None] == pair_ids[None, :]
        counts = jnp.sum(same.astype(f32), axis=1)
        index_all = jnp.arange(npairs)
        diag_mask = (index_all[:, None] == index_all[None, :]).astype(f32)
        grad_row, part_row = rank_terms(
            cosine, same, diag_mask, (1.0 / counts)[:, None], scale_value, 1
        )
        grad_col, part_col = rank_terms(
            cosine, same, diag_mask, (1.0 / counts)[None, :], scale_value, 0
        )
        grad_all = grad_row + grad_col
        grad_src = scale_value * jnp.dot(grad_all, all_tgt.astype(f32), precision=high)
        grad_tgt = scale_value * jnp.einsum(
            "km,kd->md", grad_all, all_src.astype(f32), precision=high
        )
        new_scale = scale - step_rate * (jnp.sum(part_row) + jnp.sum(part_col))
        grad_emb = jnp.stack([grad_src, grad_tgt], axis=1).reshape(2 * npairs, width)
        grad_pooled = inv_len * (
            grad_emb - emb_full * jnp.sum(emb_full * grad_emb, axis=-1, keepdims=True)
        )
        grad_ppre = (grad_pooled * (1.0 - pooled * pooled)).astype(low)
        grad_pool = jnp.einsum("sd,se->de", first_rows, grad_ppre, preferred_element_type=f32)
        grad_b_pool = jnp.sum(grad_ppre.astype(f32), axis=0)
        own_ppre = lax.dynamic_slice_in_dim(
            grad_ppre, lax.axis_index(("dp", "mp")) * sents, sents, 0
        )
        grad_first = jnp.einsum("se,de->sd", own_ppre, w_pool, preferred_element_type=f32)
        grad_first = jnp.pad(grad_first, ((0, BLOCK - sents), (0, 0)))
        return grad_first, grad_pool, grad_b_pool, new_scale

    def on_device(
        inputs,
        token_ids,
        out_cot,
        pair_ids,
        w_qkv,
        b_qv,
        w_attn,
        b_attn,
        norm1_gain,
        norm1_bias,
        w_in,
        b_in,
        w_out,
        b_out,
        norm2_gain,
        norm2_bias,
        w_pool,
        b_pool,
        scale,
    ):
        rows, width = inputs.shape
        cols = w_qkv.shape[2]
        units = w_in.shape[1]
        sents = rows // SEQ
        shape = jax.ShapeDtypeStruct
        dma = pltpu.SemaphoreType.DMA
        vmem = pltpu.VMEM

        def row(v):
            return v.astype(f32)[None, :]

        qkv_t = w_qkv.transpose(0, 2, 1)
        att_shard = jnp.concatenate([qkv_t.reshape(3 * cols, width), w_attn])
        size = att_shard.shape[0] // SLICES
        small = jnp.pad(jnp.concatenate([b_qv.reshape(-1), b_in]), (0, 2 * width - 2 * cols - units))
        small = small.reshape(2, width)
        att_r = over_z(jnp.concatenate([own_piece(att_shard), small]))
        small = jnp.stack([small] + [r[size:] for r in att_r]).reshape(n_mp, -1).astype(f32)
        b_q, b_v = small[:, :cols].reshape(1, -1), small[:, cols : 2 * cols].reshape(1, -1)
        b_mid = small[:, None, 2 * cols : 2 * cols + units]
        att_one = att_r[0][None, :size]
        att_near = over_plane(att_one)
        att_r = jnp.stack([r[:size] for r in after(att_r[1:], att_near[0])])
        att_far = over_plane(att_r)
        in_z = over_z(after(own_piece(w_in), att_r, *att_near))
        att_parts = over_core([att_one] + att_near) + over_core([att_r] + att_far)
        in_r = jnp.stack(in_z)
        in_near = over_plane(after(in_r, *att_far))
        out_z = over_z_slow(after(own_piece(w_out), in_r))
        nc = n_copies(n_mp)
        own_qkv = att_shard[: 3 * cols].reshape(3, cols, width)

        def here(*arrays):
            return [(a, True) for a in arrays]

        def away(*arrays):
            return [(a, False) for a in arrays]

        gain_one, shift_one = row(norm1_gain), row(norm1_bias)
        gain_two, shift_two = row(norm2_gain), row(norm2_bias)
        ids = token_ids.reshape(rows // PAIR, 1, PAIR)

        rows_low, rows_f = shape((rows, width), low), shape((rows, width), f32)
        thin = shape((rows, 128), f32)
        w_shape = shape((4, n_mp * cols, width), low)
        p_shape = shape((rows // PAIR, width // LANES, PAIR, 2 * PAIR), f32)
        query, key_part, value_part, context, hat_one, inv_one, h1, w_all, p_all = call(
            functools.partial(attention_forward, n_mp, cols),
            here(after(inputs, out_z[0]), ids, b_q, b_v, row(b_attn), gain_one, shift_one)
            + away(own_qkv, w_attn, *att_parts),
            here(rows_low, rows_low, rows_low, rows_low, rows_f, thin, rows_low)
            + away(w_shape, p_shape),
            [vmem(w_shape.shape, low), vmem(p_shape.shape, f32), dma((nc,)), dma((2,))],
            11,
        )
        out_r = jnp.stack(after(out_z, h1))
        out_near = over_plane(out_r)
        in_parts = over_core(after([in_r] + in_near, h1))
        mid = shape((n_mp, rows, units), low)
        tiny_shape = shape((BLOCK, width), f32)
        ids_row = jnp.repeat(pair_ids.reshape(-1, sents // 2), 2, axis=1)
        ids_row = jnp.pad(ids_row, ((0, 0), (0, BLOCK - sents))).reshape(1, -1)
        hidden, slope = call(
            functools.partial(ffn_in_forward, n_mp),
            here(h1, b_mid) + away(w_in, *in_parts),
            away(mid, mid),
            [vmem((n_mp, width, units), low), vmem(mid.shape, low), vmem(mid.shape, low)]
            + [dma((nc,)), dma((2 * n_mp,))],
            9,
        )
        out_parts = over_core(after([out_r] + out_near, hidden))
        layer_out, hat_two, inv_two, own_first = call(
            functools.partial(ffn_out_forward, n_mp),
            here(hat_one, gain_one, shift_one, row(b_out), gain_two, shift_two)
            + away(hidden, w_out, *out_parts),
            here(rows_low, rows_f, thin, shape((BLOCK, width), low)),
            [vmem((n_mp, units, width), low), vmem(mid.shape, low), vmem((rows, width), f32)]
            + [dma((nc,)), dma((n_mp,))],
            6,
        )
        if n_dp == SLICES:
            n = n_dp * n_mp * BLOCK
            r = jnp.stack([own_first, dpx(own_first, 1)])
            r = jnp.stack([r] + over_z(r))
            grad_first, all_first, all_ppre, grad_b_pool, new_scale = call(
                functools.partial(ranking, n_mp, sents),
                here(ids_row, ids_row.reshape(n, 1), w_pool, row(b_pool))
                + here(jnp.broadcast_to(scale[None], (1, n)))
                + away(r, *over_plane(r)),
                here(tiny_shape, shape((n, width), low), shape((n, width), low))
                + here(shape((1, width), f32), shape((1, n), f32)),
                [vmem((n_dp * n_mp, BLOCK, width), low), vmem((n, width), f32)]
                + [dma((n_dp * n_mp,))],
                6,
            )
            grad_b_pool, new_scale = grad_b_pool[0], new_scale[0, :1]
        else:
            grad_first, grad_pool, grad_b_pool, new_scale = rank_part(
                gather_all(own_first), sents, pair_ids, w_pool, b_pool, scale
            )
        lot = shape((2, 2, 2, n_mp // 2, size, width), low)
        tiny = shape((BLOCK, width), f32)
        grad_z2, small_two, keep_o, send = call(
            functools.partial(out_backward, n_mp),
            here(out_cot, grad_first, hat_two, inv_two, gain_two) + away(hidden),
            here(rows_f, tiny) + away(lot, lot),
            [vmem((n_mp, units, width), low), vmem(mid.shape, low)]
            + [dma((SLICES * n_mp,)), dma((n_mp,))],
            10,
        )
        got_o = dpx(send, 1)
        grad_z1, grad_b_in, small_one, keep_i, send = call(
            functools.partial(in_backward, n_mp),
            here(grad_z2, h1, hat_one, inv_one, gain_one)
            + away(slope, w_in, w_out, *in_parts, *out_parts),
            here(rows_f, shape((n_mp, 1, units), f32), tiny) + away(lot, lot),
            [
                vmem((n_mp, width, units), low),
                vmem((n_mp, units, width), low),
                vmem(mid.shape, low),
                vmem((n_mp, width, units), low),
                vmem((rows, width), f32),
                dma((2 * nc,)),
                dma((SLICES * n_mp,)),
                dma((n_mp,)),
            ],
            17,
        )
        got_i = dpx(send, 1)
        step_o = reduce_one(keep_o, after(got_o, grad_z1))
        a_o, b_o = dpx(step_o[0], 2), dpx(step_o[1], 4)
        grad_q, grad_k, grad_v, total, grad_wo = call(
            functools.partial(attention_backward, n_mp, cols),
            here(after(grad_z1, step_o[0], step_o[1]), query, key_part, value_part, context)
            + here(grad_b_in, small_one, small_two)
            + away(w_all, p_all),
            here(rows_low, rows_low, rows_low, shape((BLOCK + 2 * n_mp, width), f32))
            + here(shape((n_mp * cols, width), low)),
            [vmem((n_mp * cols, width), low), vmem(p_shape.shape, f32), vmem((rows, width), low)]
            + [dma((1,)), dma((rows // PAIR,))],
            15,
        )
        hops = [functools.partial(mpx, bit=1 << i) for i in range(n_mp.bit_length() - 1)]
        hops += [functools.partial(dpx, bit=1)]
        hops += [functools.partial(dpx, bit=1 << i) for i in range(3, n_dp.bit_length() - 1)]
        hop = hops[0](total)
        step_i = reduce_one(keep_i, after(got_i, grad_q))
        a_i, b_i = dpx(step_i[0], 2), dpx(step_i[1], 4)
        step_o = reduce_two(step_o[2], step_o[3], after(a_o, grad_q), after(b_o, grad_q))
        a2_o, b2_o = dpx(step_o[0], 4), dpx(step_o[1], 2)
        keep_a, send = call(
            functools.partial(attention_weights, n_mp, cols),
            here(after(inputs, step_i[0], step_i[1], step_o[0], step_o[1]))
            + here(grad_q, grad_k, grad_v, grad_wo),
            away(lot, lot),
            [vmem((4, n_mp * cols, width), low), dma((SLICES * n_mp,))],
            7,
        )
        got_a = dpx(send, 1)
        total = total + after(hop, keep_a)
        hop = hops[1](total)
        (input_grad,) = call(
            functools.partial(attention_inputs, n_mp, cols),
            here(grad_z1, after(grad_q, keep_a), grad_k, grad_v) + away(w_all),
            here(rows_f),
            [vmem((3, n_mp * cols, width), low), dma((3,))],
            7,
        )
        step_a = reduce_one(keep_a, after(got_a, input_grad))
        a_a, b_a = dpx(step_a[0], 2), dpx(step_a[1], 4)
        step_o = reduce_three(*step_o[2:], *after([a2_o, b2_o], step_a[0], step_a[1]))
        z_o = [mpx(step_o[i], i) for i in range(1, n_mp)]
        total = total + after(hop, step_a[0])
        hop = hops[2](total)
        step_i = reduce_two(step_i[2], step_i[3], *after([a_i, b_i], step_a[0], step_a[1]))
        a2_i, b2_i = dpx(step_i[0], 4), dpx(step_i[1], 2)
        step_a = reduce_two(step_a[2], step_a[3], *after([a_a, b_a], step_i[0], step_i[1]))
        a2_a, b2_a = dpx(step_a[0], 4), dpx(step_a[1], 2)
        red_out = reduce_last(after([step_o[0]] + z_o, step_a[0]))
        total = total + after(hop, step_a[0])
        for h in hops[3:]:
            total = total + h(total)
        step_i = reduce_three(*step_i[2:], *after([a2_i, b2_i], step_a[0], step_a[1]))
        z_i = [mpx(step_i[i], i) for i in range(1, n_mp)]
        step_a = reduce_three(*step_a[2:], *after([a2_a, b2_a], step_i[0]))
        z_a = [mpx(step_a[i], i) for i in range(1, n_mp)]
        red_in = reduce_last(after([step_i[0]] + z_i, step_a[0]))
        out_own = plane_parts(red_out)
        total = total + dpx(after(total, step_a[0]), 2)
        total = total + dpx(total, 4)
        red_att = reduce_last(after([step_a[0]] + z_a, total))
        last_own = plane_parts(jnp.concatenate([red_in, red_att]))
        if n_dp == SLICES:
            grad_pool = tn(after(all_first, step_a[0]), all_ppre)
        take = lax.axis_index("mp")
        out_b_in = lax.dynamic_slice_in_dim(total, BLOCK + take, 1, 0)[0]
        out_b_qv = lax.dynamic_slice_in_dim(total, BLOCK + n_mp + take, 1, 0)
        out_b_qv = out_b_qv[0, : 2 * cols].reshape(2, cols)
        whole = shape((SLICES * size, width), f32)

        (done_out,) = call(
            functools.partial(finish_rows, 0),
            away(*out_own),
            here(whole),
            [vmem((1, SLICES * size, width), low), dma((SLICES,))],
            3,
        )
        done_in, done_qkv, done_attn = call(
            functools.partial(finish_rows, cols),
            away(*last_own),
            here(whole, shape((3, cols, width), f32), shape((cols, width), f32)),
            [vmem((1, SLICES * size, width), low), dma((SLICES,))]
            + [vmem((4, cols, width), low), dma((SLICES,))],
            4,
        )
        return (
            layer_out,
            input_grad,
            done_qkv.transpose(0, 2, 1),
            out_b_qv,
            done_attn,
            total[0],
            total[1],
            total[2],
            done_in,
            out_b_in,
            done_out,
            total[3],
            total[4],
            total[5],
            grad_pool,
            grad_b_pool,
            new_scale,
        )

    return on_device


def solution(mesh):
    rows, whole = P(("dp", "mp"), None), P()
    in_specs = (
        rows,
        P(("dp", "mp")),
        rows,
        whole,
        P(None, None, "mp"),
        P(None, "mp"),
        P("mp", None),
        whole,
        whole,
        whole,
        P(None, "mp"),
        P("mp"),
        P("mp", None),
        whole,
        whole,
        whole,
        whole,
        whole,
        whole,
    )
    out_specs = (
        rows,
        rows,
        P(None, None, "mp"),
        P(None, "mp"),
        P("mp", None),
        whole,
        whole,
        whole,
        P(None, "mp"),
        P("mp"),
        P("mp", None),
        whole,
        whole,
        whole,
        whole,
        whole,
        whole,
    )
    return jax.shard_map(
        make(mesh), mesh=mesh, in_specs=in_specs, out_specs=out_specs, check_vma=False
    )
```

```python
import functools

import jax
import jax.numpy as jnp
from jax import lax
from jax.experimental import pallas as pl
from jax.experimental.pallas import tpu as pltpu
from jax.sharding import PartitionSpec as P

HEAD_DIM = 64
SEQ = 64
SLICES = 8
PARTS = 8
PAIR = 2 * SEQ
LANES = 2 * HEAD_DIM
BLOCK = 8

eps_norm = 1e-12
margin = 0.3
step_rate = 1.0
masked_low = -1e30
high = lax.Precision.HIGHEST
f32 = jnp.float32
low = jnp.bfloat16
VMEM_BYTES = 58 << 20


def nn(a, b):
    return jnp.dot(a, b, preferred_element_type=f32)


def nt(a, b):
    return lax.dot_general(a, b, (((1,), (1,)), ((), ())), preferred_element_type=f32)


def tn(a, b):
    return lax.dot_general(a, b, (((0,), (0,)), ((), ())), preferred_element_type=f32)


def rank_terms(cosine, same, diag_mask, weight, scale_value, axis_of):
    shifted = cosine - margin * diag_mask
    logits = jnp.where(same, scale_value * shifted, masked_low)
    top = jnp.max(logits, axis=axis_of, keepdims=True)
    lse = top + jnp.log(jnp.sum(jnp.exp(logits - top), axis=axis_of, keepdims=True))
    probs = jnp.exp(logits - lse)
    grad_logit = weight * (probs - diag_mask)
    return (grad_logit, grad_logit * shifted)


def call(body, ins, outs, scratch, micros):
    def spec(vmem):
        return pl.BlockSpec(memory_space=pltpu.VMEM if vmem else pltpu.HBM)

    return pl.pallas_call(
        body,
        out_shape=[jax.ShapeDtypeStruct(o.shape, o.dtype) for o, _ in outs],
        in_specs=[spec(v) for _, v in ins],
        out_specs=[spec(v) for _, v in outs],
        scratch_shapes=scratch,
        compiler_params=pltpu.CompilerParams(vmem_limit_bytes=VMEM_BYTES),
        cost_estimate=pl.CostEstimate(flops=int(micros * 1.1e9), bytes_accessed=0, transcendentals=0),
    )(*[a for a, _ in ins])


def slot(p):
    me = lax.rem(lax.axis_index("dp"), SLICES)
    return jnp.bitwise_xor(me, p)


def start_all(copies):
    for c in copies:
        c.start()
    return copies


def wait_all(copies):
    for c in copies:
        c.wait()


def att_spot(ref, s, p, cols, size, first=0, rows=None):
    at = slot(p)
    row = pl.multiple_of(s * cols + lax.rem(at, 2) * size + first, 16)
    return ref.at[at // 2, pl.ds(row, rows or size)]


def row_spot(ref, s, p, size, first=0, rows=None):
    return ref.at[s, pl.ds(pl.multiple_of(slot(p) * size + first, 16), rows or size)]


def slices_of(parts):
    full = parts[0].shape[-2]
    return [(part, 2 * (i % 4) + i // 4, 0, full) for i, part in enumerate(parts)]


def fetch_att(own_qkv, own_o, parts, dst, sem, cols):
    copies = []
    for i in range(3):
        copies.append(pltpu.make_async_copy(own_qkv.at[i], dst.at[i, pl.ds(0, cols)], sem.at[i]))
    copies.append(pltpu.make_async_copy(own_o, dst.at[3, pl.ds(0, cols)], sem.at[3]))
    k = 4
    size = parts[0].shape[1]
    for part, p, at, n in slices_of(parts):
        for s in range(part.shape[0]):
            spot = att_spot(dst, s + 1, p, cols, size, at, n)
            copies.append(pltpu.make_async_copy(part.at[s], spot, sem.at[k]))
            k += 1
    return start_all(copies)


def fetch_rows(own, parts, dst, sem, base):
    copies = [[pltpu.make_async_copy(own, dst.at[0], sem.at[base])]]
    k = base + 1
    size = parts[0].shape[1]
    for s in range(parts[0].shape[0]):
        copies.append([])
        for part, p, at, n in slices_of(parts):
            spot = row_spot(dst, s + 1, p, size, at, n)
            copies[-1].append(pltpu.make_async_copy(part.at[s], spot, sem.at[k]))
            k += 1
    return copies


def each_of(src, dst, sem):
    return [pltpu.make_async_copy(src.at[i], dst.at[i], sem.at[i]) for i in range(src.shape[0])]


def fetch_each(src, dst, sem):
    return start_all(each_of(src, dst, sem))


AHEAD = 2


def n_copies(n_mp):
    return 4 + PARTS * (n_mp - 1)


def send_shard(src_of, s, g_keep, g_send, sem, n_mp):
    copies = []
    for p in range(SLICES):
        dst = g_send if p & 1 else g_keep
        spot = dst.at[s // 2, p >> 2, (p >> 1) & 1, s % 2]
        copies.append(pltpu.make_async_copy(src_of(s, p), spot, sem.at[SLICES * s + p]))
    return start_all(copies)


def mean_of(v):
    return jnp.sum(v, axis=-1, keepdims=True) * (1.0 / v.shape[-1])


def norm_rows(z):
    center = z - mean_of(z)
    inv = lax.rsqrt(mean_of(center * center) + eps_norm)
    return center * inv, inv


def norm_back(grad_out, hat, inv, gain):
    scaled = grad_out * gain
    return inv * (scaled - mean_of(scaled) - hat * mean_of(scaled * hat))


def pair_mask(ids_row):
    row = lax.broadcasted_iota(jnp.int32, (PAIR, PAIR), 0) >= SEQ
    col = lax.broadcasted_iota(jnp.int32, (PAIR, PAIR), 1) >= SEQ
    return jnp.logical_and(row == col, ids_row != 0)


def split_heads(v):
    first = lax.broadcasted_iota(jnp.int32, v.shape, 1) < HEAD_DIM
    zero = jnp.zeros_like(v)
    return jnp.concatenate([jnp.where(first, v, zero), jnp.where(first, zero, v)], axis=0)


def join_heads(v):
    half = v.shape[0] // 2
    first = lax.broadcasted_iota(jnp.int32, (half, v.shape[1]), 1) < HEAD_DIM
    return jnp.where(first, v[:half], v[half:])


def softmax_of(scores, mask):
    scores = jnp.where(mask, scores * 0.125, masked_low)
    expd = jnp.exp(scores - jnp.max(scores, axis=-1, keepdims=True))
    return expd / jnp.sum(expd, axis=-1, keepdims=True)


def attention_forward(n_mp, cols, *refs):
    x, ids, small, vecs, own_qkv, own_o = refs[:6]
    parts = refs[6 : 6 + PARTS]
    q, k, v, ctx, hat_out, inv_out, h1, w_all, p_all = refs[14:23]
    w, p_keep, sem, sem2 = refs[23:]
    b_attn, gain, shift = vecs[0:1], vecs[1:2], vecs[2:3]
    copies = fetch_att(own_qkv, own_o, parts, w, sem, cols)
    wait_all(copies)
    sent = start_all([pltpu.make_async_copy(w, w_all, sem2.at[0])])
    rows, width = x.shape
    b_q = jnp.concatenate([small[s : s + 1, :cols] for s in range(n_mp)], axis=1)
    b_v = jnp.concatenate([small[s : s + 1, cols : 2 * cols] for s in range(n_mp)], axis=1)
    q[...] = (nt(x[...], w[0]) + b_q).astype(low)
    k[...] = nt(x[...], w[1]).astype(low)
    v[...] = (nt(x[...], w[2]) + b_v).astype(low)

    for t in range(rows // PAIR):
        at = slice(t * PAIR, (t + 1) * PAIR)
        mask = pair_mask(ids[t])
        for j in range(width // LANES):
            lanes = slice(j * LANES, (j + 1) * LANES)
            raw = nt(q[at, lanes], split_heads(k[at, lanes]))
            probs = [softmax_of(raw[:, i * PAIR : (i + 1) * PAIR], mask) for i in (0, 1)]
            probs = jnp.concatenate(probs, axis=1)
            p_keep[t, j] = probs
            out = nn(probs.astype(low), split_heads(v[at, lanes]))
            ctx[at, lanes] = out.astype(low)

    sent += start_all([pltpu.make_async_copy(p_keep, p_all, sem2.at[1])])
    z = x[...].astype(f32) + nn(ctx[...], w[3]) + b_attn
    hat, inv = norm_rows(z)
    hat_out[...] = hat
    inv_out[...] = jnp.broadcast_to(inv, inv_out.shape)
    h1[...] = (hat * gain + shift).astype(low)
    wait_all(sent)


def gelu_pair(pre):
    size = jnp.abs(pre)
    t = 1.0 / (1.0 + 0.2316418882663604 * size)
    bell = jnp.exp(-0.5 * pre * pre)
    poly = t * (
        0.127414796
        + t * (-0.142248368 + t * (0.7107068705 + t * (-0.7265760135 + t * 0.5307027145)))
    )
    tail = poly * bell
    phi = jnp.where(pre >= 0.0, 1.0 - tail, tail)
    return pre * phi, phi + pre * (bell * 0.3989422804014327)


def ffn_in_forward(n_mp, spot, *refs):
    h1, small, own_in = refs[:3]
    parts = refs[3 : 3 + SLICES]
    hidden, slope, w_in, act_s, slope_s, sem, sem2 = refs[11:]
    copies = fetch_rows(own_in, parts, w_in, sem, 0)
    sent = []
    for s in range(AHEAD):
        start_all(copies[s])
    for s in range(n_mp):
        wait_all(copies[s])
        if s + AHEAD < n_mp:
            start_all(copies[s + AHEAD])
        pre = nn(h1[...], w_in[s]) + small[s : s + 1, spot : spot + w_in.shape[2]]
        act, grad = gelu_pair(pre)
        act_s[s] = act.astype(low)
        slope_s[s] = grad.astype(low)
        sent.append(pltpu.make_async_copy(act_s.at[s], hidden.at[s], sem2.at[2 * s]))
        sent.append(pltpu.make_async_copy(slope_s.at[s], slope.at[s], sem2.at[2 * s + 1]))
        start_all(sent[-2:])
    wait_all(sent)


def ffn_out_forward(n_mp, *refs):
    hat1, vecs, hidden, own_out = refs[:4]
    parts = refs[4 : 4 + SLICES]
    layer_out, hat_out, inv_out, first = refs[12:16]
    w_out, act_s, acc, sem, sem2 = refs[16:]
    gain1, shift1, b_out, gain2, shift2 = [vecs[i : i + 1] for i in range(1, 6)]
    acts = each_of(hidden, act_s, sem2)
    copies = fetch_rows(own_out, parts, w_out, sem, 0)
    copies = [[acts[s]] + copies[s] for s in range(n_mp)]
    for s in range(AHEAD):
        start_all(copies[s])
    acc[...] = hat1[...] * gain1 + shift1 + b_out
    for s in range(n_mp):
        wait_all(copies[s])
        if s + AHEAD < n_mp:
            start_all(copies[s + AHEAD])
        acc[...] += nn(act_s[s], w_out[s])

    hat, inv = norm_rows(acc[...])
    hat_out[...] = hat
    inv_out[...] = jnp.broadcast_to(inv, inv_out.shape)
    out = (hat * gain2 + shift2).astype(low)
    layer_out[...] = out
    rows = [out[i * SEQ : i * SEQ + 1].astype(f32) for i in range(out.shape[0] // SEQ)]
    rows.append(jnp.zeros((BLOCK - len(rows), out.shape[1]), f32))
    first[...] = jnp.concatenate(rows, axis=0).astype(low)


def ranking(n_mp, sents, *refs):
    ids_row, ids_col, w_pool, vecs, scale = refs[:5]
    parts = refs[5:9]
    g_first, rows_out, g_out, g_bias, scale_out = refs[9:14]
    got, g_all, sem = refs[14:]
    me = lax.axis_index("mp")
    copies = []
    for p in range(SLICES):
        for s in range(n_mp):
            spot = got.at[slot(p) * n_mp + jnp.bitwise_xor(me, s)]
            copies.append(
                pltpu.make_async_copy(parts[p >> 1].at[s, p & 1], spot, sem.at[p * n_mp + s])
            )
    wait_all(start_all(copies))
    n = ids_row.shape[1]
    first = got[...].astype(f32).reshape(n, -1).astype(low)
    rows_out[...] = first
    pooled = jnp.tanh(nn(first, w_pool[...]) + vecs[6:7])
    inv_len = lax.rsqrt(jnp.sum(pooled * pooled, axis=-1, keepdims=True) + eps_norm)
    emb = pooled * inv_len
    emb_low = emb.astype(low)
    cosine = nt(emb_low, emb_low)
    row = lax.broadcasted_iota(jnp.int32, (n, n), 0)
    col = lax.broadcasted_iota(jnp.int32, (n, n), 1)
    even = lax.rem(row, 2) == 0
    in_row = jnp.logical_and(even, lax.rem(row, BLOCK) < sents)
    in_col = jnp.logical_and(lax.rem(col, 2) == 1, lax.rem(col, BLOCK) < sents)
    in_both = jnp.logical_and(in_row, in_col)
    same = jnp.logical_and(in_both, ids_col[...] == ids_row[...])
    one = same.astype(f32)
    diag = jnp.logical_and(in_both, col == row + 1).astype(f32)
    shifted = cosine - margin * diag
    logits = jnp.where(same, scale[...] * shifted, masked_low)
    grad = jnp.zeros_like(cosine)
    for axis in (1, 0):
        expd = jnp.exp(logits - jnp.max(logits, axis=axis, keepdims=True))
        expd = jnp.where(same, expd, 0.0)
        total = jnp.maximum(jnp.sum(expd, axis=axis, keepdims=True), 1e-30)
        count = jnp.maximum(jnp.sum(one, axis=axis, keepdims=True), 1.0)
        grad = grad + (expd / total - diag) / count
    scale_grad = jnp.sum(jnp.sum(grad * shifted, axis=1, keepdims=True), axis=0, keepdims=True)
    scale_out[...] = scale[...] - step_rate * jnp.broadcast_to(scale_grad, scale_out.shape)
    both = grad + grad.T
    g_emb = jnp.zeros_like(pooled)
    for _ in range(3):
        part = both.astype(low)
        both = both - part.astype(f32)
        g_emb = g_emb + nn(part, emb_low)
    g_emb = scale[0:1, 0:1] * g_emb
    g_pooled = inv_len * (g_emb - emb * jnp.sum(emb * g_emb, axis=-1, keepdims=True))
    g_pre = (g_pooled * (1.0 - pooled * pooled)).astype(low)
    g_out[...] = g_pre
    g_all[...] = g_pre.astype(f32)
    g_bias[...] = jnp.sum(g_all[...], axis=0, keepdims=True)
    at = (lax.axis_index("dp") * n_mp + me) * BLOCK
    own = g_all[pl.ds(pl.multiple_of(at, BLOCK), BLOCK)].astype(low)
    g_first[...] = nt(own, w_pool[...])


def out_backward(n_mp, *refs):
    cot, g_first, hat, inv, vecs, hidden = refs[:6]
    gain = vecs[4:5]
    g_z2, small, keep, send = refs[6:10]
    g_w, act_s, sem, sem2 = refs[10:]
    acts = fetch_each(hidden, act_s, sem2)
    rows = cot.shape[0]
    g_z2[...] = cot[...].astype(f32)
    for i in range(rows // SEQ):
        g_z2[i * SEQ : i * SEQ + 1] += g_first[i : i + 1]
    g_y = g_z2[...]
    small[...] = jnp.zeros_like(small)
    small[1:2] = jnp.sum(g_y * hat[...], axis=0, keepdims=True)
    small[2:3] = jnp.sum(g_y, axis=0, keepdims=True)
    g_z = norm_back(g_y, hat[...], inv[:, :1], gain)
    g_z2[...] = g_z
    small[0:1] = jnp.sum(g_z, axis=0, keepdims=True)
    g_ffn = g_z.astype(low)

    size = keep.shape[-2]
    sent = []
    for s in range(n_mp):
        acts[s].wait()
        g_w[s] = tn(act_s[s], g_ffn).astype(low)
        sent += send_shard(lambda s, p: row_spot(g_w, s, p, size), s, keep, send, sem, n_mp)
    wait_all(sent)


def in_backward(n_mp, *refs):
    g_z2, h1, hat, inv, vecs, slope, own_in, own_out = refs[:8]
    gain = vecs[1:2]
    in_parts = refs[8 : 8 + SLICES]
    out_parts = refs[16 : 16 + SLICES]
    g_z1, g_mid, small, keep, send = refs[24:29]
    w_in, w_out, slope_s, g_w, acc, sem, sem2, sem3 = refs[29:]
    slopes = each_of(slope, slope_s, sem3)
    out_copies = fetch_rows(own_out, out_parts, w_out, sem, 0)
    in_copies = fetch_rows(own_in, in_parts, w_in, sem, n_copies(n_mp))
    for s in range(AHEAD):
        start_all([slopes[s]] + out_copies[s] + in_copies[s])
    acc[...] = g_z2[...]
    g_ffn = g_z2[...].astype(low)
    size = keep.shape[-2]
    copies = []
    for s in range(n_mp):
        wait_all([slopes[s]] + out_copies[s])
        if s + AHEAD < n_mp:
            start_all([slopes[s + AHEAD]] + out_copies[s + AHEAD] + in_copies[s + AHEAD])
        g_pre = (nt(g_ffn, w_out[s]) * slope_s[s].astype(f32)).astype(low)
        g_mid[s] = jnp.sum(g_pre.astype(f32), axis=0, keepdims=True)
        g_w[s] = tn(h1[...], g_pre).astype(low)
        copies += send_shard(lambda s, p: row_spot(g_w, s, p, size), s, keep, send, sem2, n_mp)
        wait_all(in_copies[s])
        acc[...] += nt(g_pre, w_in[s])
    g_h1 = acc[...]
    small[...] = jnp.zeros_like(small)
    small[1:2] = jnp.sum(g_h1 * hat[...], axis=0, keepdims=True)
    small[2:3] = jnp.sum(g_h1, axis=0, keepdims=True)
    g_z = norm_back(g_h1, hat[...], inv[:, :1], gain)
    g_z1[...] = g_z
    small[0:1] = jnp.sum(g_z, axis=0, keepdims=True)
    wait_all(copies)


def attention_backward(n_mp, cols, *refs):
    g_z1, q, k, v, ctx, g_mid, small_one, small_two, w_all, p_all = refs[:10]
    g_q, g_k, g_v, total, g_wo = refs[10:15]
    w, p_keep, g_ctx, sem, sem2 = refs[15:]
    fetch = start_all([pltpu.make_async_copy(w_all.at[3], w, sem.at[0])])
    probs = fetch_each(p_all, p_keep, sem2)
    rows, width = g_z1.shape
    g_attn = g_z1[...].astype(low)
    wait_all(fetch)
    g_ctx[...] = nt(g_attn, w[...]).astype(low)
    for t in range(rows // PAIR):
        at = slice(t * PAIR, (t + 1) * PAIR)
        probs[t].wait()
        for j in range(width // LANES):
            lanes = slice(j * LANES, (j + 1) * LANES)
            q2, g2 = q[at, lanes], g_ctx[at, lanes]
            k2, v2 = split_heads(k[at, lanes]), split_heads(v[at, lanes])
            p = p_keep[t, j]
            g_p = nt(g2, v2)
            g_raw = []
            for i in (0, 1):
                half = slice(i * PAIR, (i + 1) * PAIR)
                inner = jnp.sum(p[:, half] * g_p[:, half], axis=-1, keepdims=True)
                g_raw.append((p[:, half] * (g_p[:, half] - inner) * 0.125).astype(low))
            g_raw = jnp.concatenate(g_raw, axis=1)
            g_v[at, lanes] = join_heads(tn(p.astype(low), g2)).astype(low)
            g_q[at, lanes] = nn(g_raw, k2).astype(low)
            g_k[at, lanes] = join_heads(tn(g_raw, q2)).astype(low)

    g_wo[...] = tn(ctx[...], g_attn).astype(low)
    total[...] = jnp.zeros_like(total)
    total[0:3] = small_one[0:3]
    total[3:6] = small_two[0:3]
    b_q = jnp.sum(g_q[...].astype(f32), axis=0, keepdims=True)
    b_v = jnp.sum(g_v[...].astype(f32), axis=0, keepdims=True)
    for s in range(n_mp):
        at = jnp.bitwise_xor(lax.axis_index("mp"), s)
        total[pl.ds(BLOCK + at, 1)] = g_mid[s]
        lanes = slice(s * cols, (s + 1) * cols)
        total[pl.ds(BLOCK + n_mp + at, 1), 0:cols] = b_q[:, lanes]
        total[pl.ds(BLOCK + n_mp + at, 1), cols : 2 * cols] = b_v[:, lanes]


def attention_weights(n_mp, cols, *refs):
    x, g_q, g_k, g_v, g_wo, keep, send, g_w, sem = refs
    g_w[3] = g_wo[...]
    g_w[0] = tn(g_q[...], x[...]).astype(low)
    g_w[1] = tn(g_k[...], x[...]).astype(low)
    g_w[2] = tn(g_v[...], x[...]).astype(low)
    size = keep.shape[-2]
    sent = []
    for s in range(n_mp):
        sent += send_shard(lambda s, p: att_spot(g_w, s, p, cols, size), s, keep, send, sem, n_mp)
    wait_all(sent)


def attention_inputs(n_mp, cols, *refs):
    g_z1, g_q, g_k, g_v, w_all, g_x, w, sem = refs
    fetch = start_all([pltpu.make_async_copy(w_all.at[i], w.at[i], sem.at[i]) for i in range(3)])
    total = g_z1[...]
    for i, g in enumerate((g_q, g_k, g_v)):
        fetch[i].wait()
        total = total + nn(g[...], w[i])
    g_x[...] = total


def finish_rows(cols, *refs):
    parts = refs[:SLICES]
    if cols:
        out, out_qkv, out_o, got, sem, got_att, sem_att = refs[SLICES:]
    else:
        out, got, sem = refs[SLICES:]
    size = parts[0].shape[0] // (2 if cols else 1)
    copies, more = [], []
    for p in range(SLICES):
        part = parts[p].at[pl.ds(0, size)]
        copies.append(pltpu.make_async_copy(part, row_spot(got, 0, p, size), sem.at[p]))
        if cols:
            part = parts[p].at[pl.ds(size, size)]
            spot = att_spot(got_att, 0, p, cols, size)
            more.append(pltpu.make_async_copy(part, spot, sem_att.at[p]))
    start_all(copies + more)
    wait_all(copies)
    out[...] = got[0].astype(f32)
    if cols:
        wait_all(more)
        for i in range(3):
            out_qkv[i] = got_att[i].astype(f32)
        out_o[...] = got_att[3].astype(f32)


def make(mesh):
    n_dp = mesh.shape["dp"]
    n_mp = mesh.shape["mp"]

    def dpx(x, bit):
        return lax.ppermute(x, "dp", [(i, i ^ bit) for i in range(n_dp)])

    def mpx(x, bit):
        return lax.ppermute(x, "mp", [(i, i ^ bit) for i in range(n_mp)])

    def bit_of(axis, bit):
        return (lax.axis_index(axis) & bit) != 0

    def flips(v, axis, bits, dims):
        for bit, dim in zip(bits, dims):
            v = jnp.where(bit_of(axis, bit), jnp.flip(v, dim), v)
        return v

    def plane_parts(r):
        got = [None] * SLICES
        for p in (0, 2, 4, 6):
            got[p] = dpx(r, p) if p else r
        for p in (0, 2, 4, 6):
            got[p + 1] = dpx(got[p], 1)
        return got

    def over_z(piece):
        return [mpx(piece, i) for i in range(1, n_mp)]

    def over_z_slow(own, *deps):
        got = [mpx(own, 1)]
        own = after(own, *deps)
        bit = 2
        while bit < n_mp:
            far = mpx(jnp.stack([own] + got), bit)
            got += [far[i] for i in range(bit)]
            bit *= 2
        return got

    def over_plane(r):
        return [dpx(r, 2), dpx(r, 4), dpx(r, 6)]

    def over_core(parts):
        return parts + [dpx(part, 1) for part in parts]

    def after(x, *deps):
        return lax.optimization_barrier((x, deps))[0]

    def own_piece(shard):
        rows = shard.shape[0] // SLICES
        return lax.dynamic_slice_in_dim(shard, (lax.axis_index("dp") % SLICES) * rows, rows, 0)

    def add(a, b):
        return (a.astype(f32) + b.astype(f32)).astype(low)

    def reduce_one(keep, got):
        return (
            add(keep[0, :, 1], got[0, :, 1]),
            add(keep[1, 1], got[1, 1]),
            add(keep[0, :, 0], got[0, :, 0]),
            add(keep[1, 0], got[1, 0]),
        )

    def reduce_two(a0, b0, a1, b1):
        return add(a0[1], a1[1]), add(b0[1], b1[1]), a0[0], a1[0], b0[0], b1[0]

    def reduce_three(a0, a1, b0, b1, a2, b2):
        a = a0.astype(f32) + a1.astype(f32) + a2.astype(f32)
        b = b0.astype(f32) + b1.astype(f32) + b2.astype(f32)
        u = [a[0], a[1], b[0], b[1]]
        bit = SLICES
        while bit < n_dp:
            u = [w.astype(low) for w in u]
            u = [w.astype(f32) + dpx(w, bit).astype(f32) for w in u]
            bit *= 2
        return [w.astype(low) for w in u]

    def reduce_last(u):
        total = u[0].astype(f32)
        for w in u[1:]:
            total = total + w.astype(f32)
        return total.astype(low)

    def mp_natural(v):
        bits = [1 << i for i in reversed(range(n_mp.bit_length() - 1))]
        shape = v.shape
        v = v.reshape((2,) * len(bits) + shape[1:])
        return flips(v, "mp", bits, range(len(bits))).reshape(shape)

    def gather_all(own):
        r = jnp.stack([own] + [mpx(own, s) for s in range(1, n_mp)])
        r = mp_natural(r)
        z = jnp.stack([r] + [dpx(r, b) for b in (2, 4, 6)])
        v = jnp.stack([z, dpx(z, 1)], 1).reshape((2, 2, 2) + r.shape)
        v = flips(v, "dp", (4, 2, 1), (0, 1, 2)).reshape((SLICES,) + r.shape)
        bit = SLICES
        while bit < n_dp:
            o = dpx(v, bit)
            up = bit_of("dp", bit)
            v = jnp.concatenate([jnp.where(up, o, v), jnp.where(up, v, o)], 0)
            bit *= 2
        return v.reshape((n_dp * n_mp,) + own.shape)

    def rank_part(first_rows, sents, pair_ids, w_pool, b_pool, scale):
        n_all = n_dp * n_mp
        width = first_rows.shape[-1]
        first_rows = first_rows[:, :sents].reshape(n_all * sents, width).astype(low)
        npairs = n_all * sents // 2
        pooled = jnp.tanh(
            jnp.dot(first_rows, w_pool, preferred_element_type=f32) + b_pool.astype(f32)
        )
        inv_len = lax.rsqrt(jnp.sum(pooled * pooled, axis=-1, keepdims=True) + eps_norm)
        emb_full = pooled * inv_len
        emb_pairs = emb_full.astype(low).reshape(npairs, 2, width)
        all_src, all_tgt = emb_pairs[:, 0, :], emb_pairs[:, 1, :]
        scale_value = scale[0]
        cosine = jnp.einsum("kd,md->km", all_src, all_tgt, preferred_element_type=f32)
        same = pair_ids[:, None] == pair_ids[None, :]
        counts = jnp.sum(same.astype(f32), axis=1)
        index_all = jnp.arange(npairs)
        diag_mask = (index_all[:, None] == index_all[None, :]).astype(f32)
        grad_row, part_row = rank_terms(
            cosine, same, diag_mask, (1.0 / counts)[:, None], scale_value, 1
        )
        grad_col, part_col = rank_terms(
            cosine, same, diag_mask, (1.0 / counts)[None, :], scale_value, 0
        )
        grad_all = grad_row + grad_col
        grad_src = scale_value * jnp.dot(grad_all, all_tgt.astype(f32), precision=high)
        grad_tgt = scale_value * jnp.einsum(
            "km,kd->md", grad_all, all_src.astype(f32), precision=high
        )
        new_scale = scale - step_rate * (jnp.sum(part_row) + jnp.sum(part_col))
        grad_emb = jnp.stack([grad_src, grad_tgt], axis=1).reshape(2 * npairs, width)
        grad_pooled = inv_len * (
            grad_emb - emb_full * jnp.sum(emb_full * grad_emb, axis=-1, keepdims=True)
        )
        grad_ppre = (grad_pooled * (1.0 - pooled * pooled)).astype(low)
        grad_pool = jnp.einsum("sd,se->de", first_rows, grad_ppre, preferred_element_type=f32)
        grad_b_pool = jnp.sum(grad_ppre.astype(f32), axis=0)
        own_ppre = lax.dynamic_slice_in_dim(
            grad_ppre, lax.axis_index(("dp", "mp")) * sents, sents, 0
        )
        grad_first = jnp.einsum("se,de->sd", own_ppre, w_pool, preferred_element_type=f32)
        grad_first = jnp.pad(grad_first, ((0, BLOCK - sents), (0, 0)))
        return grad_first, grad_pool, grad_b_pool, new_scale

    def on_device(
        inputs,
        token_ids,
        out_cot,
        pair_ids,
        w_qkv,
        b_qv,
        w_attn,
        b_attn,
        norm1_gain,
        norm1_bias,
        w_in,
        b_in,
        w_out,
        b_out,
        norm2_gain,
        norm2_bias,
        w_pool,
        b_pool,
        scale,
    ):
        rows, width = inputs.shape
        cols = w_qkv.shape[2]
        units = w_in.shape[1]
        sents = rows // SEQ
        shape = jax.ShapeDtypeStruct
        dma = pltpu.SemaphoreType.DMA
        vmem = pltpu.VMEM

        qkv_t = w_qkv.transpose(0, 2, 1)
        att_shard = jnp.concatenate([qkv_t.reshape(3 * cols, width), w_attn])
        size = att_shard.shape[0] // SLICES
        small = jnp.pad(jnp.concatenate([b_qv.reshape(-1), b_in]), (0, 2 * width - 2 * cols - units))
        small = small.reshape(2, width)
        att_z = over_z(jnp.concatenate([own_piece(att_shard), small]))
        vecs = jnp.stack(
            [b_attn, norm1_gain, norm1_bias, b_out, norm2_gain, norm2_bias, b_pool, b_pool]
        ).astype(f32)
        pieces = own_piece(w_in), own_piece(w_out)
        att_z[0] = after(att_z[0], vecs, *pieces)
        small = jnp.stack([small] + [r[size:] for r in att_z]).reshape(n_mp, -1).astype(f32)
        att_r = jnp.stack([r[:size] for r in att_z])
        in_z = over_z_slow(after(pieces[0], att_r))
        att_near = over_plane(att_r)
        att_parts = over_core([att_r] + att_near)
        in_r = jnp.stack(in_z)
        in_near = over_plane(after(in_r, *att_near))
        out_z = over_z_slow(after(pieces[1], in_z[0]), in_r)
        nc = n_copies(n_mp)
        own_qkv = att_shard[: 3 * cols].reshape(3, cols, width)

        def here(*arrays):
            return [(a, True) for a in arrays]

        def away(*arrays):
            return [(a, False) for a in arrays]

        ids = token_ids.reshape(rows // PAIR, 1, PAIR)

        rows_low, rows_f = shape((rows, width), low), shape((rows, width), f32)
        thin = shape((rows, 128), f32)
        w_shape = shape((4, n_mp * cols, width), low)
        p_shape = shape((rows // PAIR, width // LANES, PAIR, 2 * PAIR), f32)
        query, key_part, value_part, context, hat_one, inv_one, h1, w_all, p_all = call(
            functools.partial(attention_forward, n_mp, cols),
            here(after(inputs, out_z[0]), ids, small, vecs)
            + away(own_qkv, w_attn, *att_parts),
            here(rows_low, rows_low, rows_low, rows_low, rows_f, thin, rows_low)
            + away(w_shape, p_shape),
            [vmem(w_shape.shape, low), vmem(p_shape.shape, f32), dma((nc,)), dma((2,))],
            11,
        )
        out_r = jnp.stack(after(out_z, h1))
        out_near = over_plane(out_r)
        in_parts = over_core(after([in_r] + in_near, h1))
        mid = shape((n_mp, rows, units), low)
        tiny_shape = shape((BLOCK, width), f32)
        ids_row = jnp.repeat(pair_ids.reshape(-1, sents // 2), 2, axis=1)
        ids_row = jnp.pad(ids_row, ((0, 0), (0, BLOCK - sents))).reshape(1, -1)
        hidden, slope = call(
            functools.partial(ffn_in_forward, n_mp, 2 * cols),
            here(h1, small) + away(w_in, *in_parts),
            away(mid, mid),
            [vmem((n_mp, width, units), low), vmem(mid.shape, low), vmem(mid.shape, low)]
            + [dma((nc,)), dma((2 * n_mp,))],
            9,
        )
        out_parts = over_core(after([out_r] + out_near, hidden))
        layer_out, hat_two, inv_two, own_first = call(
            functools.partial(ffn_out_forward, n_mp),
            here(hat_one, vecs)
            + away(hidden, w_out, *out_parts),
            here(rows_low, rows_f, thin, shape((BLOCK, width), low)),
            [vmem((n_mp, units, width), low), vmem(mid.shape, low), vmem((rows, width), f32)]
            + [dma((nc,)), dma((n_mp,))],
            6,
        )
        if n_dp == SLICES:
            n = n_dp * n_mp * BLOCK
            r = jnp.stack([own_first, dpx(own_first, 1)])
            r = jnp.stack([r] + over_z(r))
            grad_first, all_first, all_ppre, grad_b_pool, new_scale = call(
                functools.partial(ranking, n_mp, sents),
                here(ids_row, ids_row.reshape(n, 1), w_pool, vecs)
                + here(jnp.broadcast_to(scale[None], (1, n)))
                + away(r, *over_plane(r)),
                here(tiny_shape, shape((n, width), low), shape((n, width), low))
                + here(shape((1, width), f32), shape((1, n), f32)),
                [vmem((n_dp * n_mp, BLOCK, width), low), vmem((n, width), f32)]
                + [dma((n_dp * n_mp,))],
                6,
            )
            grad_b_pool, new_scale = grad_b_pool[0], new_scale[0, :1]
        else:
            grad_first, grad_pool, grad_b_pool, new_scale = rank_part(
                gather_all(own_first), sents, pair_ids, w_pool, b_pool, scale
            )
        lot = shape((2, 2, 2, n_mp // 2, size, width), low)
        tiny = shape((BLOCK, width), f32)
        grad_z2, small_two, keep_o, send = call(
            functools.partial(out_backward, n_mp),
            here(out_cot, grad_first, hat_two, inv_two, vecs) + away(hidden),
            here(rows_f, tiny) + away(lot, lot),
            [vmem((n_mp, units, width), low), vmem(mid.shape, low)]
            + [dma((SLICES * n_mp,)), dma((n_mp,))],
            10,
        )
        got_o = dpx(send, 1)
        grad_z1, grad_b_in, small_one, keep_i, send = call(
            functools.partial(in_backward, n_mp),
            here(grad_z2, h1, hat_one, inv_one, vecs)
            + away(slope, w_in, w_out, *in_parts, *out_parts),
            here(rows_f, shape((n_mp, 1, units), f32), tiny) + away(lot, lot),
            [
                vmem((n_mp, width, units), low),
                vmem((n_mp, units, width), low),
                vmem(mid.shape, low),
                vmem((n_mp, width, units), low),
                vmem((rows, width), f32),
                dma((2 * nc,)),
                dma((SLICES * n_mp,)),
                dma((n_mp,)),
            ],
            17,
        )
        got_i = dpx(send, 1)
        step_o = reduce_one(keep_o, after(got_o, grad_z1))
        a_o, b_o = dpx(step_o[0], 2), dpx(step_o[1], 4)
        grad_q, grad_k, grad_v, total, grad_wo = call(
            functools.partial(attention_backward, n_mp, cols),
            here(after(grad_z1, step_o[0], step_o[1]), query, key_part, value_part, context)
            + here(grad_b_in, small_one, small_two)
            + away(w_all, p_all),
            here(rows_low, rows_low, rows_low, shape((BLOCK + 2 * n_mp, width), f32))
            + here(shape((n_mp * cols, width), low)),
            [vmem((n_mp * cols, width), low), vmem(p_shape.shape, f32), vmem((rows, width), low)]
            + [dma((1,)), dma((rows // PAIR,))],
            15,
        )
        hops = [functools.partial(mpx, bit=1 << i) for i in range(n_mp.bit_length() - 1)]
        hops += [functools.partial(dpx, bit=1)]
        hops += [functools.partial(dpx, bit=1 << i) for i in range(3, n_dp.bit_length() - 1)]
        hop = hops[0](total)
        step_i = reduce_one(keep_i, after(got_i, grad_q))
        a_i, b_i = dpx(step_i[0], 2), dpx(step_i[1], 4)
        step_o = reduce_two(step_o[2], step_o[3], after(a_o, grad_q), after(b_o, grad_q))
        a2_o, b2_o = dpx(step_o[0], 4), dpx(step_o[1], 2)
        keep_a, send = call(
            functools.partial(attention_weights, n_mp, cols),
            here(after(inputs, step_i[0], step_i[1], step_o[0], step_o[1]))
            + here(grad_q, grad_k, grad_v, grad_wo),
            away(lot, lot),
            [vmem((4, n_mp * cols, width), low), dma((SLICES * n_mp,))],
            7,
        )
        got_a = dpx(send, 1)
        total = total + after(hop, keep_a)
        hop = hops[1](total)
        (input_grad,) = call(
            functools.partial(attention_inputs, n_mp, cols),
            here(grad_z1, after(grad_q, keep_a), grad_k, grad_v) + away(w_all),
            here(rows_f),
            [vmem((3, n_mp * cols, width), low), dma((3,))],
            7,
        )
        step_a = reduce_one(keep_a, after(got_a, input_grad))
        a_a, b_a = dpx(step_a[0], 2), dpx(step_a[1], 4)
        step_o = reduce_three(*step_o[2:], *after([a2_o, b2_o], step_a[0], step_a[1]))
        z_o = [mpx(step_o[i], i) for i in range(1, n_mp)]
        total = total + after(hop, step_a[0])
        hop = hops[2](total)
        step_i = reduce_two(step_i[2], step_i[3], *after([a_i, b_i], step_a[0], step_a[1]))
        a2_i, b2_i = dpx(step_i[0], 4), dpx(step_i[1], 2)
        step_a = reduce_two(step_a[2], step_a[3], *after([a_a, b_a], step_i[0], step_i[1]))
        a2_a, b2_a = dpx(step_a[0], 4), dpx(step_a[1], 2)
        red_out = reduce_last(after([step_o[0]] + z_o, step_a[0]))
        total = total + after(hop, step_a[0])
        for h in hops[3:]:
            total = total + h(total)
        step_i = reduce_three(*step_i[2:], *after([a2_i, b2_i], step_a[0], step_a[1]))
        z_i = [mpx(step_i[i], i) for i in range(1, n_mp)]
        step_a = reduce_three(*step_a[2:], *after([a2_a, b2_a], step_i[0]))
        z_a = [mpx(step_a[i], i) for i in range(1, n_mp)]
        red_in = reduce_last(after([step_i[0]] + z_i, step_a[0]))
        out_own = plane_parts(red_out)
        total = total + dpx(after(total, step_a[0]), 2)
        total = total + dpx(total, 4)
        red_att = reduce_last(after([step_a[0]] + z_a, total))
        last_own = plane_parts(jnp.concatenate([red_in, red_att]))
        if n_dp == SLICES:
            grad_pool = tn(after(all_first, step_a[0]), all_ppre)
        take = lax.axis_index("mp")
        out_b_in = lax.dynamic_slice_in_dim(total, BLOCK + take, 1, 0)[0]
        out_b_qv = lax.dynamic_slice_in_dim(total, BLOCK + n_mp + take, 1, 0)
        out_b_qv = out_b_qv[0, : 2 * cols].reshape(2, cols)
        whole = shape((SLICES * size, width), f32)

        (done_out,) = call(
            functools.partial(finish_rows, 0),
            away(*out_own),
            here(whole),
            [vmem((1, SLICES * size, width), low), dma((SLICES,))],
            3,
        )
        done_in, done_qkv, done_attn = call(
            functools.partial(finish_rows, cols),
            away(*last_own),
            here(whole, shape((3, cols, width), f32), shape((cols, width), f32)),
            [vmem((1, SLICES * size, width), low), dma((SLICES,))]
            + [vmem((4, cols, width), low), dma((SLICES,))],
            4,
        )
        return (
            layer_out,
            input_grad,
            done_qkv.transpose(0, 2, 1),
            out_b_qv,
            done_attn,
            total[0],
            total[1],
            total[2],
            done_in,
            out_b_in,
            done_out,
            total[3],
            total[4],
            total[5],
            grad_pool,
            grad_b_pool,
            new_scale,
        )

    return on_device


def solution(mesh):
    rows, whole = P(("dp", "mp"), None), P()
    in_specs = (
        rows,
        P(("dp", "mp")),
        rows,
        whole,
        P(None, None, "mp"),
        P(None, "mp"),
        P("mp", None),
        whole,
        whole,
        whole,
        P(None, "mp"),
        P("mp"),
        P("mp", None),
        whole,
        whole,
        whole,
        whole,
        whole,
        whole,
    )
    out_specs = (
        rows,
        rows,
        P(None, None, "mp"),
        P(None, "mp"),
        P("mp", None),
        whole,
        whole,
        whole,
        P(None, "mp"),
        P("mp"),
        P("mp", None),
        whole,
        whole,
        whole,
        whole,
        whole,
        whole,
    )
    return jax.shard_map(
        make(mesh), mesh=mesh, in_specs=in_specs, out_specs=out_specs, check_vma=False
    )
```

```python
import functools

import jax
import jax.numpy as jnp
from jax import lax
from jax.experimental import pallas as pl
from jax.experimental.pallas import tpu as pltpu
from jax.sharding import PartitionSpec as P

HEAD_DIM = 64
SEQ = 64
SLICES = 8
PARTS = 8
PAIR = 2 * SEQ
LANES = 2 * HEAD_DIM
BLOCK = 8

eps_norm = 1e-12
margin = 0.3
step_rate = 1.0
masked_low = -1e30
high = lax.Precision.HIGHEST
f32 = jnp.float32
low = jnp.bfloat16
VMEM_BYTES = 58 << 20


def nn(a, b):
    return jnp.dot(a, b, preferred_element_type=f32)


def nt(a, b):
    return lax.dot_general(a, b, (((1,), (1,)), ((), ())), preferred_element_type=f32)


def tn(a, b):
    return lax.dot_general(a, b, (((0,), (0,)), ((), ())), preferred_element_type=f32)


def rank_terms(cosine, same, diag_mask, weight, scale_value, axis_of):
    shifted = cosine - margin * diag_mask
    logits = jnp.where(same, scale_value * shifted, masked_low)
    top = jnp.max(logits, axis=axis_of, keepdims=True)
    lse = top + jnp.log(jnp.sum(jnp.exp(logits - top), axis=axis_of, keepdims=True))
    probs = jnp.exp(logits - lse)
    grad_logit = weight * (probs - diag_mask)
    return (grad_logit, grad_logit * shifted)


def call(body, ins, outs, scratch, micros):
    def spec(vmem):
        return pl.BlockSpec(memory_space=pltpu.VMEM if vmem else pltpu.HBM)

    return pl.pallas_call(
        body,
        out_shape=[jax.ShapeDtypeStruct(o.shape, o.dtype) for o, _ in outs],
        in_specs=[spec(v) for _, v in ins],
        out_specs=[spec(v) for _, v in outs],
        scratch_shapes=scratch,
        compiler_params=pltpu.CompilerParams(vmem_limit_bytes=VMEM_BYTES),
        cost_estimate=pl.CostEstimate(flops=int(micros * 1.1e9), bytes_accessed=0, transcendentals=0),
    )(*[a for a, _ in ins])


def slot(p):
    me = lax.rem(lax.axis_index("dp"), SLICES)
    return jnp.bitwise_xor(me, p)


def start_all(copies):
    for c in copies:
        c.start()
    return copies


def wait_all(copies):
    for c in copies:
        c.wait()


def att_spot(ref, s, p, cols, size, first=0, rows=None):
    at = slot(p)
    row = pl.multiple_of(s * cols + lax.rem(at, 2) * size + first, 16)
    return ref.at[at // 2, pl.ds(row, rows or size)]


def row_spot(ref, s, p, size, first=0, rows=None):
    return ref.at[s, pl.ds(pl.multiple_of(slot(p) * size + first, 16), rows or size)]


def slices_of(parts):
    full = parts[0].shape[-2]
    return [(part, 2 * (i % 4) + i // 4, 0, full) for i, part in enumerate(parts)]


def fetch_att(own_qkv, own_o, parts, dst, sem, cols):
    copies = []
    for i in range(3):
        copies.append(pltpu.make_async_copy(own_qkv.at[i], dst.at[i, pl.ds(0, cols)], sem.at[i]))
    copies.append(pltpu.make_async_copy(own_o, dst.at[3, pl.ds(0, cols)], sem.at[3]))
    k = 4
    size = parts[0].shape[1]
    for part, p, at, n in slices_of(parts):
        for s in range(part.shape[0]):
            spot = att_spot(dst, s + 1, p, cols, size, at, n)
            copies.append(pltpu.make_async_copy(part.at[s], spot, sem.at[k]))
            k += 1
    return start_all(copies)


def fetch_rows(own, parts, dst, sem, base):
    copies = [[pltpu.make_async_copy(own, dst.at[0], sem.at[base])]]
    k = base + 1
    size = parts[0].shape[1]
    for s in range(parts[0].shape[0]):
        copies.append([])
        for part, p, at, n in slices_of(parts):
            spot = row_spot(dst, s + 1, p, size, at, n)
            copies[-1].append(pltpu.make_async_copy(part.at[s], spot, sem.at[k]))
            k += 1
    return copies


def each_of(src, dst, sem):
    return [pltpu.make_async_copy(src.at[i], dst.at[i], sem.at[i]) for i in range(src.shape[0])]


def fetch_each(src, dst, sem):
    return start_all(each_of(src, dst, sem))


AHEAD = 2


def n_copies(n_mp):
    return 4 + PARTS * (n_mp - 1)


def send_shard(src_of, s, g_keep, g_send, sem, n_mp):
    copies = []
    for p in range(SLICES):
        dst = g_send if p & 1 else g_keep
        spot = dst.at[s // 2, p >> 2, (p >> 1) & 1, s % 2]
        copies.append(pltpu.make_async_copy(src_of(s, p), spot, sem.at[SLICES * s + p]))
    return start_all(copies)


def mean_of(v):
    return jnp.sum(v, axis=-1, keepdims=True) * (1.0 / v.shape[-1])


def norm_rows(z):
    center = z - mean_of(z)
    inv = lax.rsqrt(mean_of(center * center) + eps_norm)
    return center * inv, inv


def norm_back(grad_out, hat, inv, gain):
    scaled = grad_out * gain
    return inv * (scaled - mean_of(scaled) - hat * mean_of(scaled * hat))


def pair_mask(ids_row):
    row = lax.broadcasted_iota(jnp.int32, (PAIR, PAIR), 0) >= SEQ
    col = lax.broadcasted_iota(jnp.int32, (PAIR, PAIR), 1) >= SEQ
    return jnp.logical_and(row == col, ids_row != 0)


def split_heads(v):
    first = lax.broadcasted_iota(jnp.int32, v.shape, 1) < HEAD_DIM
    zero = jnp.zeros_like(v)
    return jnp.concatenate([jnp.where(first, v, zero), jnp.where(first, zero, v)], axis=0)


def join_heads(v):
    half = v.shape[0] // 2
    first = lax.broadcasted_iota(jnp.int32, (half, v.shape[1]), 1) < HEAD_DIM
    return jnp.where(first, v[:half], v[half:])


def softmax_of(scores, mask):
    scores = jnp.where(mask, scores * 0.125, masked_low)
    expd = jnp.exp(scores - jnp.max(scores, axis=-1, keepdims=True))
    return expd / jnp.sum(expd, axis=-1, keepdims=True)


def attention_forward(n_mp, cols, *refs):
    x, ids, small, vecs, own_qkv, own_o = refs[:6]
    parts = refs[6 : 6 + PARTS]
    q, k, v, ctx, hat_out, inv_out, h1, w_all, p_all = refs[14:23]
    w, p_keep, sem, sem2 = refs[23:]
    b_attn, gain, shift = vecs[0:1], vecs[1:2], vecs[2:3]
    copies = fetch_att(own_qkv, own_o, parts, w, sem, cols)
    wait_all(copies)
    sent = start_all([pltpu.make_async_copy(w, w_all, sem2.at[0])])
    rows, width = x.shape
    b_q = jnp.concatenate([small[s : s + 1, :cols] for s in range(n_mp)], axis=1)
    b_v = jnp.concatenate([small[s : s + 1, cols : 2 * cols] for s in range(n_mp)], axis=1)
    q[...] = (nt(x[...], w[0]) + b_q).astype(low)
    k[...] = nt(x[...], w[1]).astype(low)
    v[...] = (nt(x[...], w[2]) + b_v).astype(low)

    for t in range(rows // PAIR):
        at = slice(t * PAIR, (t + 1) * PAIR)
        mask = pair_mask(ids[t])
        for j in range(width // LANES):
            lanes = slice(j * LANES, (j + 1) * LANES)
            raw = nt(q[at, lanes], split_heads(k[at, lanes]))
            probs = [softmax_of(raw[:, i * PAIR : (i + 1) * PAIR], mask) for i in (0, 1)]
            probs = jnp.concatenate(probs, axis=1)
            p_keep[t, j] = probs
            out = nn(probs.astype(low), split_heads(v[at, lanes]))
            ctx[at, lanes] = out.astype(low)

    sent += start_all([pltpu.make_async_copy(p_keep, p_all, sem2.at[1])])
    z = x[...].astype(f32) + nn(ctx[...], w[3]) + b_attn
    hat, inv = norm_rows(z)
    hat_out[...] = hat
    inv_out[...] = jnp.broadcast_to(inv, inv_out.shape)
    h1[...] = (hat * gain + shift).astype(low)
    wait_all(sent)


def gelu_pair(pre):
    size = jnp.abs(pre)
    t = 1.0 / (1.0 + 0.2316418882663604 * size)
    bell = jnp.exp(-0.5 * pre * pre)
    poly = t * (
        0.127414796
        + t * (-0.142248368 + t * (0.7107068705 + t * (-0.7265760135 + t * 0.5307027145)))
    )
    tail = poly * bell
    phi = jnp.where(pre >= 0.0, 1.0 - tail, tail)
    return pre * phi, phi + pre * (bell * 0.3989422804014327)


def ffn_in_forward(n_mp, spot, *refs):
    h1, small, own_in = refs[:3]
    parts = refs[3 : 3 + SLICES]
    hidden, slope, w_in, act_s, slope_s, sem, sem2 = refs[11:]
    copies = fetch_rows(own_in, parts, w_in, sem, 0)
    sent = []
    for s in range(AHEAD):
        start_all(copies[s])
    for s in range(n_mp):
        wait_all(copies[s])
        if s + AHEAD < n_mp:
            start_all(copies[s + AHEAD])
        pre = nn(h1[...], w_in[s]) + small[s : s + 1, spot : spot + w_in.shape[2]]
        act, grad = gelu_pair(pre)
        act_s[s] = act.astype(low)
        slope_s[s] = grad.astype(low)
        sent.append(pltpu.make_async_copy(act_s.at[s], hidden.at[s], sem2.at[2 * s]))
        sent.append(pltpu.make_async_copy(slope_s.at[s], slope.at[s], sem2.at[2 * s + 1]))
        start_all(sent[-2:])
    wait_all(sent)


def ffn_out_forward(n_mp, *refs):
    hat1, vecs, hidden, own_out = refs[:4]
    parts = refs[4 : 4 + SLICES]
    layer_out, hat_out, inv_out, first = refs[12:16]
    w_out, act_s, acc, sem, sem2 = refs[16:]
    gain1, shift1, b_out, gain2, shift2 = [vecs[i : i + 1] for i in range(1, 6)]
    acts = each_of(hidden, act_s, sem2)
    copies = fetch_rows(own_out, parts, w_out, sem, 0)
    copies = [[acts[s]] + copies[s] for s in range(n_mp)]
    for s in range(AHEAD):
        start_all(copies[s])
    acc[...] = hat1[...] * gain1 + shift1 + b_out
    for s in range(n_mp):
        wait_all(copies[s])
        if s + AHEAD < n_mp:
            start_all(copies[s + AHEAD])
        acc[...] += nn(act_s[s], w_out[s])

    hat, inv = norm_rows(acc[...])
    hat_out[...] = hat
    inv_out[...] = jnp.broadcast_to(inv, inv_out.shape)
    out = (hat * gain2 + shift2).astype(low)
    layer_out[...] = out
    rows = [out[i * SEQ : i * SEQ + 1].astype(f32) for i in range(out.shape[0] // SEQ)]
    rows.append(jnp.zeros((BLOCK - len(rows), out.shape[1]), f32))
    first[...] = jnp.concatenate(rows, axis=0).astype(low)


def ranking(n_mp, sents, *refs):
    ids_row, ids_col, w_pool, vecs, scale = refs[:5]
    parts = refs[5:9]
    g_first, rows_out, g_out, g_bias, scale_out = refs[9:14]
    got, g_all, sem = refs[14:]
    me = lax.axis_index("mp")
    copies = []
    for p in range(SLICES):
        for s in range(n_mp):
            spot = got.at[slot(p) * n_mp + jnp.bitwise_xor(me, s)]
            copies.append(
                pltpu.make_async_copy(parts[p >> 1].at[s, p & 1], spot, sem.at[p * n_mp + s])
            )
    wait_all(start_all(copies))
    n = ids_row.shape[1]
    first = got[...].astype(f32).reshape(n, -1).astype(low)
    rows_out[...] = first
    pooled = jnp.tanh(nn(first, w_pool[...]) + vecs[6:7])
    inv_len = lax.rsqrt(jnp.sum(pooled * pooled, axis=-1, keepdims=True) + eps_norm)
    emb = pooled * inv_len
    emb_low = emb.astype(low)
    cosine = nt(emb_low, emb_low)
    row = lax.broadcasted_iota(jnp.int32, (n, n), 0)
    col = lax.broadcasted_iota(jnp.int32, (n, n), 1)
    even = lax.rem(row, 2) == 0
    in_row = jnp.logical_and(even, lax.rem(row, BLOCK) < sents)
    in_col = jnp.logical_and(lax.rem(col, 2) == 1, lax.rem(col, BLOCK) < sents)
    in_both = jnp.logical_and(in_row, in_col)
    same = jnp.logical_and(in_both, ids_col[...] == ids_row[...])
    one = same.astype(f32)
    diag = jnp.logical_and(in_both, col == row + 1).astype(f32)
    shifted = cosine - margin * diag
    logits = jnp.where(same, scale[...] * shifted, masked_low)
    grad = jnp.zeros_like(cosine)
    for axis in (1, 0):
        expd = jnp.exp(logits - jnp.max(logits, axis=axis, keepdims=True))
        expd = jnp.where(same, expd, 0.0)
        total = jnp.maximum(jnp.sum(expd, axis=axis, keepdims=True), 1e-30)
        count = jnp.maximum(jnp.sum(one, axis=axis, keepdims=True), 1.0)
        grad = grad + (expd / total - diag) / count
    scale_grad = jnp.sum(jnp.sum(grad * shifted, axis=1, keepdims=True), axis=0, keepdims=True)
    scale_out[...] = scale[...] - step_rate * jnp.broadcast_to(scale_grad, scale_out.shape)
    both = grad + grad.T
    g_emb = jnp.zeros_like(pooled)
    for _ in range(3):
        part = both.astype(low)
        both = both - part.astype(f32)
        g_emb = g_emb + nn(part, emb_low)
    g_emb = scale[0:1, 0:1] * g_emb
    g_pooled = inv_len * (g_emb - emb * jnp.sum(emb * g_emb, axis=-1, keepdims=True))
    g_pre = (g_pooled * (1.0 - pooled * pooled)).astype(low)
    g_out[...] = g_pre
    g_all[...] = g_pre.astype(f32)
    g_bias[...] = jnp.sum(g_all[...], axis=0, keepdims=True)
    at = (lax.axis_index("dp") * n_mp + me) * BLOCK
    own = g_all[pl.ds(pl.multiple_of(at, BLOCK), BLOCK)].astype(low)
    g_first[...] = nt(own, w_pool[...])


def out_backward(n_mp, *refs):
    cot, g_first, hat, inv, vecs, hidden = refs[:6]
    gain = vecs[4:5]
    g_z2, small, keep, send = refs[6:10]
    g_w, act_s, sem, sem2 = refs[10:]
    acts = fetch_each(hidden, act_s, sem2)
    rows = cot.shape[0]
    g_z2[...] = cot[...].astype(f32)
    for i in range(rows // SEQ):
        g_z2[i * SEQ : i * SEQ + 1] += g_first[i : i + 1]
    g_y = g_z2[...]
    small[...] = jnp.zeros_like(small)
    small[1:2] = jnp.sum(g_y * hat[...], axis=0, keepdims=True)
    small[2:3] = jnp.sum(g_y, axis=0, keepdims=True)
    g_z = norm_back(g_y, hat[...], inv[:, :1], gain)
    g_z2[...] = g_z
    small[0:1] = jnp.sum(g_z, axis=0, keepdims=True)
    g_ffn = g_z.astype(low)

    size = keep.shape[-2]
    sent = []
    for s in range(n_mp):
        acts[s].wait()
        g_w[s] = tn(act_s[s], g_ffn).astype(low)
        sent += send_shard(lambda s, p: row_spot(g_w, s, p, size), s, keep, send, sem, n_mp)
    wait_all(sent)


def in_backward(n_mp, *refs):
    g_z2, h1, hat, inv, vecs, slope, own_in, own_out = refs[:8]
    gain = vecs[1:2]
    in_parts = refs[8 : 8 + SLICES]
    out_parts = refs[16 : 16 + SLICES]
    g_z1, g_mid, small, keep, send = refs[24:29]
    w_in, w_out, slope_s, g_w, acc, sem, sem2, sem3 = refs[29:]
    slopes = each_of(slope, slope_s, sem3)
    out_copies = fetch_rows(own_out, out_parts, w_out, sem, 0)
    in_copies = fetch_rows(own_in, in_parts, w_in, sem, n_copies(n_mp))
    for s in range(AHEAD):
        start_all([slopes[s]] + out_copies[s] + in_copies[s])
    acc[...] = g_z2[...]
    g_ffn = g_z2[...].astype(low)
    size = keep.shape[-2]
    copies = []
    for s in range(n_mp):
        wait_all([slopes[s]] + out_copies[s])
        if s + AHEAD < n_mp:
            start_all([slopes[s + AHEAD]] + out_copies[s + AHEAD] + in_copies[s + AHEAD])
        g_pre = (nt(g_ffn, w_out[s]) * slope_s[s].astype(f32)).astype(low)
        g_mid[s] = jnp.sum(g_pre.astype(f32), axis=0, keepdims=True)
        g_w[s] = tn(h1[...], g_pre).astype(low)
        copies += send_shard(lambda s, p: row_spot(g_w, s, p, size), s, keep, send, sem2, n_mp)
        wait_all(in_copies[s])
        acc[...] += nt(g_pre, w_in[s])
    g_h1 = acc[...]
    small[...] = jnp.zeros_like(small)
    small[1:2] = jnp.sum(g_h1 * hat[...], axis=0, keepdims=True)
    small[2:3] = jnp.sum(g_h1, axis=0, keepdims=True)
    g_z = norm_back(g_h1, hat[...], inv[:, :1], gain)
    g_z1[...] = g_z
    small[0:1] = jnp.sum(g_z, axis=0, keepdims=True)
    wait_all(copies)


def attention_backward(n_mp, cols, *refs):
    g_z1, q, k, v, ctx, g_mid, small_one, small_two, w_all, p_all = refs[:10]
    g_q, g_k, g_v, total, g_wo = refs[10:15]
    w, p_keep, g_ctx, sem, sem2 = refs[15:]
    fetch = start_all([pltpu.make_async_copy(w_all.at[3], w, sem.at[0])])
    probs = fetch_each(p_all, p_keep, sem2)
    rows, width = g_z1.shape
    g_attn = g_z1[...].astype(low)
    wait_all(fetch)
    g_ctx[...] = nt(g_attn, w[...]).astype(low)
    for t in range(rows // PAIR):
        at = slice(t * PAIR, (t + 1) * PAIR)
        probs[t].wait()
        for j in range(width // LANES):
            lanes = slice(j * LANES, (j + 1) * LANES)
            q2, g2 = q[at, lanes], g_ctx[at, lanes]
            k2, v2 = split_heads(k[at, lanes]), split_heads(v[at, lanes])
            p = p_keep[t, j]
            g_p = nt(g2, v2)
            g_raw = []
            for i in (0, 1):
                half = slice(i * PAIR, (i + 1) * PAIR)
                inner = jnp.sum(p[:, half] * g_p[:, half], axis=-1, keepdims=True)
                g_raw.append((p[:, half] * (g_p[:, half] - inner) * 0.125).astype(low))
            g_raw = jnp.concatenate(g_raw, axis=1)
            g_v[at, lanes] = join_heads(tn(p.astype(low), g2)).astype(low)
            g_q[at, lanes] = nn(g_raw, k2).astype(low)
            g_k[at, lanes] = join_heads(tn(g_raw, q2)).astype(low)

    g_wo[...] = tn(ctx[...], g_attn).astype(low)
    total[...] = jnp.zeros_like(total)
    total[0:3] = small_one[0:3]
    total[3:6] = small_two[0:3]
    b_q = jnp.sum(g_q[...].astype(f32), axis=0, keepdims=True)
    b_v = jnp.sum(g_v[...].astype(f32), axis=0, keepdims=True)
    for s in range(n_mp):
        at = jnp.bitwise_xor(lax.axis_index("mp"), s)
        total[pl.ds(BLOCK + at, 1)] = g_mid[s]
        lanes = slice(s * cols, (s + 1) * cols)
        total[pl.ds(BLOCK + n_mp + at, 1), 0:cols] = b_q[:, lanes]
        total[pl.ds(BLOCK + n_mp + at, 1), cols : 2 * cols] = b_v[:, lanes]


def attention_weights(n_mp, cols, *refs):
    x, g_q, g_k, g_v, g_wo, keep, send, g_w, sem = refs
    g_w[3] = g_wo[...]
    g_w[0] = tn(g_q[...], x[...]).astype(low)
    g_w[1] = tn(g_k[...], x[...]).astype(low)
    g_w[2] = tn(g_v[...], x[...]).astype(low)
    size = keep.shape[-2]
    sent = []
    for s in range(n_mp):
        sent += send_shard(lambda s, p: att_spot(g_w, s, p, cols, size), s, keep, send, sem, n_mp)
    wait_all(sent)


def attention_inputs(n_mp, cols, *refs):
    g_z1, g_q, g_k, g_v, w_all, g_x, w, sem = refs
    fetch = start_all([pltpu.make_async_copy(w_all.at[i], w.at[i], sem.at[i]) for i in range(3)])
    total = g_z1[...]
    for i, g in enumerate((g_q, g_k, g_v)):
        fetch[i].wait()
        total = total + nn(g[...], w[i])
    g_x[...] = total


def finish_rows(cols, *refs):
    parts = refs[:SLICES]
    if cols:
        out, out_qkv, out_o = refs[SLICES:]
    else:
        (out,) = refs[SLICES:]
    size = parts[0].shape[0] // (2 if cols else 1)
    for p in range(SLICES):
        at = slot(p)
        out[pl.ds(pl.multiple_of(at * size, 32), size)] = parts[p][0:size].astype(f32)
        if cols:
            rows = pl.ds(pl.multiple_of(lax.rem(at, 2) * size, 32), size)

            @pl.when(at // 2 < 3)
            def _():
                out_qkv[at // 2, rows] = parts[p][size : 2 * size].astype(f32)

            @pl.when(at // 2 == 3)
            def _():
                out_o[rows] = parts[p][size : 2 * size].astype(f32)


def make(mesh):
    n_dp = mesh.shape["dp"]
    n_mp = mesh.shape["mp"]

    def dpx(x, bit):
        return lax.ppermute(x, "dp", [(i, i ^ bit) for i in range(n_dp)])

    def mpx(x, bit):
        return lax.ppermute(x, "mp", [(i, i ^ bit) for i in range(n_mp)])

    def bit_of(axis, bit):
        return (lax.axis_index(axis) & bit) != 0

    def flips(v, axis, bits, dims):
        for bit, dim in zip(bits, dims):
            v = jnp.where(bit_of(axis, bit), jnp.flip(v, dim), v)
        return v

    def plane_parts(r):
        got = [None] * SLICES
        for p in (0, 2, 4, 6):
            got[p] = dpx(r, p) if p else r
        for p in (0, 2, 4, 6):
            got[p + 1] = dpx(got[p], 1)
        return got

    def over_z(piece):
        return [mpx(piece, i) for i in range(1, n_mp)]

    def over_z_slow(own, *deps):
        got = [mpx(own, 1)]
        own = after(own, *deps)
        bit = 2
        while bit < n_mp:
            far = mpx(jnp.stack([own] + got), bit)
            got += [far[i] for i in range(bit)]
            bit *= 2
        return got

    def over_plane(r):
        return [dpx(r, 2), dpx(r, 4), dpx(r, 6)]

    def over_core(parts):
        return parts + [dpx(part, 1) for part in parts]

    def after(x, *deps):
        return lax.optimization_barrier((x, deps))[0]

    def own_piece(shard):
        rows = shard.shape[0] // SLICES
        return lax.dynamic_slice_in_dim(shard, (lax.axis_index("dp") % SLICES) * rows, rows, 0)

    def add(a, b):
        return (a.astype(f32) + b.astype(f32)).astype(low)

    def reduce_one(keep, got):
        return (
            add(keep[0, :, 1], got[0, :, 1]),
            add(keep[1, 1], got[1, 1]),
            add(keep[0, :, 0], got[0, :, 0]),
            add(keep[1, 0], got[1, 0]),
        )

    def reduce_two(a0, b0, a1, b1):
        return add(a0[1], a1[1]), add(b0[1], b1[1]), a0[0], a1[0], b0[0], b1[0]

    def reduce_three(a0, a1, b0, b1, a2, b2):
        a = a0.astype(f32) + a1.astype(f32) + a2.astype(f32)
        b = b0.astype(f32) + b1.astype(f32) + b2.astype(f32)
        u = [a[0], a[1], b[0], b[1]]
        bit = SLICES
        while bit < n_dp:
            u = [w.astype(low) for w in u]
            u = [w.astype(f32) + dpx(w, bit).astype(f32) for w in u]
            bit *= 2
        return [w.astype(low) for w in u]

    def reduce_last(u):
        total = u[0].astype(f32)
        for w in u[1:]:
            total = total + w.astype(f32)
        return total.astype(low)

    def mp_natural(v):
        bits = [1 << i for i in reversed(range(n_mp.bit_length() - 1))]
        shape = v.shape
        v = v.reshape((2,) * len(bits) + shape[1:])
        return flips(v, "mp", bits, range(len(bits))).reshape(shape)

    def gather_all(own):
        r = jnp.stack([own] + [mpx(own, s) for s in range(1, n_mp)])
        r = mp_natural(r)
        z = jnp.stack([r] + [dpx(r, b) for b in (2, 4, 6)])
        v = jnp.stack([z, dpx(z, 1)], 1).reshape((2, 2, 2) + r.shape)
        v = flips(v, "dp", (4, 2, 1), (0, 1, 2)).reshape((SLICES,) + r.shape)
        bit = SLICES
        while bit < n_dp:
            o = dpx(v, bit)
            up = bit_of("dp", bit)
            v = jnp.concatenate([jnp.where(up, o, v), jnp.where(up, v, o)], 0)
            bit *= 2
        return v.reshape((n_dp * n_mp,) + own.shape)

    def rank_part(first_rows, sents, pair_ids, w_pool, b_pool, scale):
        n_all = n_dp * n_mp
        width = first_rows.shape[-1]
        first_rows = first_rows[:, :sents].reshape(n_all * sents, width).astype(low)
        npairs = n_all * sents // 2
        pooled = jnp.tanh(
            jnp.dot(first_rows, w_pool, preferred_element_type=f32) + b_pool.astype(f32)
        )
        inv_len = lax.rsqrt(jnp.sum(pooled * pooled, axis=-1, keepdims=True) + eps_norm)
        emb_full = pooled * inv_len
        emb_pairs = emb_full.astype(low).reshape(npairs, 2, width)
        all_src, all_tgt = emb_pairs[:, 0, :], emb_pairs[:, 1, :]
        scale_value = scale[0]
        cosine = jnp.einsum("kd,md->km", all_src, all_tgt, preferred_element_type=f32)
        same = pair_ids[:, None] == pair_ids[None, :]
        counts = jnp.sum(same.astype(f32), axis=1)
        index_all = jnp.arange(npairs)
        diag_mask = (index_all[:, None] == index_all[None, :]).astype(f32)
        grad_row, part_row = rank_terms(
            cosine, same, diag_mask, (1.0 / counts)[:, None], scale_value, 1
        )
        grad_col, part_col = rank_terms(
            cosine, same, diag_mask, (1.0 / counts)[None, :], scale_value, 0
        )
        grad_all = grad_row + grad_col
        grad_src = scale_value * jnp.dot(grad_all, all_tgt.astype(f32), precision=high)
        grad_tgt = scale_value * jnp.einsum(
            "km,kd->md", grad_all, all_src.astype(f32), precision=high
        )
        new_scale = scale - step_rate * (jnp.sum(part_row) + jnp.sum(part_col))
        grad_emb = jnp.stack([grad_src, grad_tgt], axis=1).reshape(2 * npairs, width)
        grad_pooled = inv_len * (
            grad_emb - emb_full * jnp.sum(emb_full * grad_emb, axis=-1, keepdims=True)
        )
        grad_ppre = (grad_pooled * (1.0 - pooled * pooled)).astype(low)
        grad_pool = jnp.einsum("sd,se->de", first_rows, grad_ppre, preferred_element_type=f32)
        grad_b_pool = jnp.sum(grad_ppre.astype(f32), axis=0)
        own_ppre = lax.dynamic_slice_in_dim(
            grad_ppre, lax.axis_index(("dp", "mp")) * sents, sents, 0
        )
        grad_first = jnp.einsum("se,de->sd", own_ppre, w_pool, preferred_element_type=f32)
        grad_first = jnp.pad(grad_first, ((0, BLOCK - sents), (0, 0)))
        return grad_first, grad_pool, grad_b_pool, new_scale

    def on_device(
        inputs,
        token_ids,
        out_cot,
        pair_ids,
        w_qkv,
        b_qv,
        w_attn,
        b_attn,
        norm1_gain,
        norm1_bias,
        w_in,
        b_in,
        w_out,
        b_out,
        norm2_gain,
        norm2_bias,
        w_pool,
        b_pool,
        scale,
    ):
        rows, width = inputs.shape
        cols = w_qkv.shape[2]
        units = w_in.shape[1]
        sents = rows // SEQ
        shape = jax.ShapeDtypeStruct
        dma = pltpu.SemaphoreType.DMA
        vmem = pltpu.VMEM

        qkv_t = w_qkv.transpose(0, 2, 1)
        att_shard = jnp.concatenate([qkv_t.reshape(3 * cols, width), w_attn])
        size = att_shard.shape[0] // SLICES
        small = jnp.pad(jnp.concatenate([b_qv.reshape(-1), b_in]), (0, 2 * width - 2 * cols - units))
        small = small.reshape(2, width)
        att_z = over_z(jnp.concatenate([own_piece(att_shard), small]))
        vecs = jnp.stack(
            [b_attn, norm1_gain, norm1_bias, b_out, norm2_gain, norm2_bias, b_pool, b_pool]
        ).astype(f32)
        pieces = own_piece(w_in), own_piece(w_out)
        att_z[0] = after(att_z[0], vecs, *pieces)
        small = jnp.stack([small] + [r[size:] for r in att_z]).reshape(n_mp, -1).astype(f32)
        att_r = jnp.stack([r[:size] for r in att_z])
        in_z = over_z_slow(after(pieces[0], att_r))
        att_near = over_plane(att_r)
        att_parts = over_core([att_r] + att_near)
        in_r = jnp.stack(in_z)
        in_near = over_plane(after(in_r, *att_near))
        out_z = over_z_slow(after(pieces[1], in_z[0]), in_r)
        nc = n_copies(n_mp)
        own_qkv = att_shard[: 3 * cols].reshape(3, cols, width)

        def here(*arrays):
            return [(a, True) for a in arrays]

        def away(*arrays):
            return [(a, False) for a in arrays]

        ids = token_ids.reshape(rows // PAIR, 1, PAIR)

        rows_low, rows_f = shape((rows, width), low), shape((rows, width), f32)
        thin = shape((rows, 128), f32)
        w_shape = shape((4, n_mp * cols, width), low)
        p_shape = shape((rows // PAIR, width // LANES, PAIR, 2 * PAIR), f32)
        query, key_part, value_part, context, hat_one, inv_one, h1, w_all, p_all = call(
            functools.partial(attention_forward, n_mp, cols),
            here(after(inputs, out_z[0]), ids, small, vecs)
            + away(own_qkv, w_attn, *att_parts),
            here(rows_low, rows_low, rows_low, rows_low, rows_f, thin, rows_low)
            + away(w_shape, p_shape),
            [vmem(w_shape.shape, low), vmem(p_shape.shape, f32), dma((nc,)), dma((2,))],
            11,
        )
        out_r = jnp.stack(after(out_z, h1))
        out_near = over_plane(out_r)
        in_parts = over_core(after([in_r] + in_near, h1))
        mid = shape((n_mp, rows, units), low)
        tiny_shape = shape((BLOCK, width), f32)
        ids_row = jnp.repeat(pair_ids.reshape(-1, sents // 2), 2, axis=1)
        ids_row = jnp.pad(ids_row, ((0, 0), (0, BLOCK - sents))).reshape(1, -1)
        hidden, slope = call(
            functools.partial(ffn_in_forward, n_mp, 2 * cols),
            here(h1, small) + away(w_in, *in_parts),
            away(mid, mid),
            [vmem((n_mp, width, units), low), vmem(mid.shape, low), vmem(mid.shape, low)]
            + [dma((nc,)), dma((2 * n_mp,))],
            9,
        )
        out_parts = over_core(after([out_r] + out_near, hidden))
        layer_out, hat_two, inv_two, own_first = call(
            functools.partial(ffn_out_forward, n_mp),
            here(hat_one, vecs)
            + away(hidden, w_out, *out_parts),
            here(rows_low, rows_f, thin, shape((BLOCK, width), low)),
            [vmem((n_mp, units, width), low), vmem(mid.shape, low), vmem((rows, width), f32)]
            + [dma((nc,)), dma((n_mp,))],
            6,
        )
        if n_dp == SLICES:
            n = n_dp * n_mp * BLOCK
            r = jnp.stack([own_first, dpx(own_first, 1)])
            r = jnp.stack([r] + over_z(r))
            grad_first, all_first, all_ppre, grad_b_pool, new_scale = call(
                functools.partial(ranking, n_mp, sents),
                here(ids_row, ids_row.reshape(n, 1), w_pool, vecs)
                + here(jnp.broadcast_to(scale[None], (1, n)))
                + away(r, *over_plane(r)),
                here(tiny_shape, shape((n, width), low), shape((n, width), low))
                + here(shape((1, width), f32), shape((1, n), f32)),
                [vmem((n_dp * n_mp, BLOCK, width), low), vmem((n, width), f32)]
                + [dma((n_dp * n_mp,))],
                6,
            )
            grad_b_pool, new_scale = grad_b_pool[0], new_scale[0, :1]
        else:
            grad_first, grad_pool, grad_b_pool, new_scale = rank_part(
                gather_all(own_first), sents, pair_ids, w_pool, b_pool, scale
            )
        lot = shape((2, 2, 2, n_mp // 2, size, width), low)
        tiny = shape((BLOCK, width), f32)
        grad_z2, small_two, keep_o, send = call(
            functools.partial(out_backward, n_mp),
            here(out_cot, grad_first, hat_two, inv_two, vecs) + away(hidden),
            here(rows_f, tiny) + away(lot, lot),
            [vmem((n_mp, units, width), low), vmem(mid.shape, low)]
            + [dma((SLICES * n_mp,)), dma((n_mp,))],
            10,
        )
        got_o = dpx(send, 1)
        grad_z1, grad_b_in, small_one, keep_i, send = call(
            functools.partial(in_backward, n_mp),
            here(grad_z2, h1, hat_one, inv_one, vecs)
            + away(slope, w_in, w_out, *in_parts, *out_parts),
            here(rows_f, shape((n_mp, 1, units), f32), tiny) + away(lot, lot),
            [
                vmem((n_mp, width, units), low),
                vmem((n_mp, units, width), low),
                vmem(mid.shape, low),
                vmem((n_mp, width, units), low),
                vmem((rows, width), f32),
                dma((2 * nc,)),
                dma((SLICES * n_mp,)),
                dma((n_mp,)),
            ],
            17,
        )
        got_i = dpx(send, 1)
        step_o = reduce_one(keep_o, after(got_o, grad_z1))
        a_o, b_o = dpx(step_o[0], 2), dpx(step_o[1], 4)
        grad_q, grad_k, grad_v, total, grad_wo = call(
            functools.partial(attention_backward, n_mp, cols),
            here(after(grad_z1, step_o[0], step_o[1]), query, key_part, value_part, context)
            + here(grad_b_in, small_one, small_two)
            + away(w_all, p_all),
            here(rows_low, rows_low, rows_low, shape((BLOCK + 2 * n_mp, width), f32))
            + here(shape((n_mp * cols, width), low)),
            [vmem((n_mp * cols, width), low), vmem(p_shape.shape, f32), vmem((rows, width), low)]
            + [dma((1,)), dma((rows // PAIR,))],
            15,
        )
        hops = [functools.partial(mpx, bit=1 << i) for i in range(n_mp.bit_length() - 1)]
        hops += [functools.partial(dpx, bit=1)]
        hops += [functools.partial(dpx, bit=1 << i) for i in range(3, n_dp.bit_length() - 1)]
        hop = hops[0](total)
        step_i = reduce_one(keep_i, after(got_i, grad_q))
        a_i, b_i = dpx(step_i[0], 2), dpx(step_i[1], 4)
        step_o = reduce_two(step_o[2], step_o[3], after(a_o, grad_q), after(b_o, grad_q))
        a2_o, b2_o = dpx(step_o[0], 4), dpx(step_o[1], 2)
        keep_a, send = call(
            functools.partial(attention_weights, n_mp, cols),
            here(after(inputs, step_i[0], step_i[1], step_o[0], step_o[1]))
            + here(grad_q, grad_k, grad_v, grad_wo),
            away(lot, lot),
            [vmem((4, n_mp * cols, width), low), dma((SLICES * n_mp,))],
            7,
        )
        got_a = dpx(send, 1)
        total = total + after(hop, keep_a)
        hop = hops[1](total)
        (input_grad,) = call(
            functools.partial(attention_inputs, n_mp, cols),
            here(grad_z1, after(grad_q, keep_a), grad_k, grad_v) + away(w_all),
            here(rows_f),
            [vmem((3, n_mp * cols, width), low), dma((3,))],
            7,
        )
        step_a = reduce_one(keep_a, after(got_a, input_grad))
        a_a, b_a = dpx(step_a[0], 2), dpx(step_a[1], 4)
        step_o = reduce_three(*step_o[2:], *after([a2_o, b2_o], step_a[0], step_a[1]))
        z_o = [mpx(step_o[i], i) for i in range(1, n_mp)]
        total = total + after(hop, step_a[0])
        hop = hops[2](total)
        step_i = reduce_two(step_i[2], step_i[3], *after([a_i, b_i], step_a[0], step_a[1]))
        a2_i, b2_i = dpx(step_i[0], 4), dpx(step_i[1], 2)
        step_a = reduce_two(step_a[2], step_a[3], *after([a_a, b_a], step_i[0], step_i[1]))
        a2_a, b2_a = dpx(step_a[0], 4), dpx(step_a[1], 2)
        red_out = reduce_last(after([step_o[0]] + z_o, step_a[0]))
        total = total + after(hop, step_i[0])
        for h in hops[3:]:
            total = total + h(total)
        step_i = reduce_three(*step_i[2:], *after([a2_i, b2_i], step_a[0], step_a[1]))
        z_i = [mpx(step_i[i], i) for i in range(1, n_mp)]
        step_a = reduce_three(*step_a[2:], *after([a2_a, b2_a], step_i[0]))
        z_a = [mpx(step_a[i], i) for i in range(1, n_mp)]
        red_in = reduce_last(after([step_i[0]] + z_i, step_a[0]))
        out_own = plane_parts(red_out)
        total = total + dpx(after(total, step_a[0]), 2)
        total = total + dpx(total, 4)
        if n_dp == SLICES:
            grad_pool = tn(after(all_first, step_a[0]), all_ppre)
        take = lax.axis_index("mp")
        out_b_in = lax.dynamic_slice_in_dim(total, BLOCK + take, 1, 0)[0]
        out_b_qv = lax.dynamic_slice_in_dim(total, BLOCK + n_mp + take, 1, 0)
        out_b_qv = out_b_qv[0, : 2 * cols].reshape(2, cols)
        sums = [total[i] for i in range(6)]
        extras = [*sums, out_b_in, out_b_qv, grad_pool, grad_b_pool, new_scale]
        red_att = reduce_last(after([step_a[0]] + z_a, *extras))
        last = jnp.concatenate([red_in, red_att])
        last = [last] + over_plane(last)
        whole = shape((SLICES * size, width), f32)

        (done_out,) = call(functools.partial(finish_rows, 0), here(*out_own), here(whole), [], 3)
        last_own = []
        for part in last:
            last_own += [part, dpx(after(part, done_out), 1)]
        done_in, done_qkv, done_attn = call(
            functools.partial(finish_rows, cols),
            here(*last_own),
            here(whole, shape((3, cols, width), f32), shape((cols, width), f32)),
            [],
            4,
        )
        return (
            layer_out,
            input_grad,
            done_qkv.transpose(0, 2, 1),
            out_b_qv,
            done_attn,
            sums[0],
            sums[1],
            sums[2],
            done_in,
            out_b_in,
            done_out,
            sums[3],
            sums[4],
            sums[5],
            grad_pool,
            grad_b_pool,
            new_scale,
        )

    return on_device


def solution(mesh):
    rows, whole = P(("dp", "mp"), None), P()
    in_specs = (
        rows,
        P(("dp", "mp")),
        rows,
        whole,
        P(None, None, "mp"),
        P(None, "mp"),
        P("mp", None),
        whole,
        whole,
        whole,
        P(None, "mp"),
        P("mp"),
        P("mp", None),
        whole,
        whole,
        whole,
        whole,
        whole,
        whole,
    )
    out_specs = (
        rows,
        rows,
        P(None, None, "mp"),
        P(None, "mp"),
        P("mp", None),
        whole,
        whole,
        whole,
        P(None, "mp"),
        P("mp"),
        P("mp", None),
        whole,
        whole,
        whole,
        whole,
        whole,
        whole,
    )
    return jax.shard_map(
        make(mesh), mesh=mesh, in_specs=in_specs, out_specs=out_specs, check_vma=False
    )
```

```python
import functools

import jax
import jax.numpy as jnp
from jax import lax
from jax.experimental import pallas as pl
from jax.experimental.pallas import tpu as pltpu
from jax.sharding import PartitionSpec as P

HEAD_DIM = 64
SEQ = 64
SLICES = 8
PARTS = 8
PAIR = 2 * SEQ
LANES = 2 * HEAD_DIM
BLOCK = 8

eps_norm = 1e-12
margin = 0.3
step_rate = 1.0
masked_low = -1e30
high = lax.Precision.HIGHEST
f32 = jnp.float32
low = jnp.bfloat16
VMEM_BYTES = 58 << 20


def nn(a, b):
    return jnp.dot(a, b, preferred_element_type=f32)


def nt(a, b):
    return lax.dot_general(a, b, (((1,), (1,)), ((), ())), preferred_element_type=f32)


def tn(a, b):
    return lax.dot_general(a, b, (((0,), (0,)), ((), ())), preferred_element_type=f32)


def rank_terms(cosine, same, diag_mask, weight, scale_value, axis_of):
    shifted = cosine - margin * diag_mask
    logits = jnp.where(same, scale_value * shifted, masked_low)
    top = jnp.max(logits, axis=axis_of, keepdims=True)
    lse = top + jnp.log(jnp.sum(jnp.exp(logits - top), axis=axis_of, keepdims=True))
    probs = jnp.exp(logits - lse)
    grad_logit = weight * (probs - diag_mask)
    return (grad_logit, grad_logit * shifted)


def call(body, ins, outs, scratch, micros):
    def spec(vmem):
        return pl.BlockSpec(memory_space=pltpu.VMEM if vmem else pltpu.HBM)

    return pl.pallas_call(
        body,
        out_shape=[jax.ShapeDtypeStruct(o.shape, o.dtype) for o, _ in outs],
        in_specs=[spec(v) for _, v in ins],
        out_specs=[spec(v) for _, v in outs],
        scratch_shapes=scratch,
        compiler_params=pltpu.CompilerParams(vmem_limit_bytes=VMEM_BYTES),
        cost_estimate=pl.CostEstimate(flops=int(micros * 1.1e9), bytes_accessed=0, transcendentals=0),
    )(*[a for a, _ in ins])


def slot(p):
    me = lax.rem(lax.axis_index("dp"), SLICES)
    return jnp.bitwise_xor(me, p)


def start_all(copies):
    for c in copies:
        c.start()
    return copies


def wait_all(copies):
    for c in copies:
        c.wait()


def att_spot(ref, s, p, cols, size, first=0, rows=None):
    at = slot(p)
    row = pl.multiple_of(s * cols + lax.rem(at, 2) * size + first, 16)
    return ref.at[at // 2, pl.ds(row, rows or size)]


def row_spot(ref, s, p, size, first=0, rows=None):
    return ref.at[s, pl.ds(pl.multiple_of(slot(p) * size + first, 16), rows or size)]


def slices_of(parts):
    full = parts[0].shape[-2]
    return [(part, 2 * (i % 4) + i // 4, 0, full) for i, part in enumerate(parts)]


def fetch_att(own_qkv, own_o, parts, dst, sem, cols):
    copies = []
    for i in range(3):
        copies.append(pltpu.make_async_copy(own_qkv.at[i], dst.at[i, pl.ds(0, cols)], sem.at[i]))
    copies.append(pltpu.make_async_copy(own_o, dst.at[3, pl.ds(0, cols)], sem.at[3]))
    k = 4
    size = parts[0].shape[1]
    for part, p, at, n in slices_of(parts):
        for s in range(part.shape[0]):
            spot = att_spot(dst, s + 1, p, cols, size, at, n)
            copies.append(pltpu.make_async_copy(part.at[s], spot, sem.at[k]))
            k += 1
    return start_all(copies)


def fetch_rows(own, parts, dst, sem, base):
    copies = [[pltpu.make_async_copy(own, dst.at[0], sem.at[base])]]
    k = base + 1
    size = parts[0].shape[1]
    for s in range(parts[0].shape[0]):
        copies.append([])
        for part, p, at, n in slices_of(parts):
            spot = row_spot(dst, s + 1, p, size, at, n)
            copies[-1].append(pltpu.make_async_copy(part.at[s], spot, sem.at[k]))
            k += 1
    return copies


def each_of(src, dst, sem):
    return [pltpu.make_async_copy(src.at[i], dst.at[i], sem.at[i]) for i in range(src.shape[0])]


def fetch_each(src, dst, sem):
    return start_all(each_of(src, dst, sem))


AHEAD = 2


def n_copies(n_mp):
    return 4 + PARTS * (n_mp - 1)


def send_shard(src_of, s, g_keep, g_send, sem, n_mp):
    copies = []
    for p in range(SLICES):
        dst = g_send if p & 1 else g_keep
        spot = dst.at[s // 2, p >> 2, (p >> 1) & 1, s % 2]
        copies.append(pltpu.make_async_copy(src_of(s, p), spot, sem.at[SLICES * s + p]))
    return start_all(copies)


def mean_of(v):
    return jnp.sum(v, axis=-1, keepdims=True) * (1.0 / v.shape[-1])


def norm_rows(z):
    center = z - mean_of(z)
    inv = lax.rsqrt(mean_of(center * center) + eps_norm)
    return center * inv, inv


def norm_back(grad_out, hat, inv, gain):
    scaled = grad_out * gain
    return inv * (scaled - mean_of(scaled) - hat * mean_of(scaled * hat))


def pair_mask(ids_row):
    row = lax.broadcasted_iota(jnp.int32, (PAIR, PAIR), 0) >= SEQ
    col = lax.broadcasted_iota(jnp.int32, (PAIR, PAIR), 1) >= SEQ
    return jnp.logical_and(row == col, ids_row != 0)


def split_heads(v):
    first = lax.broadcasted_iota(jnp.int32, v.shape, 1) < HEAD_DIM
    zero = jnp.zeros_like(v)
    return jnp.concatenate([jnp.where(first, v, zero), jnp.where(first, zero, v)], axis=0)


def join_heads(v):
    half = v.shape[0] // 2
    first = lax.broadcasted_iota(jnp.int32, (half, v.shape[1]), 1) < HEAD_DIM
    return jnp.where(first, v[:half], v[half:])


def softmax_of(scores, mask):
    scores = jnp.where(mask, scores * 0.125, masked_low)
    expd = jnp.exp(scores - jnp.max(scores, axis=-1, keepdims=True))
    return expd / jnp.sum(expd, axis=-1, keepdims=True)


def attention_forward(n_mp, cols, *refs):
    x, ids, small, vecs, own_qkv, own_o = refs[:6]
    parts = refs[6 : 6 + PARTS]
    q, k, v, ctx, hat_out, inv_out, h1, w_all, p_all = refs[14:23]
    w, p_keep, sem, sem2 = refs[23:]
    b_attn, gain, shift = vecs[0:1], vecs[1:2], vecs[2:3]
    copies = fetch_att(own_qkv, own_o, parts, w, sem, cols)
    wait_all(copies)
    sent = start_all([pltpu.make_async_copy(w, w_all, sem2.at[0])])
    rows, width = x.shape
    b_q = jnp.concatenate([small[s : s + 1, :cols] for s in range(n_mp)], axis=1)
    b_v = jnp.concatenate([small[s : s + 1, cols : 2 * cols] for s in range(n_mp)], axis=1)
    q[...] = (nt(x[...], w[0]) + b_q).astype(low)
    k[...] = nt(x[...], w[1]).astype(low)
    v[...] = (nt(x[...], w[2]) + b_v).astype(low)

    for t in range(rows // PAIR):
        at = slice(t * PAIR, (t + 1) * PAIR)
        mask = pair_mask(ids[t])
        for j in range(width // LANES):
            lanes = slice(j * LANES, (j + 1) * LANES)
            raw = nt(q[at, lanes], split_heads(k[at, lanes]))
            probs = [softmax_of(raw[:, i * PAIR : (i + 1) * PAIR], mask) for i in (0, 1)]
            probs = jnp.concatenate(probs, axis=1)
            p_keep[t, j] = probs
            out = nn(probs.astype(low), split_heads(v[at, lanes]))
            ctx[at, lanes] = out.astype(low)

    sent += start_all([pltpu.make_async_copy(p_keep, p_all, sem2.at[1])])
    z = x[...].astype(f32) + nn(ctx[...], w[3]) + b_attn
    hat, inv = norm_rows(z)
    hat_out[...] = hat
    inv_out[...] = jnp.broadcast_to(inv, inv_out.shape)
    h1[...] = (hat * gain + shift).astype(low)
    wait_all(sent)


def gelu_pair(pre):
    size = jnp.abs(pre)
    t = 1.0 / (1.0 + 0.2316418882663604 * size)
    bell = jnp.exp(-0.5 * pre * pre)
    poly = t * (
        0.127414796
        + t * (-0.142248368 + t * (0.7107068705 + t * (-0.7265760135 + t * 0.5307027145)))
    )
    tail = poly * bell
    phi = jnp.where(pre >= 0.0, 1.0 - tail, tail)
    return pre * phi, phi + pre * (bell * 0.3989422804014327)


def ffn_in_forward(n_mp, spot, *refs):
    h1, small, own_in = refs[:3]
    parts = refs[3 : 3 + SLICES]
    hidden, slope, w_in, act_s, slope_s, sem, sem2 = refs[11:]
    copies = fetch_rows(own_in, parts, w_in, sem, 0)
    sent = []
    for s in range(AHEAD):
        start_all(copies[s])
    for s in range(n_mp):
        wait_all(copies[s])
        if s + AHEAD < n_mp:
            start_all(copies[s + AHEAD])
        pre = nn(h1[...], w_in[s]) + small[s : s + 1, spot : spot + w_in.shape[2]]
        act, grad = gelu_pair(pre)
        act_s[s] = act.astype(low)
        slope_s[s] = grad.astype(low)
        sent.append(pltpu.make_async_copy(act_s.at[s], hidden.at[s], sem2.at[2 * s]))
        sent.append(pltpu.make_async_copy(slope_s.at[s], slope.at[s], sem2.at[2 * s + 1]))
        start_all(sent[-2:])
    wait_all(sent)


def ffn_out_forward(n_mp, *refs):
    hat1, vecs, hidden, own_out = refs[:4]
    parts = refs[4 : 4 + SLICES]
    layer_out, hat_out, inv_out, first = refs[12:16]
    w_out, act_s, acc, sem, sem2 = refs[16:]
    gain1, shift1, b_out, gain2, shift2 = [vecs[i : i + 1] for i in range(1, 6)]
    acts = each_of(hidden, act_s, sem2)
    copies = fetch_rows(own_out, parts, w_out, sem, 0)
    copies = [[acts[s]] + copies[s] for s in range(n_mp)]
    for s in range(AHEAD):
        start_all(copies[s])
    acc[...] = hat1[...] * gain1 + shift1 + b_out
    for s in range(n_mp):
        wait_all(copies[s])
        if s + AHEAD < n_mp:
            start_all(copies[s + AHEAD])
        acc[...] += nn(act_s[s], w_out[s])

    hat, inv = norm_rows(acc[...])
    hat_out[...] = hat
    inv_out[...] = jnp.broadcast_to(inv, inv_out.shape)
    out = (hat * gain2 + shift2).astype(low)
    layer_out[...] = out
    rows = [out[i * SEQ : i * SEQ + 1].astype(f32) for i in range(out.shape[0] // SEQ)]
    rows.append(jnp.zeros((BLOCK - len(rows), out.shape[1]), f32))
    first[...] = jnp.concatenate(rows, axis=0).astype(low)


def ranking(n_mp, sents, *refs):
    ids_row, ids_col, w_pool, vecs, scale = refs[:5]
    parts = refs[5:9]
    g_first, rows_out, g_out, g_bias, scale_out = refs[9:14]
    got, g_all, sem = refs[14:]
    me = lax.axis_index("mp")
    copies = []
    for p in range(SLICES):
        for s in range(n_mp):
            spot = got.at[slot(p) * n_mp + jnp.bitwise_xor(me, s)]
            copies.append(
                pltpu.make_async_copy(parts[p >> 1].at[s, p & 1], spot, sem.at[p * n_mp + s])
            )
    wait_all(start_all(copies))
    n = ids_row.shape[1]
    first = got[...].astype(f32).reshape(n, -1).astype(low)
    rows_out[...] = first
    pooled = jnp.tanh(nn(first, w_pool[...]) + vecs[6:7])
    inv_len = lax.rsqrt(jnp.sum(pooled * pooled, axis=-1, keepdims=True) + eps_norm)
    emb = pooled * inv_len
    emb_low = emb.astype(low)
    cosine = nt(emb_low, emb_low)
    row = lax.broadcasted_iota(jnp.int32, (n, n), 0)
    col = lax.broadcasted_iota(jnp.int32, (n, n), 1)
    even = lax.rem(row, 2) == 0
    in_row = jnp.logical_and(even, lax.rem(row, BLOCK) < sents)
    in_col = jnp.logical_and(lax.rem(col, 2) == 1, lax.rem(col, BLOCK) < sents)
    in_both = jnp.logical_and(in_row, in_col)
    same = jnp.logical_and(in_both, ids_col[...] == ids_row[...])
    one = same.astype(f32)
    diag = jnp.logical_and(in_both, col == row + 1).astype(f32)
    shifted = cosine - margin * diag
    logits = jnp.where(same, scale[...] * shifted, masked_low)
    grad = jnp.zeros_like(cosine)
    for axis in (1, 0):
        expd = jnp.exp(logits - jnp.max(logits, axis=axis, keepdims=True))
        expd = jnp.where(same, expd, 0.0)
        total = jnp.maximum(jnp.sum(expd, axis=axis, keepdims=True), 1e-30)
        count = jnp.maximum(jnp.sum(one, axis=axis, keepdims=True), 1.0)
        grad = grad + (expd / total - diag) / count
    scale_grad = jnp.sum(jnp.sum(grad * shifted, axis=1, keepdims=True), axis=0, keepdims=True)
    scale_out[...] = scale[...] - step_rate * jnp.broadcast_to(scale_grad, scale_out.shape)
    both = grad + grad.T
    g_emb = jnp.zeros_like(pooled)
    for _ in range(3):
        part = both.astype(low)
        both = both - part.astype(f32)
        g_emb = g_emb + nn(part, emb_low)
    g_emb = scale[0:1, 0:1] * g_emb
    g_pooled = inv_len * (g_emb - emb * jnp.sum(emb * g_emb, axis=-1, keepdims=True))
    g_pre = (g_pooled * (1.0 - pooled * pooled)).astype(low)
    g_out[...] = g_pre
    g_all[...] = g_pre.astype(f32)
    g_bias[...] = jnp.sum(g_all[...], axis=0, keepdims=True)
    at = (lax.axis_index("dp") * n_mp + me) * BLOCK
    own = g_all[pl.ds(pl.multiple_of(at, BLOCK), BLOCK)].astype(low)
    g_first[...] = nt(own, w_pool[...])


def out_backward(n_mp, *refs):
    cot, g_first, hat, inv, vecs, hidden = refs[:6]
    gain = vecs[4:5]
    g_z2, small, keep, send = refs[6:10]
    g_w, act_s, sem, sem2 = refs[10:]
    acts = fetch_each(hidden, act_s, sem2)
    rows = cot.shape[0]
    g_z2[...] = cot[...].astype(f32)
    for i in range(rows // SEQ):
        g_z2[i * SEQ : i * SEQ + 1] += g_first[i : i + 1]
    g_y = g_z2[...]
    small[...] = jnp.zeros_like(small)
    small[1:2] = jnp.sum(g_y * hat[...], axis=0, keepdims=True)
    small[2:3] = jnp.sum(g_y, axis=0, keepdims=True)
    g_z = norm_back(g_y, hat[...], inv[:, :1], gain)
    g_z2[...] = g_z
    small[0:1] = jnp.sum(g_z, axis=0, keepdims=True)
    g_ffn = g_z.astype(low)

    size = keep.shape[-2]
    sent = []
    for s in range(n_mp):
        acts[s].wait()
        g_w[s] = tn(act_s[s], g_ffn).astype(low)
        sent += send_shard(lambda s, p: row_spot(g_w, s, p, size), s, keep, send, sem, n_mp)
    wait_all(sent)


def in_backward(n_mp, *refs):
    g_z2, h1, hat, inv, vecs, slope, own_in, own_out = refs[:8]
    gain = vecs[1:2]
    in_parts = refs[8 : 8 + SLICES]
    out_parts = refs[16 : 16 + SLICES]
    g_z1, g_mid, small, keep, send = refs[24:29]
    w_in, w_out, slope_s, g_w, acc, sem, sem2, sem3 = refs[29:]
    slopes = each_of(slope, slope_s, sem3)
    out_copies = fetch_rows(own_out, out_parts, w_out, sem, 0)
    in_copies = fetch_rows(own_in, in_parts, w_in, sem, n_copies(n_mp))
    for s in range(AHEAD):
        start_all([slopes[s]] + out_copies[s] + in_copies[s])
    acc[...] = g_z2[...]
    g_ffn = g_z2[...].astype(low)
    size = keep.shape[-2]
    copies = []
    for s in range(n_mp):
        wait_all([slopes[s]] + out_copies[s])
        if s + AHEAD < n_mp:
            start_all([slopes[s + AHEAD]] + out_copies[s + AHEAD] + in_copies[s + AHEAD])
        g_pre = (nt(g_ffn, w_out[s]) * slope_s[s].astype(f32)).astype(low)
        g_mid[s] = jnp.sum(g_pre.astype(f32), axis=0, keepdims=True)
        g_w[s] = tn(h1[...], g_pre).astype(low)
        copies += send_shard(lambda s, p: row_spot(g_w, s, p, size), s, keep, send, sem2, n_mp)
        wait_all(in_copies[s])
        acc[...] += nt(g_pre, w_in[s])
    g_h1 = acc[...]
    small[...] = jnp.zeros_like(small)
    small[1:2] = jnp.sum(g_h1 * hat[...], axis=0, keepdims=True)
    small[2:3] = jnp.sum(g_h1, axis=0, keepdims=True)
    g_z = norm_back(g_h1, hat[...], inv[:, :1], gain)
    g_z1[...] = g_z
    small[0:1] = jnp.sum(g_z, axis=0, keepdims=True)
    wait_all(copies)


def attention_backward(n_mp, cols, *refs):
    g_z1, q, k, v, ctx, g_mid, small_one, small_two, w_all, p_all = refs[:10]
    g_q, g_k, g_v, total, g_wo = refs[10:15]
    w, p_keep, g_ctx, sem, sem2 = refs[15:]
    fetch = start_all([pltpu.make_async_copy(w_all.at[3], w, sem.at[0])])
    probs = fetch_each(p_all, p_keep, sem2)
    rows, width = g_z1.shape
    g_attn = g_z1[...].astype(low)
    wait_all(fetch)
    g_ctx[...] = nt(g_attn, w[...]).astype(low)
    for t in range(rows // PAIR):
        at = slice(t * PAIR, (t + 1) * PAIR)
        probs[t].wait()
        for j in range(width // LANES):
            lanes = slice(j * LANES, (j + 1) * LANES)
            q2, g2 = q[at, lanes], g_ctx[at, lanes]
            k2, v2 = split_heads(k[at, lanes]), split_heads(v[at, lanes])
            p = p_keep[t, j]
            g_p = nt(g2, v2)
            g_raw = []
            for i in (0, 1):
                half = slice(i * PAIR, (i + 1) * PAIR)
                inner = jnp.sum(p[:, half] * g_p[:, half], axis=-1, keepdims=True)
                g_raw.append((p[:, half] * (g_p[:, half] - inner) * 0.125).astype(low))
            g_raw = jnp.concatenate(g_raw, axis=1)
            g_v[at, lanes] = join_heads(tn(p.astype(low), g2)).astype(low)
            g_q[at, lanes] = nn(g_raw, k2).astype(low)
            g_k[at, lanes] = join_heads(tn(g_raw, q2)).astype(low)

    g_wo[...] = tn(ctx[...], g_attn).astype(low)
    total[...] = jnp.zeros_like(total)
    total[0:3] = small_one[0:3]
    total[3:6] = small_two[0:3]
    b_q = jnp.sum(g_q[...].astype(f32), axis=0, keepdims=True)
    b_v = jnp.sum(g_v[...].astype(f32), axis=0, keepdims=True)
    for s in range(n_mp):
        at = jnp.bitwise_xor(lax.axis_index("mp"), s)
        total[pl.ds(BLOCK + at, 1)] = g_mid[s]
        lanes = slice(s * cols, (s + 1) * cols)
        total[pl.ds(BLOCK + n_mp + at, 1), 0:cols] = b_q[:, lanes]
        total[pl.ds(BLOCK + n_mp + at, 1), cols : 2 * cols] = b_v[:, lanes]


def attention_weights(n_mp, cols, *refs):
    x, g_q, g_k, g_v, g_wo, keep, send, g_w, sem = refs
    g_w[3] = g_wo[...]
    g_w[0] = tn(g_q[...], x[...]).astype(low)
    g_w[1] = tn(g_k[...], x[...]).astype(low)
    g_w[2] = tn(g_v[...], x[...]).astype(low)
    size = keep.shape[-2]
    sent = []
    for s in range(n_mp):
        sent += send_shard(lambda s, p: att_spot(g_w, s, p, cols, size), s, keep, send, sem, n_mp)
    wait_all(sent)


def attention_inputs(n_mp, cols, *refs):
    g_z1, g_q, g_k, g_v, w_all, g_x, w, sem = refs
    fetch = start_all([pltpu.make_async_copy(w_all.at[i], w.at[i], sem.at[i]) for i in range(3)])
    total = g_z1[...]
    for i, g in enumerate((g_q, g_k, g_v)):
        fetch[i].wait()
        total = total + nn(g[...], w[i])
    g_x[...] = total


def finish_rows(cols, *refs):
    parts = refs[:SLICES]
    if cols:
        out, out_qkv, out_o = refs[SLICES:]
    else:
        (out,) = refs[SLICES:]
    size = parts[0].shape[0] // (2 if cols else 1)
    for p in range(SLICES):
        at = slot(p)
        out[pl.ds(pl.multiple_of(at * size, 32), size)] = parts[p][0:size].astype(f32)
        if cols:
            rows = pl.ds(pl.multiple_of(lax.rem(at, 2) * size, 32), size)

            @pl.when(at // 2 < 3)
            def _():
                out_qkv[at // 2, rows] = parts[p][size : 2 * size].astype(f32)

            @pl.when(at // 2 == 3)
            def _():
                out_o[rows] = parts[p][size : 2 * size].astype(f32)


def make(mesh):
    n_dp = mesh.shape["dp"]
    n_mp = mesh.shape["mp"]

    def dpx(x, bit):
        return lax.ppermute(x, "dp", [(i, i ^ bit) for i in range(n_dp)])

    def mpx(x, bit):
        return lax.ppermute(x, "mp", [(i, i ^ bit) for i in range(n_mp)])

    def bit_of(axis, bit):
        return (lax.axis_index(axis) & bit) != 0

    def flips(v, axis, bits, dims):
        for bit, dim in zip(bits, dims):
            v = jnp.where(bit_of(axis, bit), jnp.flip(v, dim), v)
        return v

    def plane_parts(r):
        got = [None] * SLICES
        for p in (0, 2, 4, 6):
            got[p] = dpx(r, p) if p else r
        for p in (0, 2, 4, 6):
            got[p + 1] = dpx(got[p], 1)
        return got

    def over_z(piece):
        return [mpx(piece, i) for i in range(1, n_mp)]

    def over_z_slow(own, *deps):
        got = [mpx(own, 1)]
        own = after(own, *deps)
        bit = 2
        while bit < n_mp:
            far = mpx(jnp.stack([own] + got), bit)
            got += [far[i] for i in range(bit)]
            bit *= 2
        return got

    def over_plane(r):
        return [dpx(r, 2), dpx(r, 4), dpx(r, 6)]

    def over_core(parts):
        return parts + [dpx(part, 1) for part in parts]

    def after(x, *deps):
        return lax.optimization_barrier((x, deps))[0]

    def own_piece(shard, place=0):
        rows = shard.shape[0] // SLICES
        at = jnp.bitwise_xor(lax.axis_index("dp") % SLICES, place)
        return lax.dynamic_slice_in_dim(shard, at * rows, rows, 0)

    def add(a, b):
        return (a.astype(f32) + b.astype(f32)).astype(low)

    def reduce_one(keep, got):
        return (
            add(keep[0, :, 1], got[0, :, 1]),
            add(keep[1, 1], got[1, 1]),
            add(keep[0, :, 0], got[0, :, 0]),
            add(keep[1, 0], got[1, 0]),
        )

    def reduce_two(a0, b0, a1, b1):
        return add(a0[1], a1[1]), add(b0[1], b1[1]), a0[0], a1[0], b0[0], b1[0]

    def reduce_three(a0, a1, b0, b1, a2, b2):
        a = a0.astype(f32) + a1.astype(f32) + a2.astype(f32)
        b = b0.astype(f32) + b1.astype(f32) + b2.astype(f32)
        u = [a[0], a[1], b[0], b[1]]
        bit = SLICES
        while bit < n_dp:
            u = [w.astype(low) for w in u]
            u = [w.astype(f32) + dpx(w, bit).astype(f32) for w in u]
            bit *= 2
        return [w.astype(low) for w in u]

    def reduce_last(u):
        total = u[0].astype(f32)
        for w in u[1:]:
            total = total + w.astype(f32)
        return total.astype(low)

    def mp_natural(v):
        bits = [1 << i for i in reversed(range(n_mp.bit_length() - 1))]
        shape = v.shape
        v = v.reshape((2,) * len(bits) + shape[1:])
        return flips(v, "mp", bits, range(len(bits))).reshape(shape)

    def gather_all(own):
        r = jnp.stack([own] + [mpx(own, s) for s in range(1, n_mp)])
        r = mp_natural(r)
        z = jnp.stack([r] + [dpx(r, b) for b in (2, 4, 6)])
        v = jnp.stack([z, dpx(z, 1)], 1).reshape((2, 2, 2) + r.shape)
        v = flips(v, "dp", (4, 2, 1), (0, 1, 2)).reshape((SLICES,) + r.shape)
        bit = SLICES
        while bit < n_dp:
            o = dpx(v, bit)
            up = bit_of("dp", bit)
            v = jnp.concatenate([jnp.where(up, o, v), jnp.where(up, v, o)], 0)
            bit *= 2
        return v.reshape((n_dp * n_mp,) + own.shape)

    def rank_part(first_rows, sents, pair_ids, w_pool, b_pool, scale):
        n_all = n_dp * n_mp
        width = first_rows.shape[-1]
        first_rows = first_rows[:, :sents].reshape(n_all * sents, width).astype(low)
        npairs = n_all * sents // 2
        pooled = jnp.tanh(
            jnp.dot(first_rows, w_pool, preferred_element_type=f32) + b_pool.astype(f32)
        )
        inv_len = lax.rsqrt(jnp.sum(pooled * pooled, axis=-1, keepdims=True) + eps_norm)
        emb_full = pooled * inv_len
        emb_pairs = emb_full.astype(low).reshape(npairs, 2, width)
        all_src, all_tgt = emb_pairs[:, 0, :], emb_pairs[:, 1, :]
        scale_value = scale[0]
        cosine = jnp.einsum("kd,md->km", all_src, all_tgt, preferred_element_type=f32)
        same = pair_ids[:, None] == pair_ids[None, :]
        counts = jnp.sum(same.astype(f32), axis=1)
        index_all = jnp.arange(npairs)
        diag_mask = (index_all[:, None] == index_all[None, :]).astype(f32)
        grad_row, part_row = rank_terms(
            cosine, same, diag_mask, (1.0 / counts)[:, None], scale_value, 1
        )
        grad_col, part_col = rank_terms(
            cosine, same, diag_mask, (1.0 / counts)[None, :], scale_value, 0
        )
        grad_all = grad_row + grad_col
        grad_src = scale_value * jnp.dot(grad_all, all_tgt.astype(f32), precision=high)
        grad_tgt = scale_value * jnp.einsum(
            "km,kd->md", grad_all, all_src.astype(f32), precision=high
        )
        new_scale = scale - step_rate * (jnp.sum(part_row) + jnp.sum(part_col))
        grad_emb = jnp.stack([grad_src, grad_tgt], axis=1).reshape(2 * npairs, width)
        grad_pooled = inv_len * (
            grad_emb - emb_full * jnp.sum(emb_full * grad_emb, axis=-1, keepdims=True)
        )
        grad_ppre = (grad_pooled * (1.0 - pooled * pooled)).astype(low)
        grad_pool = jnp.einsum("sd,se->de", first_rows, grad_ppre, preferred_element_type=f32)
        grad_b_pool = jnp.sum(grad_ppre.astype(f32), axis=0)
        own_ppre = lax.dynamic_slice_in_dim(
            grad_ppre, lax.axis_index(("dp", "mp")) * sents, sents, 0
        )
        grad_first = jnp.einsum("se,de->sd", own_ppre, w_pool, preferred_element_type=f32)
        grad_first = jnp.pad(grad_first, ((0, BLOCK - sents), (0, 0)))
        return grad_first, grad_pool, grad_b_pool, new_scale

    def on_device(
        inputs,
        token_ids,
        out_cot,
        pair_ids,
        w_qkv,
        b_qv,
        w_attn,
        b_attn,
        norm1_gain,
        norm1_bias,
        w_in,
        b_in,
        w_out,
        b_out,
        norm2_gain,
        norm2_bias,
        w_pool,
        b_pool,
        scale,
    ):
        rows, width = inputs.shape
        cols = w_qkv.shape[2]
        units = w_in.shape[1]
        sents = rows // SEQ
        shape = jax.ShapeDtypeStruct
        dma = pltpu.SemaphoreType.DMA
        vmem = pltpu.VMEM

        qkv_t = w_qkv.transpose(0, 2, 1)
        att_shard = jnp.concatenate([qkv_t.reshape(3 * cols, width), w_attn])
        size = att_shard.shape[0] // SLICES
        small = jnp.pad(jnp.concatenate([b_qv.reshape(-1), b_in]), (0, 2 * width - 2 * cols - units))
        small = small.reshape(2, width)
        att_z = over_z(jnp.concatenate([own_piece(att_shard), small]))
        vecs = jnp.stack(
            [b_attn, norm1_gain, norm1_bias, b_out, norm2_gain, norm2_bias, b_pool, b_pool]
        ).astype(f32)
        pieces = own_piece(w_in), own_piece(w_out), own_piece(w_out, 6)
        att_z[0] = after(att_z[0], vecs, *pieces)
        small = jnp.stack([small] + [r[size:] for r in att_z]).reshape(n_mp, -1).astype(f32)
        att_r = jnp.stack([r[:size] for r in att_z])
        in_z = over_z_slow(after(pieces[0], att_r))
        att_near = over_plane(att_r)
        att_parts = over_core([att_r] + att_near)
        in_r = jnp.stack(in_z)
        in_near = over_plane(after(in_r, *att_near))
        out_z = over_z_slow(after(pieces[1], in_z[0]), in_r)
        nc = n_copies(n_mp)
        own_qkv = att_shard[: 3 * cols].reshape(3, cols, width)

        def here(*arrays):
            return [(a, True) for a in arrays]

        def away(*arrays):
            return [(a, False) for a in arrays]

        ids = token_ids.reshape(rows // PAIR, 1, PAIR)

        rows_low, rows_f = shape((rows, width), low), shape((rows, width), f32)
        thin = shape((rows, 128), f32)
        w_shape = shape((4, n_mp * cols, width), low)
        p_shape = shape((rows // PAIR, width // LANES, PAIR, 2 * PAIR), f32)
        query, key_part, value_part, context, hat_one, inv_one, h1, w_all, p_all = call(
            functools.partial(attention_forward, n_mp, cols),
            here(after(inputs, out_z[0]), ids, small, vecs)
            + away(own_qkv, w_attn, *att_parts),
            here(rows_low, rows_low, rows_low, rows_low, rows_f, thin, rows_low)
            + away(w_shape, p_shape),
            [vmem(w_shape.shape, low), vmem(p_shape.shape, f32), dma((nc,)), dma((2,))],
            11,
        )
        out_r = jnp.stack(after(out_z, h1))
        out_far = over_z(after(pieces[2], h1))
        out_near = [dpx(out_r, 2), dpx(out_r, 4)]
        in_parts = over_core(after([in_r] + in_near, h1))
        mid = shape((n_mp, rows, units), low)
        tiny_shape = shape((BLOCK, width), f32)
        ids_row = jnp.repeat(pair_ids.reshape(-1, sents // 2), 2, axis=1)
        ids_row = jnp.pad(ids_row, ((0, 0), (0, BLOCK - sents))).reshape(1, -1)
        hidden, slope = call(
            functools.partial(ffn_in_forward, n_mp, 2 * cols),
            here(h1, small) + away(w_in, *in_parts),
            away(mid, mid),
            [vmem((n_mp, width, units), low), vmem(mid.shape, low), vmem(mid.shape, low)]
            + [dma((nc,)), dma((2 * n_mp,))],
            9,
        )
        out_near += [jnp.stack(after(out_far, hidden))]
        out_parts = over_core(after([out_r] + out_near, hidden))
        layer_out, hat_two, inv_two, own_first = call(
            functools.partial(ffn_out_forward, n_mp),
            here(hat_one, vecs)
            + away(hidden, w_out, *out_parts),
            here(rows_low, rows_f, thin, shape((BLOCK, width), low)),
            [vmem((n_mp, units, width), low), vmem(mid.shape, low), vmem((rows, width), f32)]
            + [dma((nc,)), dma((n_mp,))],
            6,
        )
        if n_dp == SLICES:
            n = n_dp * n_mp * BLOCK
            r = jnp.stack([own_first, dpx(own_first, 1)])
            r = jnp.stack([r] + over_z(r))
            grad_first, all_first, all_ppre, grad_b_pool, new_scale = call(
                functools.partial(ranking, n_mp, sents),
                here(ids_row, ids_row.reshape(n, 1), w_pool, vecs)
                + here(jnp.broadcast_to(scale[None], (1, n)))
                + away(r, *over_plane(r)),
                here(tiny_shape, shape((n, width), low), shape((n, width), low))
                + here(shape((1, width), f32), shape((1, n), f32)),
                [vmem((n_dp * n_mp, BLOCK, width), low), vmem((n, width), f32)]
                + [dma((n_dp * n_mp,))],
                6,
            )
            grad_b_pool, new_scale = grad_b_pool[0], new_scale[0, :1]
        else:
            grad_first, grad_pool, grad_b_pool, new_scale = rank_part(
                gather_all(own_first), sents, pair_ids, w_pool, b_pool, scale
            )
        lot = shape((2, 2, 2, n_mp // 2, size, width), low)
        tiny = shape((BLOCK, width), f32)
        grad_z2, small_two, keep_o, send = call(
            functools.partial(out_backward, n_mp),
            here(out_cot, grad_first, hat_two, inv_two, vecs) + away(hidden),
            here(rows_f, tiny) + away(lot, lot),
            [vmem((n_mp, units, width), low), vmem(mid.shape, low)]
            + [dma((SLICES * n_mp,)), dma((n_mp,))],
            10,
        )
        got_o = dpx(send, 1)
        grad_z1, grad_b_in, small_one, keep_i, send = call(
            functools.partial(in_backward, n_mp),
            here(grad_z2, h1, hat_one, inv_one, vecs)
            + away(slope, w_in, w_out, *in_parts, *out_parts),
            here(rows_f, shape((n_mp, 1, units), f32), tiny) + away(lot, lot),
            [
                vmem((n_mp, width, units), low),
                vmem((n_mp, units, width), low),
                vmem(mid.shape, low),
                vmem((n_mp, width, units), low),
                vmem((rows, width), f32),
                dma((2 * nc,)),
                dma((SLICES * n_mp,)),
                dma((n_mp,)),
            ],
            17,
        )
        got_i = dpx(send, 1)
        step_o = reduce_one(keep_o, after(got_o, grad_z1))
        a_o, b_o = dpx(step_o[0], 2), dpx(step_o[1], 4)
        grad_q, grad_k, grad_v, total, grad_wo = call(
            functools.partial(attention_backward, n_mp, cols),
            here(after(grad_z1, step_o[0], step_o[1]), query, key_part, value_part, context)
            + here(grad_b_in, small_one, small_two)
            + away(w_all, p_all),
            here(rows_low, rows_low, rows_low, shape((BLOCK + 2 * n_mp, width), f32))
            + here(shape((n_mp * cols, width), low)),
            [vmem((n_mp * cols, width), low), vmem(p_shape.shape, f32), vmem((rows, width), low)]
            + [dma((1,)), dma((rows // PAIR,))],
            15,
        )
        hops = [functools.partial(mpx, bit=1 << i) for i in range(n_mp.bit_length() - 1)]
        hops += [functools.partial(dpx, bit=1)]
        hops += [functools.partial(dpx, bit=1 << i) for i in range(3, n_dp.bit_length() - 1)]
        hop = hops[0](total)
        step_i = reduce_one(keep_i, after(got_i, grad_q))
        a_i, b_i = dpx(step_i[0], 2), dpx(step_i[1], 4)
        step_o = reduce_two(step_o[2], step_o[3], after(a_o, grad_q), after(b_o, grad_q))
        a2_o, b2_o = dpx(step_o[0], 4), dpx(step_o[1], 2)
        keep_a, send = call(
            functools.partial(attention_weights, n_mp, cols),
            here(after(inputs, step_i[0], step_i[1], step_o[0], step_o[1]))
            + here(grad_q, grad_k, grad_v, grad_wo),
            away(lot, lot),
            [vmem((4, n_mp * cols, width), low), dma((SLICES * n_mp,))],
            7,
        )
        got_a = dpx(send, 1)
        total = total + after(hop, keep_a)
        hop = hops[1](total)
        (input_grad,) = call(
            functools.partial(attention_inputs, n_mp, cols),
            here(grad_z1, after(grad_q, keep_a), grad_k, grad_v) + away(w_all),
            here(rows_f),
            [vmem((3, n_mp * cols, width), low), dma((3,))],
            7,
        )
        step_a = reduce_one(keep_a, after(got_a, input_grad))
        a_a, b_a = dpx(step_a[0], 2), dpx(step_a[1], 4)
        step_o = reduce_three(*step_o[2:], *after([a2_o, b2_o], step_a[0], step_a[1]))
        z_o = [mpx(step_o[i], i) for i in range(1, n_mp)]
        total = total + after(hop, step_a[0])
        hop = hops[2](total)
        step_i = reduce_two(step_i[2], step_i[3], *after([a_i, b_i], step_a[0], step_a[1]))
        a2_i, b2_i = dpx(step_i[0], 4), dpx(step_i[1], 2)
        step_a = reduce_two(step_a[2], step_a[3], *after([a_a, b_a], step_i[0], step_i[1]))
        a2_a, b2_a = dpx(step_a[0], 4), dpx(step_a[1], 2)
        red_out = reduce_last(after([step_o[0]] + z_o, step_a[0]))
        total = total + after(hop, step_i[0])
        for h in hops[3:]:
            total = total + h(total)
        step_i = reduce_three(*step_i[2:], *after([a2_i, b2_i], step_a[0], step_a[1]))
        z_i = [mpx(step_i[i], i) for i in range(1, n_mp)]
        step_a = reduce_three(*step_a[2:], *after([a2_a, b2_a], step_i[0]))
        z_a = [mpx(step_a[i], i) for i in range(1, n_mp)]
        red_in = reduce_last(after([step_i[0]] + z_i, step_a[0]))
        out_own = plane_parts(red_out)
        total = total + dpx(after(total, step_a[0]), 2)
        total = total + dpx(total, 4)
        if n_dp == SLICES:
            grad_pool = tn(after(all_first, step_a[0]), all_ppre)
        take = lax.axis_index("mp")
        out_b_in = lax.dynamic_slice_in_dim(total, BLOCK + take, 1, 0)[0]
        out_b_qv = lax.dynamic_slice_in_dim(total, BLOCK + n_mp + take, 1, 0)
        out_b_qv = out_b_qv[0, : 2 * cols].reshape(2, cols)
        sums = [total[i] for i in range(6)]
        extras = [*sums, out_b_in, out_b_qv, grad_pool, grad_b_pool, new_scale]
        red_att = reduce_last(after([step_a[0]] + z_a, *extras))
        last = jnp.concatenate([red_in, red_att])
        last = [last] + over_plane(last)
        whole = shape((SLICES * size, width), f32)

        (done_out,) = call(functools.partial(finish_rows, 0), here(*out_own), here(whole), [], 3)
        last_own = []
        for part in last:
            last_own += [part, dpx(after(part, done_out), 1)]
        done_in, done_qkv, done_attn = call(
            functools.partial(finish_rows, cols),
            here(*last_own),
            here(whole, shape((3, cols, width), f32), shape((cols, width), f32)),
            [],
            4,
        )
        return (
            layer_out,
            input_grad,
            done_qkv.transpose(0, 2, 1),
            out_b_qv,
            done_attn,
            sums[0],
            sums[1],
            sums[2],
            done_in,
            out_b_in,
            done_out,
            sums[3],
            sums[4],
            sums[5],
            grad_pool,
            grad_b_pool,
            new_scale,
        )

    return on_device


def solution(mesh):
    rows, whole = P(("dp", "mp"), None), P()
    in_specs = (
        rows,
        P(("dp", "mp")),
        rows,
        whole,
        P(None, None, "mp"),
        P(None, "mp"),
        P("mp", None),
        whole,
        whole,
        whole,
        P(None, "mp"),
        P("mp"),
        P("mp", None),
        whole,
        whole,
        whole,
        whole,
        whole,
        whole,
    )
    out_specs = (
        rows,
        rows,
        P(None, None, "mp"),
        P(None, "mp"),
        P("mp", None),
        whole,
        whole,
        whole,
        P(None, "mp"),
        P("mp"),
        P("mp", None),
        whole,
        whole,
        whole,
        whole,
        whole,
        whole,
    )
    return jax.shard_map(
        make(mesh), mesh=mesh, in_specs=in_specs, out_specs=out_specs, check_vma=False
    )
```

```python
import functools

import jax
import jax.numpy as jnp
from jax import lax
from jax.experimental import pallas as pl
from jax.experimental.pallas import tpu as pltpu
from jax.sharding import PartitionSpec as P

HEAD_DIM = 64
SEQ = 64
SLICES = 8
PARTS = 8
PAIR = 2 * SEQ
LANES = 2 * HEAD_DIM
BLOCK = 8

eps_norm = 1e-12
margin = 0.3
step_rate = 1.0
masked_low = -1e30
high = lax.Precision.HIGHEST
f32 = jnp.float32
low = jnp.bfloat16
VMEM_BYTES = 58 << 20


def nn(a, b):
    return jnp.dot(a, b, preferred_element_type=f32)


def nt(a, b):
    return lax.dot_general(a, b, (((1,), (1,)), ((), ())), preferred_element_type=f32)


def tn(a, b):
    return lax.dot_general(a, b, (((0,), (0,)), ((), ())), preferred_element_type=f32)


def rank_terms(cosine, same, diag_mask, weight, scale_value, axis_of):
    shifted = cosine - margin * diag_mask
    logits = jnp.where(same, scale_value * shifted, masked_low)
    top = jnp.max(logits, axis=axis_of, keepdims=True)
    lse = top + jnp.log(jnp.sum(jnp.exp(logits - top), axis=axis_of, keepdims=True))
    probs = jnp.exp(logits - lse)
    grad_logit = weight * (probs - diag_mask)
    return (grad_logit, grad_logit * shifted)


def call(body, ins, outs, scratch, micros):
    def spec(vmem):
        return pl.BlockSpec(memory_space=pltpu.VMEM if vmem else pltpu.HBM)

    return pl.pallas_call(
        body,
        out_shape=[jax.ShapeDtypeStruct(o.shape, o.dtype) for o, _ in outs],
        in_specs=[spec(v) for _, v in ins],
        out_specs=[spec(v) for _, v in outs],
        scratch_shapes=scratch,
        compiler_params=pltpu.CompilerParams(vmem_limit_bytes=VMEM_BYTES),
        cost_estimate=pl.CostEstimate(flops=int(micros * 1.1e9), bytes_accessed=0, transcendentals=0),
    )(*[a for a, _ in ins])


def slot(p):
    me = lax.rem(lax.axis_index("dp"), SLICES)
    return jnp.bitwise_xor(me, p)


def start_all(copies):
    for c in copies:
        c.start()
    return copies


def wait_all(copies):
    for c in copies:
        c.wait()


def att_spot(ref, s, p, cols, size, first=0, rows=None):
    at = slot(p)
    row = pl.multiple_of(s * cols + lax.rem(at, 2) * size + first, 16)
    return ref.at[at // 2, pl.ds(row, rows or size)]


def row_spot(ref, s, p, size, first=0, rows=None):
    return ref.at[s, pl.ds(pl.multiple_of(slot(p) * size + first, 16), rows or size)]


def slices_of(parts):
    full = parts[0].shape[-2]
    return [(part, 2 * (i % 4) + i // 4, 0, full) for i, part in enumerate(parts)]


def fetch_att(own_qkv, own_o, parts, dst, sem, cols):
    copies = []
    for i in range(3):
        copies.append(pltpu.make_async_copy(own_qkv.at[i], dst.at[i, pl.ds(0, cols)], sem.at[i]))
    copies.append(pltpu.make_async_copy(own_o, dst.at[3, pl.ds(0, cols)], sem.at[3]))
    k = 4
    size = parts[0].shape[1]
    for part, p, at, n in slices_of(parts):
        for s in range(part.shape[0]):
            spot = att_spot(dst, s + 1, p, cols, size, at, n)
            copies.append(pltpu.make_async_copy(part.at[s], spot, sem.at[k]))
            k += 1
    return start_all(copies)


def fetch_rows(own, parts, dst, sem, base):
    copies = [[pltpu.make_async_copy(own, dst.at[0], sem.at[base])]]
    k = base + 1
    size = parts[0].shape[1]
    for s in range(parts[0].shape[0]):
        copies.append([])
        for part, p, at, n in slices_of(parts):
            spot = row_spot(dst, s + 1, p, size, at, n)
            copies[-1].append(pltpu.make_async_copy(part.at[s], spot, sem.at[k]))
            k += 1
    return copies


def each_of(src, dst, sem):
    return [pltpu.make_async_copy(src.at[i], dst.at[i], sem.at[i]) for i in range(src.shape[0])]


def fetch_each(src, dst, sem):
    return start_all(each_of(src, dst, sem))


AHEAD = 2


def n_copies(n_mp):
    return 4 + PARTS * (n_mp - 1)


def send_shard(src_of, s, g_keep, g_send, sem, n_mp):
    copies = []
    for p in range(SLICES):
        dst = g_send if p & 1 else g_keep
        spot = dst.at[s // 2, p >> 2, (p >> 1) & 1, s % 2]
        copies.append(pltpu.make_async_copy(src_of(s, p), spot, sem.at[SLICES * s + p]))
    return start_all(copies)


def mean_of(v):
    return jnp.sum(v, axis=-1, keepdims=True) * (1.0 / v.shape[-1])


def norm_rows(z):
    center = z - mean_of(z)
    inv = lax.rsqrt(mean_of(center * center) + eps_norm)
    return center * inv, inv


def norm_back(grad_out, hat, inv, gain):
    scaled = grad_out * gain
    return inv * (scaled - mean_of(scaled) - hat * mean_of(scaled * hat))


def pair_mask(ids_row):
    row = lax.broadcasted_iota(jnp.int32, (PAIR, PAIR), 0) >= SEQ
    col = lax.broadcasted_iota(jnp.int32, (PAIR, PAIR), 1) >= SEQ
    return jnp.logical_and(row == col, ids_row != 0)


def split_heads(v):
    first = lax.broadcasted_iota(jnp.int32, v.shape, 1) < HEAD_DIM
    zero = jnp.zeros_like(v)
    return jnp.concatenate([jnp.where(first, v, zero), jnp.where(first, zero, v)], axis=0)


def join_heads(v):
    half = v.shape[0] // 2
    first = lax.broadcasted_iota(jnp.int32, (half, v.shape[1]), 1) < HEAD_DIM
    return jnp.where(first, v[:half], v[half:])


def softmax_of(scores, mask):
    scores = jnp.where(mask, scores * 0.125, masked_low)
    expd = jnp.exp(scores - jnp.max(scores, axis=-1, keepdims=True))
    return expd / jnp.sum(expd, axis=-1, keepdims=True)


def attention_forward(n_mp, cols, *refs):
    x, ids, small, vecs, own_qkv, own_o = refs[:6]
    parts = refs[6 : 6 + PARTS]
    q, k, v, ctx, hat_out, inv_out, h1, w_all, p_all = refs[14:23]
    w, p_keep, sem, sem2 = refs[23:]
    b_attn, gain, shift = vecs[0:1], vecs[1:2], vecs[2:3]
    copies = fetch_att(own_qkv, own_o, parts, w, sem, cols)
    wait_all(copies)
    sent = start_all([pltpu.make_async_copy(w, w_all, sem2.at[0])])
    rows, width = x.shape
    b_q = jnp.concatenate([small[s : s + 1, :cols] for s in range(n_mp)], axis=1)
    b_v = jnp.concatenate([small[s : s + 1, cols : 2 * cols] for s in range(n_mp)], axis=1)
    q[...] = (nt(x[...], w[0]) + b_q).astype(low)
    k[...] = nt(x[...], w[1]).astype(low)
    v[...] = (nt(x[...], w[2]) + b_v).astype(low)

    for t in range(rows // PAIR):
        at = slice(t * PAIR, (t + 1) * PAIR)
        mask = pair_mask(ids[t])
        for j in range(width // LANES):
            lanes = slice(j * LANES, (j + 1) * LANES)
            raw = nt(q[at, lanes], split_heads(k[at, lanes]))
            probs = [softmax_of(raw[:, i * PAIR : (i + 1) * PAIR], mask) for i in (0, 1)]
            probs = jnp.concatenate(probs, axis=1)
            p_keep[t, j] = probs
            out = nn(probs.astype(low), split_heads(v[at, lanes]))
            ctx[at, lanes] = out.astype(low)

    sent += start_all([pltpu.make_async_copy(p_keep, p_all, sem2.at[1])])
    z = x[...].astype(f32) + nn(ctx[...], w[3]) + b_attn
    hat, inv = norm_rows(z)
    hat_out[...] = hat
    inv_out[...] = jnp.broadcast_to(inv, inv_out.shape)
    h1[...] = (hat * gain + shift).astype(low)
    wait_all(sent)


def gelu_pair(pre):
    size = jnp.abs(pre)
    t = 1.0 / (1.0 + 0.2316418882663604 * size)
    bell = jnp.exp(-0.5 * pre * pre)
    poly = t * (
        0.127414796
        + t * (-0.142248368 + t * (0.7107068705 + t * (-0.7265760135 + t * 0.5307027145)))
    )
    tail = poly * bell
    phi = jnp.where(pre >= 0.0, 1.0 - tail, tail)
    return pre * phi, phi + pre * (bell * 0.3989422804014327)


def ffn_in_forward(n_mp, spot, *refs):
    h1, small, own_in = refs[:3]
    parts = refs[3 : 3 + SLICES]
    hidden, slope, w_in, act_s, slope_s, sem, sem2 = refs[11:]
    copies = fetch_rows(own_in, parts, w_in, sem, 0)
    sent = []
    for s in range(AHEAD):
        start_all(copies[s])
    for s in range(n_mp):
        wait_all(copies[s])
        if s + AHEAD < n_mp:
            start_all(copies[s + AHEAD])
        pre = nn(h1[...], w_in[s]) + small[s : s + 1, spot : spot + w_in.shape[2]]
        act, grad = gelu_pair(pre)
        act_s[s] = act.astype(low)
        slope_s[s] = grad.astype(low)
        sent.append(pltpu.make_async_copy(act_s.at[s], hidden.at[s], sem2.at[2 * s]))
        sent.append(pltpu.make_async_copy(slope_s.at[s], slope.at[s], sem2.at[2 * s + 1]))
        start_all(sent[-2:])
    wait_all(sent)


def ffn_out_forward(n_mp, *refs):
    hat1, vecs, hidden, own_out = refs[:4]
    parts = refs[4 : 4 + SLICES]
    layer_out, hat_out, inv_out, first = refs[12:16]
    w_out, act_s, acc, sem, sem2 = refs[16:]
    gain1, shift1, b_out, gain2, shift2 = [vecs[i : i + 1] for i in range(1, 6)]
    acts = each_of(hidden, act_s, sem2)
    copies = fetch_rows(own_out, parts, w_out, sem, 0)
    copies = [[acts[s]] + copies[s] for s in range(n_mp)]
    for s in range(AHEAD):
        start_all(copies[s])
    acc[...] = hat1[...] * gain1 + shift1 + b_out
    for s in range(n_mp):
        wait_all(copies[s])
        if s + AHEAD < n_mp:
            start_all(copies[s + AHEAD])
        acc[...] += nn(act_s[s], w_out[s])

    hat, inv = norm_rows(acc[...])
    hat_out[...] = hat
    inv_out[...] = jnp.broadcast_to(inv, inv_out.shape)
    out = (hat * gain2 + shift2).astype(low)
    layer_out[...] = out
    rows = [out[i * SEQ : i * SEQ + 1].astype(f32) for i in range(out.shape[0] // SEQ)]
    rows.append(jnp.zeros((BLOCK - len(rows), out.shape[1]), f32))
    first[...] = jnp.concatenate(rows, axis=0).astype(low)


def ranking(n_mp, sents, *refs):
    ids_row, ids_col, w_pool, vecs, scale = refs[:5]
    parts = refs[5:9]
    g_first, rows_out, g_out, g_bias, scale_out = refs[9:14]
    got, g_all, sem = refs[14:]
    me = lax.axis_index("mp")
    copies = []
    for p in range(SLICES):
        for s in range(n_mp):
            spot = got.at[slot(p) * n_mp + jnp.bitwise_xor(me, s)]
            copies.append(
                pltpu.make_async_copy(parts[p >> 1].at[s, p & 1], spot, sem.at[p * n_mp + s])
            )
    wait_all(start_all(copies))
    n = ids_row.shape[1]
    first = got[...].astype(f32).reshape(n, -1).astype(low)
    rows_out[...] = first
    pooled = jnp.tanh(nn(first, w_pool[...]) + vecs[6:7])
    inv_len = lax.rsqrt(jnp.sum(pooled * pooled, axis=-1, keepdims=True) + eps_norm)
    emb = pooled * inv_len
    emb_low = emb.astype(low)
    cosine = nt(emb_low, emb_low)
    row = lax.broadcasted_iota(jnp.int32, (n, n), 0)
    col = lax.broadcasted_iota(jnp.int32, (n, n), 1)
    even = lax.rem(row, 2) == 0
    in_row = jnp.logical_and(even, lax.rem(row, BLOCK) < sents)
    in_col = jnp.logical_and(lax.rem(col, 2) == 1, lax.rem(col, BLOCK) < sents)
    in_both = jnp.logical_and(in_row, in_col)
    same = jnp.logical_and(in_both, ids_col[...] == ids_row[...])
    one = same.astype(f32)
    diag = jnp.logical_and(in_both, col == row + 1).astype(f32)
    shifted = cosine - margin * diag
    logits = jnp.where(same, scale[...] * shifted, masked_low)
    grad = jnp.zeros_like(cosine)
    for axis in (1, 0):
        expd = jnp.exp(logits - jnp.max(logits, axis=axis, keepdims=True))
        expd = jnp.where(same, expd, 0.0)
        total = jnp.maximum(jnp.sum(expd, axis=axis, keepdims=True), 1e-30)
        count = jnp.maximum(jnp.sum(one, axis=axis, keepdims=True), 1.0)
        grad = grad + (expd / total - diag) / count
    scale_grad = jnp.sum(jnp.sum(grad * shifted, axis=1, keepdims=True), axis=0, keepdims=True)
    scale_out[...] = scale[...] - step_rate * jnp.broadcast_to(scale_grad, scale_out.shape)
    both = grad + grad.T
    g_emb = jnp.zeros_like(pooled)
    for _ in range(3):
        part = both.astype(low)
        both = both - part.astype(f32)
        g_emb = g_emb + nn(part, emb_low)
    g_emb = scale[0:1, 0:1] * g_emb
    g_pooled = inv_len * (g_emb - emb * jnp.sum(emb * g_emb, axis=-1, keepdims=True))
    g_pre = (g_pooled * (1.0 - pooled * pooled)).astype(low)
    g_out[...] = g_pre
    g_all[...] = g_pre.astype(f32)
    g_bias[...] = jnp.sum(g_all[...], axis=0, keepdims=True)
    at = (lax.axis_index("dp") * n_mp + me) * BLOCK
    own = g_all[pl.ds(pl.multiple_of(at, BLOCK), BLOCK)].astype(low)
    g_first[...] = nt(own, w_pool[...])


def ranking_out(n_mp, sents, *refs):
    cot, hat, inv, hidden = refs[9:13]
    rank_outs, outs = refs[13:17], refs[17:21]
    got, g_all, sem, g_first, cot_s, hat_s, inv_s, g_w, act_s, sem2, sem3, sem4 = refs[21:]
    pairs = ((cot, cot_s), (hat, hat_s), (inv, inv_s))
    copies = [pltpu.make_async_copy(a, b, sem4.at[i]) for i, (a, b) in enumerate(pairs)]
    start_all(copies)
    acts = fetch_each(hidden, act_s, sem3)
    ranking(n_mp, sents, *refs[:9], g_first, *rank_outs, got, g_all, sem)
    wait_all(copies)
    ins = (cot_s, g_first, hat_s, inv_s, refs[3], hidden)
    out_backward(n_mp, *ins, *outs, g_w, act_s, sem2, sem3, acts=acts)


def out_backward(n_mp, *refs, acts=None):
    cot, g_first, hat, inv, vecs, hidden = refs[:6]
    gain = vecs[4:5]
    g_z2, small, keep, send = refs[6:10]
    g_w, act_s, sem, sem2 = refs[10:]
    acts = acts or fetch_each(hidden, act_s, sem2)
    rows = cot.shape[0]
    g_z2[...] = cot[...].astype(f32)
    for i in range(rows // SEQ):
        g_z2[i * SEQ : i * SEQ + 1] += g_first[i : i + 1]
    g_y = g_z2[...]
    small[...] = jnp.zeros_like(small)
    small[1:2] = jnp.sum(g_y * hat[...], axis=0, keepdims=True)
    small[2:3] = jnp.sum(g_y, axis=0, keepdims=True)
    g_z = norm_back(g_y, hat[...], inv[:, :1], gain)
    g_z2[...] = g_z
    small[0:1] = jnp.sum(g_z, axis=0, keepdims=True)
    g_ffn = g_z.astype(low)

    size = keep.shape[-2]
    sent = []
    for s in range(n_mp):
        acts[s].wait()
        g_w[s] = tn(act_s[s], g_ffn).astype(low)
        sent += send_shard(lambda s, p: row_spot(g_w, s, p, size), s, keep, send, sem, n_mp)
    wait_all(sent)


def in_backward(n_mp, *refs):
    g_z2, h1, hat, inv, vecs, slope, own_in, own_out = refs[:8]
    gain = vecs[1:2]
    in_parts = refs[8 : 8 + SLICES]
    out_parts = refs[16 : 16 + SLICES]
    g_z1, g_mid, small, keep, send = refs[24:29]
    w_in, w_out, slope_s, g_w, acc, sem, sem2, sem3 = refs[29:]
    slopes = each_of(slope, slope_s, sem3)
    out_copies = fetch_rows(own_out, out_parts, w_out, sem, 0)
    in_copies = fetch_rows(own_in, in_parts, w_in, sem, n_copies(n_mp))
    for s in range(AHEAD):
        start_all([slopes[s]] + out_copies[s] + in_copies[s])
    acc[...] = g_z2[...]
    g_ffn = g_z2[...].astype(low)
    size = keep.shape[-2]
    copies = []
    for s in range(n_mp):
        wait_all([slopes[s]] + out_copies[s])
        if s + AHEAD < n_mp:
            start_all([slopes[s + AHEAD]] + out_copies[s + AHEAD] + in_copies[s + AHEAD])
        g_pre = (nt(g_ffn, w_out[s]) * slope_s[s].astype(f32)).astype(low)
        g_mid[s] = jnp.sum(g_pre.astype(f32), axis=0, keepdims=True)
        g_w[s] = tn(h1[...], g_pre).astype(low)
        copies += send_shard(lambda s, p: row_spot(g_w, s, p, size), s, keep, send, sem2, n_mp)
        wait_all(in_copies[s])
        acc[...] += nt(g_pre, w_in[s])
    g_h1 = acc[...]
    small[...] = jnp.zeros_like(small)
    small[1:2] = jnp.sum(g_h1 * hat[...], axis=0, keepdims=True)
    small[2:3] = jnp.sum(g_h1, axis=0, keepdims=True)
    g_z = norm_back(g_h1, hat[...], inv[:, :1], gain)
    g_z1[...] = g_z
    small[0:1] = jnp.sum(g_z, axis=0, keepdims=True)
    wait_all(copies)


def attention_backward(n_mp, cols, *refs):
    g_z1, q, k, v, ctx, g_mid, small_one, small_two, w_all, p_all = refs[:10]
    g_q, g_k, g_v, total, g_wo = refs[10:15]
    w, p_keep, g_ctx, sem, sem2 = refs[15:]
    fetch = start_all([pltpu.make_async_copy(w_all.at[3], w, sem.at[0])])
    probs = fetch_each(p_all, p_keep, sem2)
    rows, width = g_z1.shape
    g_attn = g_z1[...].astype(low)
    wait_all(fetch)
    g_ctx[...] = nt(g_attn, w[...]).astype(low)
    for t in range(rows // PAIR):
        at = slice(t * PAIR, (t + 1) * PAIR)
        probs[t].wait()
        for j in range(width // LANES):
            lanes = slice(j * LANES, (j + 1) * LANES)
            q2, g2 = q[at, lanes], g_ctx[at, lanes]
            k2, v2 = split_heads(k[at, lanes]), split_heads(v[at, lanes])
            p = p_keep[t, j]
            g_p = nt(g2, v2)
            g_raw = []
            for i in (0, 1):
                half = slice(i * PAIR, (i + 1) * PAIR)
                inner = jnp.sum(p[:, half] * g_p[:, half], axis=-1, keepdims=True)
                g_raw.append((p[:, half] * (g_p[:, half] - inner) * 0.125).astype(low))
            g_raw = jnp.concatenate(g_raw, axis=1)
            g_v[at, lanes] = join_heads(tn(p.astype(low), g2)).astype(low)
            g_q[at, lanes] = nn(g_raw, k2).astype(low)
            g_k[at, lanes] = join_heads(tn(g_raw, q2)).astype(low)

    g_wo[...] = tn(ctx[...], g_attn).astype(low)
    total[...] = jnp.zeros_like(total)
    total[0:3] = small_one[0:3]
    total[3:6] = small_two[0:3]
    b_q = jnp.sum(g_q[...].astype(f32), axis=0, keepdims=True)
    b_v = jnp.sum(g_v[...].astype(f32), axis=0, keepdims=True)
    for s in range(n_mp):
        at = jnp.bitwise_xor(lax.axis_index("mp"), s)
        total[pl.ds(BLOCK + at, 1)] = g_mid[s]
        lanes = slice(s * cols, (s + 1) * cols)
        total[pl.ds(BLOCK + n_mp + at, 1), 0:cols] = b_q[:, lanes]
        total[pl.ds(BLOCK + n_mp + at, 1), cols : 2 * cols] = b_v[:, lanes]


def attention_weights(n_mp, cols, *refs):
    x, g_q, g_k, g_v, g_wo, keep, send, g_w, sem = refs
    g_w[3] = g_wo[...]
    g_w[0] = tn(g_q[...], x[...]).astype(low)
    g_w[1] = tn(g_k[...], x[...]).astype(low)
    g_w[2] = tn(g_v[...], x[...]).astype(low)
    size = keep.shape[-2]
    sent = []
    for s in range(n_mp):
        sent += send_shard(lambda s, p: att_spot(g_w, s, p, cols, size), s, keep, send, sem, n_mp)
    wait_all(sent)


def attention_inputs(n_mp, cols, *refs):
    g_z1, g_q, g_k, g_v, w_all, g_x, w, sem = refs
    fetch = start_all([pltpu.make_async_copy(w_all.at[i], w.at[i], sem.at[i]) for i in range(3)])
    total = g_z1[...]
    for i, g in enumerate((g_q, g_k, g_v)):
        fetch[i].wait()
        total = total + nn(g[...], w[i])
    g_x[...] = total


def finish_rows(cols, *refs):
    parts = refs[:SLICES]
    if cols:
        out, out_qkv, out_o = refs[SLICES:]
    else:
        (out,) = refs[SLICES:]
    size = parts[0].shape[0] // (2 if cols else 1)
    for p in range(SLICES):
        at = slot(p)
        out[pl.ds(pl.multiple_of(at * size, 32), size)] = parts[p][0:size].astype(f32)
        if cols:
            rows = pl.ds(pl.multiple_of(lax.rem(at, 2) * size, 32), size)

            @pl.when(at // 2 < 3)
            def _():
                out_qkv[at // 2, rows] = parts[p][size : 2 * size].astype(f32)

            @pl.when(at // 2 == 3)
            def _():
                out_o[rows] = parts[p][size : 2 * size].astype(f32)


def make(mesh):
    n_dp = mesh.shape["dp"]
    n_mp = mesh.shape["mp"]

    def dpx(x, bit):
        return lax.ppermute(x, "dp", [(i, i ^ bit) for i in range(n_dp)])

    def mpx(x, bit):
        return lax.ppermute(x, "mp", [(i, i ^ bit) for i in range(n_mp)])

    def bit_of(axis, bit):
        return (lax.axis_index(axis) & bit) != 0

    def flips(v, axis, bits, dims):
        for bit, dim in zip(bits, dims):
            v = jnp.where(bit_of(axis, bit), jnp.flip(v, dim), v)
        return v

    def plane_parts(r):
        got = [None] * SLICES
        for p in (0, 2, 4, 6):
            got[p] = dpx(r, p) if p else r
        for p in (0, 2, 4, 6):
            got[p + 1] = dpx(got[p], 1)
        return got

    def over_z(piece):
        return [mpx(piece, i) for i in range(1, n_mp)]

    def over_z_slow(own, *deps):
        got = [mpx(own, 1)]
        own = after(own, *deps)
        bit = 2
        while bit < n_mp:
            far = mpx(jnp.stack([own] + got), bit)
            got += [far[i] for i in range(bit)]
            bit *= 2
        return got

    def over_plane(r):
        return [dpx(r, 2), dpx(r, 4), dpx(r, 6)]

    def over_core(parts):
        return parts + [dpx(part, 1) for part in parts]

    def after(x, *deps):
        return lax.optimization_barrier((x, deps))[0]

    def own_piece(shard, place=0):
        rows = shard.shape[0] // SLICES
        at = jnp.bitwise_xor(lax.axis_index("dp") % SLICES, place)
        return lax.dynamic_slice_in_dim(shard, at * rows, rows, 0)

    def add(a, b):
        return (a.astype(f32) + b.astype(f32)).astype(low)

    def reduce_one(keep, got):
        return (
            add(keep[0, :, 1], got[0, :, 1]),
            add(keep[1, 1], got[1, 1]),
            add(keep[0, :, 0], got[0, :, 0]),
            add(keep[1, 0], got[1, 0]),
        )

    def reduce_two(a0, b0, a1, b1):
        return add(a0[1], a1[1]), add(b0[1], b1[1]), a0[0], a1[0], b0[0], b1[0]

    def reduce_three(a0, a1, b0, b1, a2, b2):
        a = a0.astype(f32) + a1.astype(f32) + a2.astype(f32)
        b = b0.astype(f32) + b1.astype(f32) + b2.astype(f32)
        u = [a[0], a[1], b[0], b[1]]
        bit = SLICES
        while bit < n_dp:
            u = [w.astype(low) for w in u]
            u = [w.astype(f32) + dpx(w, bit).astype(f32) for w in u]
            bit *= 2
        return [w.astype(low) for w in u]

    def reduce_last(u):
        total = u[0].astype(f32)
        for w in u[1:]:
            total = total + w.astype(f32)
        return total.astype(low)

    def mp_natural(v):
        bits = [1 << i for i in reversed(range(n_mp.bit_length() - 1))]
        shape = v.shape
        v = v.reshape((2,) * len(bits) + shape[1:])
        return flips(v, "mp", bits, range(len(bits))).reshape(shape)

    def gather_all(own):
        r = jnp.stack([own] + [mpx(own, s) for s in range(1, n_mp)])
        r = mp_natural(r)
        z = jnp.stack([r] + [dpx(r, b) for b in (2, 4, 6)])
        v = jnp.stack([z, dpx(z, 1)], 1).reshape((2, 2, 2) + r.shape)
        v = flips(v, "dp", (4, 2, 1), (0, 1, 2)).reshape((SLICES,) + r.shape)
        bit = SLICES
        while bit < n_dp:
            o = dpx(v, bit)
            up = bit_of("dp", bit)
            v = jnp.concatenate([jnp.where(up, o, v), jnp.where(up, v, o)], 0)
            bit *= 2
        return v.reshape((n_dp * n_mp,) + own.shape)

    def rank_part(first_rows, sents, pair_ids, w_pool, b_pool, scale):
        n_all = n_dp * n_mp
        width = first_rows.shape[-1]
        first_rows = first_rows[:, :sents].reshape(n_all * sents, width).astype(low)
        npairs = n_all * sents // 2
        pooled = jnp.tanh(
            jnp.dot(first_rows, w_pool, preferred_element_type=f32) + b_pool.astype(f32)
        )
        inv_len = lax.rsqrt(jnp.sum(pooled * pooled, axis=-1, keepdims=True) + eps_norm)
        emb_full = pooled * inv_len
        emb_pairs = emb_full.astype(low).reshape(npairs, 2, width)
        all_src, all_tgt = emb_pairs[:, 0, :], emb_pairs[:, 1, :]
        scale_value = scale[0]
        cosine = jnp.einsum("kd,md->km", all_src, all_tgt, preferred_element_type=f32)
        same = pair_ids[:, None] == pair_ids[None, :]
        counts = jnp.sum(same.astype(f32), axis=1)
        index_all = jnp.arange(npairs)
        diag_mask = (index_all[:, None] == index_all[None, :]).astype(f32)
        grad_row, part_row = rank_terms(
            cosine, same, diag_mask, (1.0 / counts)[:, None], scale_value, 1
        )
        grad_col, part_col = rank_terms(
            cosine, same, diag_mask, (1.0 / counts)[None, :], scale_value, 0
        )
        grad_all = grad_row + grad_col
        grad_src = scale_value * jnp.dot(grad_all, all_tgt.astype(f32), precision=high)
        grad_tgt = scale_value * jnp.einsum(
            "km,kd->md", grad_all, all_src.astype(f32), precision=high
        )
        new_scale = scale - step_rate * (jnp.sum(part_row) + jnp.sum(part_col))
        grad_emb = jnp.stack([grad_src, grad_tgt], axis=1).reshape(2 * npairs, width)
        grad_pooled = inv_len * (
            grad_emb - emb_full * jnp.sum(emb_full * grad_emb, axis=-1, keepdims=True)
        )
        grad_ppre = (grad_pooled * (1.0 - pooled * pooled)).astype(low)
        grad_pool = jnp.einsum("sd,se->de", first_rows, grad_ppre, preferred_element_type=f32)
        grad_b_pool = jnp.sum(grad_ppre.astype(f32), axis=0)
        own_ppre = lax.dynamic_slice_in_dim(
            grad_ppre, lax.axis_index(("dp", "mp")) * sents, sents, 0
        )
        grad_first = jnp.einsum("se,de->sd", own_ppre, w_pool, preferred_element_type=f32)
        grad_first = jnp.pad(grad_first, ((0, BLOCK - sents), (0, 0)))
        return grad_first, grad_pool, grad_b_pool, new_scale

    def on_device(
        inputs,
        token_ids,
        out_cot,
        pair_ids,
        w_qkv,
        b_qv,
        w_attn,
        b_attn,
        norm1_gain,
        norm1_bias,
        w_in,
        b_in,
        w_out,
        b_out,
        norm2_gain,
        norm2_bias,
        w_pool,
        b_pool,
        scale,
    ):
        rows, width = inputs.shape
        cols = w_qkv.shape[2]
        units = w_in.shape[1]
        sents = rows // SEQ
        shape = jax.ShapeDtypeStruct
        dma = pltpu.SemaphoreType.DMA
        vmem = pltpu.VMEM

        qkv_t = w_qkv.transpose(0, 2, 1)
        att_shard = jnp.concatenate([qkv_t.reshape(3 * cols, width), w_attn])
        size = att_shard.shape[0] // SLICES
        small = jnp.pad(jnp.concatenate([b_qv.reshape(-1), b_in]), (0, 2 * width - 2 * cols - units))
        small = small.reshape(2, width)
        att_z = over_z(jnp.concatenate([own_piece(att_shard), small]))
        vecs = jnp.stack(
            [b_attn, norm1_gain, norm1_bias, b_out, norm2_gain, norm2_bias, b_pool, b_pool]
        ).astype(f32)
        pieces = own_piece(w_in), own_piece(w_out), own_piece(w_out, 6)
        att_z[0] = after(att_z[0], vecs, *pieces)
        small = jnp.stack([small] + [r[size:] for r in att_z]).reshape(n_mp, -1).astype(f32)
        att_r = jnp.stack([r[:size] for r in att_z])
        in_z = over_z_slow(after(pieces[0], att_r))
        att_near = over_plane(att_r)
        att_parts = over_core([att_r] + att_near)
        in_r = jnp.stack(in_z)
        in_near = over_plane(after(in_r, *att_near))
        out_z = over_z_slow(after(pieces[1], in_z[0]), in_r)
        nc = n_copies(n_mp)
        own_qkv = att_shard[: 3 * cols].reshape(3, cols, width)

        def here(*arrays):
            return [(a, True) for a in arrays]

        def away(*arrays):
            return [(a, False) for a in arrays]

        ids = token_ids.reshape(rows // PAIR, 1, PAIR)

        rows_low, rows_f = shape((rows, width), low), shape((rows, width), f32)
        thin = shape((rows, 128), f32)
        w_shape = shape((4, n_mp * cols, width), low)
        p_shape = shape((rows // PAIR, width // LANES, PAIR, 2 * PAIR), f32)
        query, key_part, value_part, context, hat_one, inv_one, h1, w_all, p_all = call(
            functools.partial(attention_forward, n_mp, cols),
            here(after(inputs, out_z[0]), ids, small, vecs)
            + away(own_qkv, w_attn, *att_parts),
            here(rows_low, rows_low, rows_low, rows_low, rows_f, thin, rows_low)
            + away(w_shape, p_shape),
            [vmem(w_shape.shape, low), vmem(p_shape.shape, f32), dma((nc,)), dma((2,))],
            11,
        )
        out_r = jnp.stack(after(out_z, h1))
        out_far = over_z(after(pieces[2], h1))
        out_near = [dpx(out_r, 2), dpx(out_r, 4)]
        in_parts = over_core(after([in_r] + in_near, h1))
        mid = shape((n_mp, rows, units), low)
        ids_row = jnp.repeat(pair_ids.reshape(-1, sents // 2), 2, axis=1)
        ids_row = jnp.pad(ids_row, ((0, 0), (0, BLOCK - sents))).reshape(1, -1)
        hidden, slope = call(
            functools.partial(ffn_in_forward, n_mp, 2 * cols),
            here(h1, small) + away(w_in, *in_parts),
            away(mid, mid),
            [vmem((n_mp, width, units), low), vmem(mid.shape, low), vmem(mid.shape, low)]
            + [dma((nc,)), dma((2 * n_mp,))],
            9,
        )
        out_near += [jnp.stack(after(out_far, hidden))]
        out_parts = over_core(after([out_r] + out_near, hidden))
        layer_out, hat_two, inv_two, own_first = call(
            functools.partial(ffn_out_forward, n_mp),
            here(hat_one, vecs)
            + away(hidden, w_out, *out_parts),
            here(rows_low, rows_f, thin, shape((BLOCK, width), low)),
            [vmem((n_mp, units, width), low), vmem(mid.shape, low), vmem((rows, width), f32)]
            + [dma((nc,)), dma((n_mp,))],
            6,
        )
        lot = shape((2, 2, 2, n_mp // 2, size, width), low)
        tiny = shape((BLOCK, width), f32)
        out_scratch = [vmem((n_mp, units, width), low), vmem(mid.shape, low)]
        out_scratch += [dma((SLICES * n_mp,)), dma((n_mp,))]
        if n_dp == SLICES:
            n = n_dp * n_mp * BLOCK
            r = jnp.stack([own_first, dpx(own_first, 1)])
            r = jnp.stack([r] + over_z(r))
            all_first, all_ppre, grad_b_pool, new_scale, grad_z2, small_two, keep_o, send = call(
                functools.partial(ranking_out, n_mp, sents),
                here(ids_row, ids_row.reshape(n, 1), w_pool, vecs)
                + here(jnp.broadcast_to(scale[None], (1, n)))
                + away(r, *over_plane(r), out_cot, hat_two, inv_two, hidden),
                here(shape((n, width), low), shape((n, width), low))
                + here(shape((1, width), f32), shape((1, n), f32), rows_f, tiny)
                + away(lot, lot),
                [vmem((n_dp * n_mp, BLOCK, width), low), vmem((n, width), f32)]
                + [dma((n_dp * n_mp,)), vmem((BLOCK, width), f32), vmem((rows, width), low)]
                + [vmem((rows, width), f32), vmem((rows, 128), f32)]
                + out_scratch
                + [dma((3,))],
                14,
            )
            grad_b_pool, new_scale = grad_b_pool[0], new_scale[0, :1]
        else:
            grad_first, grad_pool, grad_b_pool, new_scale = rank_part(
                gather_all(own_first), sents, pair_ids, w_pool, b_pool, scale
            )
            grad_z2, small_two, keep_o, send = call(
                functools.partial(out_backward, n_mp),
                here(out_cot, grad_first, hat_two, inv_two, vecs) + away(hidden),
                here(rows_f, tiny) + away(lot, lot),
                out_scratch,
                10,
            )
        got_o = dpx(send, 1)
        grad_z1, grad_b_in, small_one, keep_i, send = call(
            functools.partial(in_backward, n_mp),
            here(grad_z2, h1, hat_one, inv_one, vecs)
            + away(slope, w_in, w_out, *in_parts, *out_parts),
            here(rows_f, shape((n_mp, 1, units), f32), tiny) + away(lot, lot),
            [
                vmem((n_mp, width, units), low),
                vmem((n_mp, units, width), low),
                vmem(mid.shape, low),
                vmem((n_mp, width, units), low),
                vmem((rows, width), f32),
                dma((2 * nc,)),
                dma((SLICES * n_mp,)),
                dma((n_mp,)),
            ],
            17,
        )
        got_i = dpx(send, 1)
        step_o = reduce_one(keep_o, after(got_o, grad_z1))
        a_o, b_o = dpx(step_o[0], 2), dpx(step_o[1], 4)
        grad_q, grad_k, grad_v, total, grad_wo = call(
            functools.partial(attention_backward, n_mp, cols),
            here(after(grad_z1, step_o[0], step_o[1]), query, key_part, value_part, context)
            + here(grad_b_in, small_one, small_two)
            + away(w_all, p_all),
            here(rows_low, rows_low, rows_low, shape((BLOCK + 2 * n_mp, width), f32))
            + here(shape((n_mp * cols, width), low)),
            [vmem((n_mp * cols, width), low), vmem(p_shape.shape, f32), vmem((rows, width), low)]
            + [dma((1,)), dma((rows // PAIR,))],
            15,
        )
        hops = [functools.partial(mpx, bit=1 << i) for i in range(n_mp.bit_length() - 1)]
        hops += [functools.partial(dpx, bit=1)]
        hops += [functools.partial(dpx, bit=1 << i) for i in range(3, n_dp.bit_length() - 1)]
        hop = hops[0](total)
        step_i = reduce_one(keep_i, after(got_i, grad_q))
        a_i, b_i = dpx(step_i[0], 2), dpx(step_i[1], 4)
        step_o = reduce_two(step_o[2], step_o[3], after(a_o, grad_q), after(b_o, grad_q))
        a2_o, b2_o = dpx(step_o[0], 4), dpx(step_o[1], 2)
        keep_a, send = call(
            functools.partial(attention_weights, n_mp, cols),
            here(after(inputs, step_i[0], step_i[1], step_o[0], step_o[1]))
            + here(grad_q, grad_k, grad_v, grad_wo),
            away(lot, lot),
            [vmem((4, n_mp * cols, width), low), dma((SLICES * n_mp,))],
            7,
        )
        got_a = dpx(send, 1)
        total = total + after(hop, keep_a)
        hop = hops[1](total)
        (input_grad,) = call(
            functools.partial(attention_inputs, n_mp, cols),
            here(grad_z1, after(grad_q, keep_a), grad_k, grad_v) + away(w_all),
            here(rows_f),
            [vmem((3, n_mp * cols, width), low), dma((3,))],
            7,
        )
        step_a = reduce_one(keep_a, after(got_a, input_grad))
        a_a, b_a = dpx(step_a[0], 2), dpx(step_a[1], 4)
        step_o = reduce_three(*step_o[2:], *after([a2_o, b2_o], step_a[0], step_a[1]))
        z_o = [mpx(step_o[i], i) for i in range(1, n_mp)]
        total = total + after(hop, step_a[0])
        hop = hops[2](total)
        step_i = reduce_two(step_i[2], step_i[3], *after([a_i, b_i], step_a[0], step_a[1]))
        a2_i, b2_i = dpx(step_i[0], 4), dpx(step_i[1], 2)
        step_a = reduce_two(step_a[2], step_a[3], *after([a_a, b_a], step_i[0], step_i[1]))
        a2_a, b2_a = dpx(step_a[0], 4), dpx(step_a[1], 2)
        red_out = reduce_last(after([step_o[0]] + z_o, step_a[0]))
        total = total + after(hop, step_i[0])
        for h in hops[3:]:
            total = total + h(total)
        step_i = reduce_three(*step_i[2:], *after([a2_i, b2_i], step_a[0], step_a[1]))
        z_i = [mpx(step_i[i], i) for i in range(1, n_mp)]
        step_a = reduce_three(*step_a[2:], *after([a2_a, b2_a], step_i[0]))
        z_a = [mpx(step_a[i], i) for i in range(1, n_mp)]
        red_in = reduce_last(after([step_i[0]] + z_i, step_a[0]))
        out_own = plane_parts(red_out)
        total = total + dpx(after(total, step_a[0]), 2)
        total = total + dpx(total, 4)
        if n_dp == SLICES:
            grad_pool = tn(after(all_first, step_a[0]), all_ppre)
        take = lax.axis_index("mp")
        out_b_in = lax.dynamic_slice_in_dim(total, BLOCK + take, 1, 0)[0]
        out_b_qv = lax.dynamic_slice_in_dim(total, BLOCK + n_mp + take, 1, 0)
        out_b_qv = out_b_qv[0, : 2 * cols].reshape(2, cols)
        sums = [total[i] for i in range(6)]
        extras = [*sums, out_b_in, out_b_qv, grad_pool, grad_b_pool, new_scale]
        red_att = reduce_last(after([step_a[0]] + z_a, *extras))
        last = jnp.concatenate([red_in, red_att])
        last = [last] + over_plane(last)
        whole = shape((SLICES * size, width), f32)

        (done_out,) = call(functools.partial(finish_rows, 0), here(*out_own), here(whole), [], 3)
        last_own = []
        for part in last:
            last_own += [part, dpx(after(part, done_out), 1)]
        done_in, done_qkv, done_attn = call(
            functools.partial(finish_rows, cols),
            here(*last_own),
            here(whole, shape((3, cols, width), f32), shape((cols, width), f32)),
            [],
            4,
        )
        return (
            layer_out,
            input_grad,
            done_qkv.transpose(0, 2, 1),
            out_b_qv,
            done_attn,
            sums[0],
            sums[1],
            sums[2],
            done_in,
            out_b_in,
            done_out,
            sums[3],
            sums[4],
            sums[5],
            grad_pool,
            grad_b_pool,
            new_scale,
        )

    return on_device


def solution(mesh):
    rows, whole = P(("dp", "mp"), None), P()
    in_specs = (
        rows,
        P(("dp", "mp")),
        rows,
        whole,
        P(None, None, "mp"),
        P(None, "mp"),
        P("mp", None),
        whole,
        whole,
        whole,
        P(None, "mp"),
        P("mp"),
        P("mp", None),
        whole,
        whole,
        whole,
        whole,
        whole,
        whole,
    )
    out_specs = (
        rows,
        rows,
        P(None, None, "mp"),
        P(None, "mp"),
        P("mp", None),
        whole,
        whole,
        whole,
        P(None, "mp"),
        P("mp"),
        P("mp", None),
        whole,
        whole,
        whole,
        whole,
        whole,
        whole,
    )
    return jax.shard_map(
        make(mesh), mesh=mesh, in_specs=in_specs, out_specs=out_specs, check_vma=False
    )
```
